128 devices in a mesh: pre: 4 (over z), dec: 32 (over y, x, core).
Axes of the slice: x: 4, y: 4, z: 4, core: 2. Of those that a mesh axis runs over, the one named last changes fastest.
Arguments:
- hidden: bfloat16 [32768, 7168], P(('pre', 'dec')), may hold values from -6 to 6
- w_down: bfloat16 [7168, 576], replicated, may hold values from -0.0625 to 0.0625
- kv_gain: float32 [512], replicated, may hold values from 0.25 to 1.75
- query_latent: bfloat16 [4, 8, 128, 512], P(None, None, 'pre')
- query_rope: bfloat16 [4, 8, 128, 64], P(None, None, 'pre'), may hold values from -9 to 9
- w_up_value: bfloat16 [128, 512, 128], P('pre'), may hold values from -0.25 to 0.25
- request_rows: int32 [4], replicated, may hold values from 1 to 16384, as said below
- row_request: int32 [8], replicated, may hold values from 0 to 3, as said below
- step_position: int32 [4, 8], replicated, may hold values from 1 to 16384, as said below
- destination: int32 [4096], replicated, may hold values from 0 to 4095, as said below
Outputs:
- attention_out: bfloat16 [4, 8, 16384], P(None, None, 'pre')
- latent_cache: bfloat16 [32768, 576], P('dec')
The draws below stay inside these ranges and needn't reach their ends.
Inputs may be any that keep to these rules, and one draw needn't show every extreme that they name: `request_rows`: the counts sum to 32768; each is at least a tenth of 8192; one request holds exactly 16384 rows. `row_request`: every request has some decode row. `step_position`: the 4 positions of a row are consecutive and at most its request's row count. `destination`: a permutation of the blocks; cache block c is held by owner c // 128; the blocks of prefill device g * 32 + e go to slots g * 32 to g * 32 + 31 of their owners; each owner receives exactly 32 blocks from each group, and each prefill device sends at most 2 blocks to one owner, exactly 2 to one of them.
All inputs are finite; a program needn't handle non-finite values.
Results may differ from the reference program's by a relative error of at most 0.008.
The reference program's roundings to bfloat16 on the way count: a program that leaves them out, or rounds other values in their place, can miss the bound.
Values may be sent and summed in bfloat16 or wider, within the bound.
No kernel may reach another device: no remote copies, remote signals or barrier semaphores. Data moves between devices by JAX's collectives and lax.ppermute only.
A program may use at most 192 MiB of HBM per device.

```python
import math
import jax
import jax.numpy as jnp
from jax import lax

D = 7168
LAT = 512
ROPE = 64
HEADS = 128
VDIM = 128
BLK = 8
BATCH = 8
STEPS = 4
REQS = 4
KVW = 576
GROUPS = 4
OWNERS = 32
NB_DEV = 32
CB_DEV = 128
ROWS = 32768
NBLK = 4096


def request_plan(key):
    key_weights, key_rows, key_start, key_long = jax.random.split(key, 4)
    long_id = jax.random.randint(key_long, (), 0, REQS)
    request_ids = jnp.arange(REQS, dtype=jnp.int32)
    weights = jax.random.randint(key_weights, (REQS,), 1, 4)
    weights = jnp.where(request_ids == long_id, 0, weights)
    long_rows = ROWS // 2
    rest_rows = ROWS - long_rows
    shares = rest_rows * weights // jnp.sum(weights)
    leftover = rest_rows - jnp.sum(shares)
    filler = (long_id + 1) % REQS
    shares = shares + jnp.where(request_ids == filler, leftover, 0)
    lengths = jnp.where(request_ids == long_id, long_rows, shares)
    key_pick, key_shuffle = jax.random.split(key_rows)
    chosen = jax.random.randint(key_pick, (BATCH,), 0, REQS)
    chosen = chosen.at[:REQS].set(request_ids)
    chosen = jax.random.permutation(key_shuffle, chosen)
    headroom = lengths[chosen] - STEPS + 1
    start_pos = jax.random.randint(key_start, (BATCH,), 0, headroom) + 1
    is_long = (chosen == long_id).astype(jnp.int32)
    first_long = jnp.argmax(is_long)
    start_pos = start_pos.at[first_long].set(headroom[first_long])
    positions = start_pos[None, :] + jnp.arange(STEPS, dtype=jnp.int32)[:, None]
    return (lengths.astype(jnp.int32), chosen.astype(jnp.int32), positions.astype(jnp.int32))


def draw_request_rows(key, part):
    return request_plan(key)[0]


def draw_row_request(key, part):
    return request_plan(key)[1]


def draw_step_position(key, part):
    return request_plan(key)[2]


def draw_destination(key, part):
    key = jax.random.fold_in(key, 5)
    key_shift, key_slot = jax.random.split(key)
    shuffles = jax.vmap(lambda sub_key: jax.random.permutation(sub_key, OWNERS))(jax.random.split(key_shift, GROUPS))
    shifts = shuffles.at[:, NB_DEV - 1].set(shuffles[:, 0])
    slot_order = jax.vmap(lambda sub_key: jax.random.permutation(sub_key, NB_DEV))(jax.random.split(key_slot, GROUPS * OWNERS)).reshape(GROUPS, OWNERS, NB_DEV)
    group_ids = jnp.arange(GROUPS, dtype=jnp.int32)[:, None, None]
    source_ids = jnp.arange(OWNERS, dtype=jnp.int32)[None, :, None]
    block_ids = jnp.arange(NB_DEV, dtype=jnp.int32)[None, None, :]
    owner_ids = (source_ids + shifts[:, None, :]) % OWNERS
    slot_ids = slot_order[group_ids, owner_ids, block_ids]
    return (owner_ids * CB_DEV + group_ids * NB_DEV + slot_ids).reshape(NBLK).astype(jnp.int32)


def draw_query_latent(key, part):
    key = jax.random.fold_in(key, 11)
    key_base = jax.random.fold_in(key, 0)
    base_draw = jax.random.normal(key_base, (STEPS, BATCH, HEADS, LAT), jnp.float32)
    return (base_draw * 1.5).astype(jnp.bfloat16)


def block_levels(key, shape, shards, least, top_value):
    def one(axis_at, parts):
        draws = jax.random.uniform(jax.random.fold_in(jax.random.fold_in(key, 6), axis_at), (parts,), jnp.float32, least / len(shards), top_value / len(shards))
        return jnp.repeat(jnp.exp(draws), shape[axis_at] // parts).reshape((-1,) + (1,) * (len(shape) - axis_at - 1))

    factor_of = one(*shards[0])
    for cut in shards[1:]:
        factor_of = factor_of * one(*cut)
    return factor_of


def gaussian(key, extent, deviation, reach, shards=(), held_as=jnp.bfloat16):
    loudness = block_levels(key, extent, shards, -0.22, 0.18) if shards else 1.0
    values = jax.random.normal(key, extent, jnp.float32) * deviation * loudness
    return jnp.minimum(jnp.maximum(values, -reach), reach).astype(held_as)


def setup_inputs(seed: int = 0) -> dict:
    key_list = jax.random.split(jax.random.key(seed), 11)
    hidden = gaussian(key_list[0], (ROWS, D), 1.0, 6.0, ((0, 128),))
    w_down = gaussian(key_list[1], (D, KVW), D ** -0.5, 0.0625)
    kv_gain = jnp.clip(1.0 + 0.15 * jax.random.normal(key_list[2], (LAT,), jnp.float32), 0.25, 1.75)
    query_latent = draw_query_latent(jax.random.fold_in(key_list[10], 71), 0)
    query_rope = gaussian(key_list[4], (STEPS, BATCH, HEADS, ROPE), 1.5, 9.0, ((2, 4),))
    w_up_value = gaussian(key_list[5], (HEADS, LAT, VDIM), LAT ** -0.5, 0.25, ((0, 4),))
    request_rows = draw_request_rows(jax.random.fold_in(key_list[10], 71), 0)
    row_request = draw_row_request(jax.random.fold_in(key_list[10], 71), 0)
    step_position = draw_step_position(jax.random.fold_in(key_list[10], 71), 0)
    destination = draw_destination(jax.random.fold_in(key_list[10], 71), 0)
    return {"hidden": hidden, "w_down": w_down, "kv_gain": kv_gain, "query_latent": query_latent, "query_rope": query_rope, "w_up_value": w_up_value, "request_rows": request_rows, "row_request": row_request, "step_position": step_position, "destination": destination}


score_scale = 0.07216878364870323
mask_value = -1e+30
norm_eps = 1e-06

def locate(lengths, row_ids):
    row_ends = jnp.cumsum(lengths)
    row_starts = row_ends - lengths
    request_of = lax.optimization_barrier(jnp.sum((row_ids[:, None] >= row_ends[None, :]).astype(jnp.int32), axis=1))
    onehot = request_of[:, None] == jnp.arange(lengths.shape[0], dtype=jnp.int32)[None, :]
    first_rows = lax.optimization_barrier(jnp.sum(jnp.where(onehot, row_starts[None, :], 0), axis=1))
    return (request_of, row_ids - first_rows)

def rotate(rotary, places):
    half_width = rotary.shape[-1] // 2
    pair_index = jnp.arange(half_width).astype(jnp.float32)
    frequency = jnp.exp(pair_index * (-2.0 * math.log(10000.0) / rotary.shape[-1]))
    angles = places.astype(jnp.float32)[:, None] * frequency[None, :]
    cosine = jnp.cos(angles)
    sine_part = jnp.sin(angles)
    first_half = rotary[:, :half_width]
    second_half = rotary[:, half_width:]
    return jnp.concatenate([first_half * cosine - second_half * sine_part, second_half * cosine + first_half * sine_part], axis=1)

def produce(hidden, w_down, kv_gain, places):
    raw_rows = jnp.dot(hidden, w_down, preferred_element_type=jnp.float32)
    latent_width = kv_gain.shape[0]
    latent = raw_rows[:, :latent_width]
    inverse_rms = lax.rsqrt(lax.optimization_barrier(jnp.mean(latent * latent, axis=1, keepdims=True)) + norm_eps)
    normed = latent * inverse_rms * kv_gain[None, :]
    return jnp.concatenate([normed, rotate(raw_rows[:, latent_width:], places)], axis=1).astype(jnp.bfloat16)

def reference(hidden, w_down, kv_gain, query_latent, query_rope, w_up_value, request_rows, row_request, step_position, destination):
    row_ids = jnp.arange(ROWS, dtype=jnp.int32)
    request_of, places = locate(request_rows, row_ids)
    produced = produce(hidden, w_down, kv_gain, places)
    kv_cache = jnp.zeros((NBLK, BLK, LAT + ROPE), jnp.bfloat16).at[destination].set(produced.reshape(NBLK, BLK, LAT + ROPE)).reshape(ROWS, LAT + ROPE)
    queries = jnp.concatenate([query_latent, query_rope], axis=3).reshape(STEPS * BATCH, HEADS, LAT + ROPE)
    limits = step_position.reshape(STEPS * BATCH)
    requests = jnp.tile(row_request, STEPS)
    latent_rows = produced[:, :LAT]
    weights_up = w_up_value.astype(jnp.float32)

    def one_row(query_item):
        query_rows, request_id, limit_here = query_item
        scores = jnp.dot(query_rows, produced.T, preferred_element_type=jnp.float32) * score_scale
        visible = (request_of == request_id) & (places < limit_here)
        masked = jnp.where(visible[None, :], scores, mask_value)
        row_peak = lax.optimization_barrier(jnp.max(masked, axis=1))
        weights = jnp.where(visible[None, :], jnp.exp(masked - row_peak[:, None]), 0.0)
        row_total = lax.optimization_barrier(jnp.sum(weights, axis=1))
        summed = jnp.dot(weights.astype(jnp.bfloat16), latent_rows, preferred_element_type=jnp.float32)
        mixed = summed / row_total[:, None]
        return jnp.einsum('hl,hlv->hv', mixed, weights_up, precision=lax.Precision.HIGHEST).reshape(-1)
    attention_out = lax.map(one_row, (queries, requests, limits)).reshape(STEPS, BATCH, HEADS * VDIM).astype(jnp.bfloat16)
    return (attention_out, kv_cache)
```

```python
import functools
import math

import jax
import jax.numpy as jnp
import numpy as np
from jax import lax
from jax.experimental import pallas as pl
from jax.experimental.pallas import tpu as pltpu
from jax.sharding import PartitionSpec as P

LAT = 512
ROPE = 64
MOST = 2
PAD = 8
SIDE = 4
CUT_HEADS = 8
DEPTH = 1024

score_scale = 0.07216878364870323
mask_value = -1e30
norm_eps = 1e-06
log2_e = 1.4426950408889634


def frequencies():
    half = ROPE // 2
    pair_index = np.arange(half, dtype=np.float64)
    frequency = np.exp(pair_index * (-2.0 * math.log(10000.0) / ROPE)).astype(np.float32)
    return np.tile(frequency[:, None], (1, 128))


def params(megabytes):
    return pltpu.CompilerParams(vmem_limit_bytes=megabytes * 1024 * 1024)


def produce_kernel(
    owners, lengths_hbm, hidden_hbm, w_hbm, gain_hbm, freq_hbm,
    out_ref, hidden_ref, w_ref, acc_ref, lengths_ref, gain_ref, freq_ref, sems, small_sems,
):
    pieces, rows, depth = hidden_ref.shape
    half = ROPE // 2
    small = [
        pltpu.make_async_copy(source, target, small_sems.at[k])
        for k, (source, target) in enumerate(
            ((lengths_hbm, lengths_ref), (gain_hbm, gain_ref), (freq_hbm, freq_ref))
        )
    ]

    def copies(k):
        columns = pl.ds(pl.multiple_of(k * depth, depth), depth)
        return (
            pltpu.make_async_copy(hidden_hbm.at[:, columns], hidden_ref.at[k], sems.at[0, k]),
            pltpu.make_async_copy(w_hbm.at[:, columns], w_ref.at[k], sems.at[1, k]),
        )

    def begin(k, carry):
        for copy in copies(k):
            copy.start()
        return carry

    lax.fori_loop(0, pieces, begin, 0)
    for copy in small:
        copy.start()
    acc_ref[...] = jnp.zeros_like(acc_ref)

    def body(k, carry):
        for copy in copies(k):
            copy.wait()
        acc_ref[...] += lax.dot_general(
            w_ref[k],
            hidden_ref[k],
            (((1,), (1,)), ((), ())),
            preferred_element_type=jnp.float32,
        )
        return carry

    lax.fori_loop(0, pieces, body, 0)
    for copy in small:
        copy.wait()
    device = lax.axis_index("pre") * owners + lax.axis_index("dec")
    row = device * rows + lax.broadcasted_iota(jnp.int32, (1, rows), 1)
    start = jnp.zeros((1, rows), jnp.int32)
    first_row = jnp.int32(0)
    for r in range(lengths_ref.shape[0] - 1):
        first_row = first_row + lengths_ref[r]
        start = jnp.where(row >= first_row, first_row, start)
    angles = freq_ref[:, 0:1] * (row - start).astype(jnp.float32)
    cosine = jnp.cos(angles)
    sine = jnp.sin(angles)
    gain = jnp.transpose(jnp.broadcast_to(gain_ref[...], (128, LAT)))[:, 0:1]
    latent = acc_ref[:LAT, :]
    inverse_rms = lax.rsqrt(jnp.mean(latent * latent, axis=0, keepdims=True) + norm_eps)
    out_ref[:LAT, :] = (latent * inverse_rms * gain).astype(out_ref.dtype)
    first = acc_ref[LAT : LAT + half, :]
    second = acc_ref[LAT + half :, :]
    turned = first * cosine - second * sine
    out_ref[LAT : LAT + half, :] = turned.astype(out_ref.dtype)
    turned = second * cosine + first * sine
    out_ref[LAT + half :, :] = turned.astype(out_ref.dtype)


def produce(owners, lengths, hidden, w_turned, gain):
    rows, width = hidden.shape
    row_width = w_turned.shape[0]
    pieces = width // DEPTH
    return pl.pallas_call(
        functools.partial(produce_kernel, owners),
        in_specs=[pl.BlockSpec(memory_space=pltpu.HBM)] * 5,
        out_specs=pl.BlockSpec(memory_space=pltpu.VMEM),
        out_shape=jax.ShapeDtypeStruct((row_width, rows), jnp.bfloat16),
        scratch_shapes=[
            pltpu.VMEM((pieces, rows, DEPTH), jnp.bfloat16),
            pltpu.VMEM((pieces, row_width, DEPTH), jnp.bfloat16),
            pltpu.VMEM((row_width, rows), jnp.float32),
            pltpu.SMEM(lengths.shape, jnp.int32),
            pltpu.VMEM((1, LAT), jnp.float32),
            pltpu.VMEM((ROPE // 2, 128), jnp.float32),
            pltpu.SemaphoreType.DMA((2, pieces)),
            pltpu.SemaphoreType.DMA((3,)),
        ],
        compiler_params=params(20),
        name="produce",
    )(lengths, hidden, w_turned, gain.reshape(1, -1), jnp.asarray(frequencies()))


WIDE = 640


def pack_kernel(groups, owners, dest_ref, rows_ref, out_ref, turned_ref, count_ref):
    width, rows = rows_ref.shape
    block_rows = out_ref.shape[1]
    blocks = rows // block_rows
    group = lax.axis_index("pre")
    first = (group * owners + lax.axis_index("dec")) * blocks
    for at in range(0, width, 128):
        count = min(128, width - at)
        wide = rows_ref[at : at + count, :].astype(jnp.float32)
        if count < 128:
            wide = jnp.concatenate([wide, jnp.zeros((128 - count, rows), jnp.float32)], axis=0)
        turned_ref[:, :, at : at + 128] = jnp.transpose(wide).reshape(blocks, block_rows, 128)

    def clear(owner, carry):
        count_ref[owner] = 0
        for rank in range(MOST):
            out_ref[owner * MOST + rank] = jnp.full(out_ref.shape[1:], -1.0, out_ref.dtype)
        return carry

    lax.fori_loop(0, owners, clear, 0)
    lane = lax.broadcasted_iota(jnp.int32, (block_rows, WIDE), 1)

    def put(b, carry):
        target = dest_ref[first + b]
        owner = lax.div(target, groups * owners)
        slot = lax.rem(target, groups * owners) - group * owners
        rank = count_ref[owner]
        count_ref[owner] = rank + 1
        block = jnp.where(lane < width, turned_ref[b], slot.astype(jnp.float32))
        out_ref[owner * MOST + rank] = block.astype(out_ref.dtype)
        return carry

    lax.fori_loop(0, blocks, put, 0)


def pack(groups, owners, destination, produced):
    width, rows = produced.shape
    block_rows = rows // owners
    return pl.pallas_call(
        functools.partial(pack_kernel, groups, owners),
        in_specs=[pl.BlockSpec(memory_space=pltpu.SMEM), pl.BlockSpec(memory_space=pltpu.VMEM)],
        out_specs=pl.BlockSpec(memory_space=pltpu.VMEM),
        out_shape=jax.ShapeDtypeStruct((owners * MOST, block_rows, WIDE), produced.dtype),
        scratch_shapes=[
            pltpu.VMEM((owners, block_rows, WIDE), jnp.float32),
            pltpu.SMEM((owners,), jnp.int32),
        ],
        compiler_params=params(8),
        name="pack",
    )(destination, produced)


def place_kernel(arrived_ref, out_ref, rows_ref):
    blocks, block_rows, _ = arrived_ref.shape
    width, rows = out_ref.shape
    part = 128 // block_rows
    row = lax.broadcasted_iota(jnp.int32, (rows, 128), 0).astype(jnp.float32)
    lane = lax.broadcasted_iota(jnp.int32, (1, 128), 1)
    within = lax.rem(lane, block_rows).astype(jnp.float32)
    rows_ref[...] = jnp.zeros_like(rows_ref)

    def body(k, carry):
        source = arrived_ref[pl.ds(k * part, part)].astype(jnp.float32).reshape(128, WIDE)
        slot = jnp.transpose(source[:, WIDE - 128 :])[127:128, :]
        select = jnp.where(row == slot * block_rows + within, 1.0, 0.0).astype(jnp.bfloat16)
        rows_ref[...] += jnp.dot(
            select, source.astype(jnp.bfloat16), preferred_element_type=jnp.float32
        )
        return carry

    lax.fori_loop(0, blocks // part, body, 0)
    for at in range(0, width, 128):
        count = min(128, width - at)
        turned = jnp.transpose(rows_ref[:, at : at + 128])
        out_ref[at : at + count, :] = turned[:count].astype(out_ref.dtype)


def place(arrived, width, rows):
    vmem = pl.BlockSpec(memory_space=pltpu.VMEM)
    return pl.pallas_call(
        place_kernel,
        in_specs=[vmem],
        out_specs=vmem,
        out_shape=jax.ShapeDtypeStruct((width, rows), arrived.dtype),
        scratch_shapes=[pltpu.VMEM((rows, WIDE), jnp.float32)],
        compiler_params=params(8),
        name="place",
    )(arrived)


def assemble_kernel(*refs):
    pieces, out_ref = refs[:-1], refs[-1]
    groups = len(pieces)
    group = lax.axis_index("pre")
    width, rows = pieces[0].shape
    step = 64

    def body(k, carry):
        part = pl.ds(pl.multiple_of(k * step, step), step)
        for shift, piece in zip((0, groups - 1, 1, 2), pieces):
            at = pl.multiple_of(lax.rem(group + shift, groups) * rows, rows)
            out_ref[part, pl.ds(at, rows)] = piece[part, :]
        return carry

    lax.fori_loop(0, width // step, body, 0)


def assemble(pieces):
    width, rows = pieces[0].shape
    vmem = pl.BlockSpec(memory_space=pltpu.VMEM)
    return pl.pallas_call(
        assemble_kernel,
        in_specs=[vmem] * len(pieces),
        out_specs=vmem,
        out_shape=jax.ShapeDtypeStruct((width, rows * len(pieces)), pieces[0].dtype),
        compiler_params=params(4),
        name="assemble",
    )(*pieces)


def fill_bias(owners, groups, shifts, lengths_ref, request_ref, position_ref, bias_ref, valid_ref):
    group, owner = lax.axis_index("pre"), lax.axis_index("dec")
    steps, batch = position_ref.shape
    heads = CUT_HEADS
    count = bias_ref.shape[1] // len(shifts)
    row = lax.broadcasted_iota(jnp.int32, (heads, count), 1)
    bases = [
        (lax.rem(group + shift, groups) * owners + owner) * count for shift in range(groups)
    ]

    def body(item, carry):
        b = lax.rem(item, batch)
        request = request_ref[b]
        start = jnp.int32(0)
        for r in range(lengths_ref.shape[0] - 1):
            start = start + jnp.where(request > r, lengths_ref[r], 0)
        stop = start + position_ref[lax.div(item, batch), b]
        at = pl.ds(pl.multiple_of(item * heads, heads), heads)
        for c, shift in enumerate(shifts):
            base = bases[shift]
            bias_ref[at, c * count : (c + 1) * count] = jnp.where(
                (row >= start - base) & (row < stop - base), 0.0, mask_value
            )
        if valid_ref is not None:
            seen = jnp.int32(0)
            for base in bases:
                seen = seen + jnp.where((start < base + count) & (stop > base), 1, 0)
            valid_ref[at, :] = jnp.full((heads, 128), seen, jnp.int32)
        return carry

    lax.fori_loop(0, steps * batch, body, 0)


def update_state(latent, rope, chunk_refs, bias_ref, state):
    rows = latent.shape[0]
    scores = []
    for c, chunk_ref in enumerate(chunk_refs):
        count = chunk_ref.shape[1]
        s = jnp.dot(latent, chunk_ref[:LAT, :], preferred_element_type=jnp.float32)
        s += jnp.dot(rope, chunk_ref[LAT:, :], preferred_element_type=jnp.float32)
        scores.append(s + bias_ref[:, c * count : (c + 1) * count])
    peaks = [jnp.max(s, axis=1, keepdims=True) for s in scores]
    if state is None:
        total = jnp.zeros((rows, 1), jnp.float32)
        mixed = jnp.zeros((rows, LAT), jnp.float32)
    else:
        old_peak, total, mixed = state
        peaks.append(old_peak)
    peak = functools.reduce(jnp.maximum, peaks)
    if state is not None:
        factor = jnp.exp2((old_peak - peak) * (score_scale * log2_e))
        total, mixed = total * factor, mixed * factor
    for s, chunk_ref in zip(scores, chunk_refs):
        p = jnp.exp2((s - peak) * (score_scale * log2_e))
        total += jnp.sum(p, axis=1, keepdims=True)
        mixed += lax.dot_general(
            p.astype(jnp.bfloat16),
            chunk_ref[:LAT, :],
            (((1,), (1,)), ((), ())),
            preferred_element_type=jnp.float32,
        )
    return peak, total, mixed


def near_kernel(
    owners, groups, lengths_ref, request_ref, position_ref, latent_ref, rope_ref,
    k0, k1, k2, mixed_ref, stat_ref, bias_ref,
):
    items, heads, _ = latent_ref.shape
    rows = items * heads
    cut = pl.program_id(0)

    @pl.when(cut == 0)
    def _():
        fill_bias(
            owners, groups, (0, groups - 1, 1),
            lengths_ref, request_ref, position_ref, bias_ref, None,
        )

    latent = latent_ref[...].reshape(rows, LAT)
    rope = rope_ref[...].reshape(rows, ROPE)
    peak, total, mixed = update_state(latent, rope, (k0, k1, k2), bias_ref, None)
    mixed_ref[cut] = mixed
    lane = lax.broadcasted_iota(jnp.int32, (rows, 128), 1)
    stat_ref[cut] = jnp.where(lane == 0, peak, total)


def far_kernel(
    owners, groups, lengths_ref, request_ref, position_ref, latent_ref, rope_ref,
    k3, mixed_ref, stat_ref, w_ref, out_ref, bias_ref, valid_ref,
):
    items, heads, _ = latent_ref.shape
    rows = items * heads
    all_heads = out_ref.shape[1] - PAD
    cut = pl.program_id(0)

    @pl.when(cut == 0)
    def _():
        fill_bias(
            owners, groups, (2,),
            lengths_ref, request_ref, position_ref, bias_ref, valid_ref,
        )
        out_ref[:, all_heads:, :] = jnp.zeros((items, PAD, 128), jnp.float32)

    latent = latent_ref[...].reshape(rows, LAT)
    rope = rope_ref[...].reshape(rows, ROPE)
    stat = stat_ref[cut]
    state = (stat[:, 0:1], stat[:, 1:2], mixed_ref[cut])
    peak, total, mixed = update_state(latent, rope, (k3,), bias_ref, state)
    valid = valid_ref[:, 0:1] > 0
    mixed = mixed * jnp.where(valid, 1.0 / total, 0.0)
    level = jnp.where(valid, peak * score_scale + jnp.log(total), mask_value)
    upper = mixed.astype(jnp.bfloat16)
    lower = (mixed - upper.astype(jnp.float32)).astype(jnp.bfloat16)
    head = lax.broadcasted_iota(jnp.int32, (rows, 128), 0) % heads
    result = jnp.zeros((rows, 128), jnp.float32)
    for h in range(0, heads, 2):
        pair = jnp.concatenate([w_ref[cut * heads + h], w_ref[cut * heads + h + 1]], axis=1)
        y = jnp.dot(upper, pair, preferred_element_type=jnp.float32)
        y += jnp.dot(lower, pair, preferred_element_type=jnp.float32)
        result = jnp.where(head == h, y[:, :128], result)
        result = jnp.where(head == h + 1, y[:, 128:], result)
    at = pl.multiple_of(cut * heads, heads)
    out_ref[:, pl.ds(at, heads), :] = result.reshape(items, heads, 128)
    lane = lax.broadcasted_iota(jnp.int32, (rows, 128), 1)
    lines = jnp.where(lane == head + at, level, 0.0).reshape(items, heads, 128)
    lines = jnp.sum(lines, axis=1, keepdims=True)
    out_ref[:, all_heads:, :] += jnp.broadcast_to(lines, (items, PAD, 128))


def attend(owners, lengths, row_request, step_position, latent, rope, chunks, w_up):
    items, heads, _ = latent.shape
    groups = len(chunks)
    cut = heads // CUT_HEADS
    rows = items * CUT_HEADS
    count = chunks[0].shape[1]
    smem = pl.BlockSpec(memory_space=pltpu.SMEM)
    vmem = pl.BlockSpec(memory_space=pltpu.VMEM)
    query_specs = [
        pl.BlockSpec((items, CUT_HEADS, LAT), lambda i: (0, i, 0)),
        pl.BlockSpec((items, CUT_HEADS, ROPE), lambda i: (0, i, 0)),
    ]
    scalars = (lengths, row_request, step_position)
    mixed, stat = pl.pallas_call(
        functools.partial(near_kernel, owners, groups),
        grid=(cut,),
        in_specs=[smem] * 3 + query_specs + [vmem] * 3,
        out_specs=[vmem, vmem],
        out_shape=[
            jax.ShapeDtypeStruct((cut, rows, LAT), jnp.float32),
            jax.ShapeDtypeStruct((cut, rows, 128), jnp.float32),
        ],
        scratch_shapes=[pltpu.VMEM((rows, 3 * count), jnp.float32)],
        compiler_params=params(16),
        name="attend_near",
    )(*scalars, latent, rope, *chunks[:3])
    return pl.pallas_call(
        functools.partial(far_kernel, owners, groups),
        grid=(cut,),
        in_specs=[smem] * 3 + query_specs + [vmem] * 4,
        out_specs=vmem,
        out_shape=jax.ShapeDtypeStruct((items, heads + PAD, 128), jnp.float32),
        scratch_shapes=[
            pltpu.VMEM((rows, count), jnp.float32),
            pltpu.VMEM((rows, 128), jnp.int32),
        ],
        compiler_params=params(16),
        name="attend_far",
    )(*scalars, latent, rope, chunks[3], mixed, stat, w_up)


def merge_kernel(last, *refs):
    parts, out_ref, scale_ref = refs[:-2], refs[-2], refs[-1]
    folded = len(parts) == 1
    sources = parts[0].shape[0] if folded else len(parts)
    items, depth, lanes = parts[0].shape[-3:]
    heads = depth - PAD
    part = (lambda k: parts[0].at[k]) if folded else (lambda k: parts[k])
    levels = [part(k)[:, heads:, :] for k in range(sources)]
    peak = functools.reduce(jnp.maximum, levels)
    scales = [jnp.exp(level - peak) for level in levels]
    total = functools.reduce(jnp.add, scales)
    for k in range(sources):
        scale_ref[k] = scales[k] / total
    lane = lax.broadcasted_iota(jnp.int32, (items, heads, lanes), 2)
    row = lax.broadcasted_iota(jnp.int32, (items, heads, lanes), 1)

    def term(k, here):
        line = scale_ref[k][:, 0:1, :]
        column = jnp.sum(jnp.where(lane == row, line, 0.0), axis=2, keepdims=True)
        return here[:, :heads, :] * column

    result = jnp.zeros((items, heads, lanes), jnp.float32)
    if folded:
        result = lax.fori_loop(
            0, sources, lambda k, so_far: so_far + term(k, parts[0].at[k]), result, unroll=4
        )
    else:
        for k in range(sources):
            result += term(k, parts[k])
    if last:
        result = result.astype(out_ref.dtype)
        for copy in range(out_ref.shape[0]):
            out_ref[copy] = result
    else:
        out_ref[:, :heads, :] = result
        out_ref[:, heads:, :] = peak + jnp.log(total)


def merge(parts, copies):
    items, depth, lanes = parts[0].shape[-3:]
    sources = parts[0].shape[0] if len(parts) == 1 else len(parts)
    last = copies > 0
    vmem = pl.BlockSpec(memory_space=pltpu.VMEM)
    if last:
        out_shape = jax.ShapeDtypeStruct((copies, items, depth - PAD, lanes), jnp.bfloat16)
    else:
        out_shape = jax.ShapeDtypeStruct((items, depth, lanes), jnp.float32)
    return pl.pallas_call(
        functools.partial(merge_kernel, last),
        in_specs=[vmem] * len(parts),
        out_specs=vmem,
        out_shape=out_shape,
        scratch_shapes=[pltpu.VMEM((sources, items, PAD, lanes), jnp.float32)],
        compiler_params=params(4),
        name="merge",
    )(*parts)


def spread_kernel(in_ref, out_ref, wide_ref):
    items, heads, lanes = in_ref.shape
    wide_ref[...] = in_ref[...].astype(jnp.float32).reshape(items * heads, lanes)

    def body(h, carry):
        rows = wide_ref[pl.ds(h, items, stride=heads), :]
        at = pl.multiple_of(h * lanes, lanes)
        out_ref[:, pl.ds(at, lanes)] = rows.astype(out_ref.dtype)
        return carry

    lax.fori_loop(0, heads, body, 0, unroll=4)


def spread(result):
    items, heads, lanes = result.shape
    vmem = pl.BlockSpec(memory_space=pltpu.VMEM)
    return pl.pallas_call(
        spread_kernel,
        in_specs=[vmem],
        out_specs=vmem,
        out_shape=jax.ShapeDtypeStruct((items, heads * lanes), result.dtype),
        scratch_shapes=[pltpu.VMEM((items * heads, lanes), jnp.float32)],
        compiler_params=params(4),
        name="spread",
    )(result)


def around(piece, groups, owners):
    core = lax.axis_index("dec") % 2
    before = lax.ppermute(piece, "pre", [(i, (i + 1) % groups) for i in range(groups)])
    after = lax.ppermute(piece, "pre", [(i, (i - 1) % groups) for i in range(groups)])
    forward = [
        (g * owners + d, (g + (1 if d % 2 == 0 else -1)) % groups * owners + d)
        for g in range(groups)
        for d in range(owners)
    ]
    far = lax.ppermute(jnp.where(core == 0, before, after), ("pre", "dec"), forward)
    return [piece, before, after, far]


def per_device(
    hidden,
    w_down,
    kv_gain,
    query_latent,
    query_rope,
    w_up_value,
    request_rows,
    row_request,
    step_position,
    destination,
):
    groups = lax.axis_size("pre")
    owners = lax.axis_size("dec")
    steps, batch, heads, _ = query_latent.shape
    items = steps * batch
    plane = [[2 * k + core for k in range(SIDE * SIDE)] for core in range(2)]
    sibling = [(d, d ^ 1) for d in range(owners)]

    produced = produce(owners, request_rows, hidden, w_down.T, kv_gain)
    chunks = around(produced, groups, owners)

    exchanged = functools.partial(
        lax.all_to_all, axis_name="dec", split_axis=0, concat_axis=0, tiled=True
    )
    parts = attend(
        owners,
        request_rows,
        row_request,
        step_position,
        query_latent.reshape(items, heads, -1),
        query_rope.reshape(items, heads, -1),
        chunks,
        w_up_value,
    )
    parts = exchanged(parts, axis_index_groups=plane)
    mine = merge([parts.reshape((SIDE * SIDE, 2) + parts.shape[1:])], 0)
    result = merge([mine, lax.ppermute(mine, "dec", sibling)], SIDE * SIDE)
    result = exchanged(result, axis_index_groups=plane)
    attention_out = spread(result.reshape((items,) + result.shape[2:])).reshape(steps, batch, -1)

    arrived = exchanged(pack(groups, owners, destination, produced))
    quarter = place(arrived, *produced.shape)
    kv_cache = assemble(around(quarter, groups, owners)).T
    return (attention_out, kv_cache)


def solution(mesh):
    return jax.shard_map(
        per_device,
        mesh=mesh,
        in_specs=(
            P(("pre", "dec"), None),
            P(),
            P(),
            P(None, None, "pre", None),
            P(None, None, "pre", None),
            P("pre", None, None),
            P(),
            P(),
            P(),
            P(),
        ),
        out_specs=(P(None, None, "pre"), P("dec", None)),
        check_vma=False,
    )
```

```python
import functools
import math

import jax
import jax.numpy as jnp
import numpy as np
from jax import lax
from jax.experimental import pallas as pl
from jax.experimental.pallas import tpu as pltpu
from jax.sharding import PartitionSpec as P

LAT = 512
ROPE = 64
MOST = 2
PAD = 8
SIDE = 4
CUT_HEADS = 8
DEPTH = 1024

score_scale = 0.07216878364870323
mask_value = -1e30
norm_eps = 1e-06
log2_e = 1.4426950408889634


def frequencies():
    half = ROPE // 2
    pair_index = np.arange(half, dtype=np.float64)
    frequency = np.exp(pair_index * (-2.0 * math.log(10000.0) / ROPE)).astype(np.float32)
    return np.tile(frequency[:, None], (1, 128))


def params(megabytes):
    return pltpu.CompilerParams(vmem_limit_bytes=megabytes * 1024 * 1024)


def produce_kernel(
    owners, lengths_hbm, hidden_hbm, w_hbm, gain_hbm, freq_hbm,
    out_ref, hidden_ref, w_ref, acc_ref, lengths_ref, gain_ref, freq_ref, sems, small_sems,
):
    pieces, rows, depth = hidden_ref.shape
    half = ROPE // 2
    small = [
        pltpu.make_async_copy(source, target, small_sems.at[k])
        for k, (source, target) in enumerate(
            ((lengths_hbm, lengths_ref), (gain_hbm, gain_ref), (freq_hbm, freq_ref))
        )
    ]

    def copies(k):
        columns = pl.ds(pl.multiple_of(k * depth, depth), depth)
        return (
            pltpu.make_async_copy(hidden_hbm.at[:, columns], hidden_ref.at[k], sems.at[0, k]),
            pltpu.make_async_copy(w_hbm.at[:, columns], w_ref.at[k], sems.at[1, k]),
        )

    def begin(k, carry):
        for copy in copies(k):
            copy.start()
        return carry

    lax.fori_loop(0, pieces, begin, 0)
    for copy in small:
        copy.start()
    acc_ref[...] = jnp.zeros_like(acc_ref)

    def body(k, carry):
        for copy in copies(k):
            copy.wait()
        acc_ref[...] += lax.dot_general(
            w_ref[k],
            hidden_ref[k],
            (((1,), (1,)), ((), ())),
            preferred_element_type=jnp.float32,
        )
        return carry

    lax.fori_loop(0, pieces, body, 0)
    for copy in small:
        copy.wait()
    device = lax.axis_index("pre") * owners + lax.axis_index("dec")
    row = device * rows + lax.broadcasted_iota(jnp.int32, (1, rows), 1)
    start = jnp.zeros((1, rows), jnp.int32)
    first_row = jnp.int32(0)
    for r in range(lengths_ref.shape[0] - 1):
        first_row = first_row + lengths_ref[r]
        start = jnp.where(row >= first_row, first_row, start)
    angles = freq_ref[:, 0:1] * (row - start).astype(jnp.float32)
    cosine = jnp.cos(angles)
    sine = jnp.sin(angles)
    gain = jnp.transpose(jnp.broadcast_to(gain_ref[...], (128, LAT)))[:, 0:1]
    latent = acc_ref[:LAT, :]
    inverse_rms = lax.rsqrt(jnp.mean(latent * latent, axis=0, keepdims=True) + norm_eps)
    out_ref[:LAT, :] = (latent * inverse_rms * gain).astype(out_ref.dtype)
    first = acc_ref[LAT : LAT + half, :]
    second = acc_ref[LAT + half :, :]
    turned = first * cosine - second * sine
    out_ref[LAT : LAT + half, :] = turned.astype(out_ref.dtype)
    turned = second * cosine + first * sine
    out_ref[LAT + half :, :] = turned.astype(out_ref.dtype)


def produce(owners, lengths, hidden, w_turned, gain):
    rows, width = hidden.shape
    row_width = w_turned.shape[0]
    pieces = width // DEPTH
    return pl.pallas_call(
        functools.partial(produce_kernel, owners),
        in_specs=[pl.BlockSpec(memory_space=pltpu.HBM)] * 5,
        out_specs=pl.BlockSpec(memory_space=pltpu.VMEM),
        out_shape=jax.ShapeDtypeStruct((row_width, rows), jnp.bfloat16),
        scratch_shapes=[
            pltpu.VMEM((pieces, rows, DEPTH), jnp.bfloat16),
            pltpu.VMEM((pieces, row_width, DEPTH), jnp.bfloat16),
            pltpu.VMEM((row_width, rows), jnp.float32),
            pltpu.SMEM(lengths.shape, jnp.int32),
            pltpu.VMEM((1, LAT), jnp.float32),
            pltpu.VMEM((ROPE // 2, 128), jnp.float32),
            pltpu.SemaphoreType.DMA((2, pieces)),
            pltpu.SemaphoreType.DMA((3,)),
        ],
        name="produce",
    )(lengths, hidden, w_turned, gain.reshape(1, -1), jnp.asarray(frequencies()))


WIDE = 640


def shift_of(count):
    assert count & (count - 1) == 0
    return count.bit_length() - 1


def pack_kernel(
    groups, owners, dest_hbm, rows_hbm, out_ref, turned_ref, dest_ref, rows_ref, count_ref, sems
):
    copies = [
        pltpu.make_async_copy(rows_hbm, rows_ref, sems.at[0]),
        pltpu.make_async_copy(dest_hbm, dest_ref, sems.at[1]),
    ]
    for copy in copies:
        copy.start()
    width, rows = rows_ref.shape
    block_rows = out_ref.shape[1]
    blocks = rows // block_rows
    group = lax.axis_index("pre")
    first = (group * owners + lax.axis_index("dec")) * blocks
    def clear(k, carry):
        for j in range(4):
            count_ref[k * 4 + j] = 0
        at = pl.ds(k * 4 * MOST, 4 * MOST)
        out_ref[at] = jnp.full((4 * MOST,) + out_ref.shape[1:], -1.0, out_ref.dtype)
        return carry

    lax.fori_loop(0, owners // 4, clear, 0)
    for copy in copies:
        copy.wait()
    for at in range(0, width, 128):
        count = min(128, width - at)
        wide = rows_ref[at : at + count, :].astype(jnp.float32)
        if count < 128:
            wide = jnp.concatenate([wide, jnp.zeros((128 - count, rows), jnp.float32)], axis=0)
        turned_ref[:, :, at : at + 128] = jnp.transpose(wide).reshape(blocks, block_rows, 128)
    lane = lax.broadcasted_iota(jnp.int32, (block_rows, WIDE), 1)

    def put(b, carry):
        target = dest_ref[first + b]
        owner = lax.shift_right_logical(target, shift_of(groups * owners))
        slot = (target & (groups * owners - 1)) - group * owners
        rank = count_ref[owner]
        count_ref[owner] = rank + 1
        block = jnp.where(lane < width, turned_ref[b], slot.astype(jnp.float32))
        out_ref[owner * MOST + rank] = block.astype(out_ref.dtype)
        return carry

    lax.fori_loop(0, blocks, put, 0)


def pack(groups, owners, destination, produced):
    width, rows = produced.shape
    block_rows = rows // owners
    return pl.pallas_call(
        functools.partial(pack_kernel, groups, owners),
        in_specs=[pl.BlockSpec(memory_space=pltpu.HBM)] * 2,
        out_specs=pl.BlockSpec(memory_space=pltpu.VMEM),
        out_shape=jax.ShapeDtypeStruct((owners * MOST, block_rows, WIDE), produced.dtype),
        scratch_shapes=[
            pltpu.VMEM((owners, block_rows, WIDE), jnp.float32),
            pltpu.SMEM(destination.shape, jnp.int32),
            pltpu.VMEM(produced.shape, produced.dtype),
            pltpu.SMEM((owners,), jnp.int32),
            pltpu.SemaphoreType.DMA((2,)),
        ],
        name="pack",
    )(destination, produced)


def place_kernel(arrived_ref, out_ref, rows_ref):
    blocks, block_rows, _ = arrived_ref.shape
    width, rows = out_ref.shape
    part = 128 // block_rows
    row = lax.broadcasted_iota(jnp.int32, (rows, 128), 0).astype(jnp.float32)
    lane = lax.broadcasted_iota(jnp.int32, (1, 128), 1)
    within = lax.rem(lane, block_rows).astype(jnp.float32)
    rows_ref[...] = jnp.zeros_like(rows_ref)

    def body(k, carry):
        source = arrived_ref[pl.ds(k * part, part)].astype(jnp.float32).reshape(128, WIDE)
        slot = jnp.transpose(source[:, WIDE - 128 :])[127:128, :]
        select = jnp.where(row == slot * block_rows + within, 1.0, 0.0).astype(jnp.bfloat16)
        rows_ref[...] += jnp.dot(
            select, source.astype(jnp.bfloat16), preferred_element_type=jnp.float32
        )
        return carry

    lax.fori_loop(0, blocks // part, body, 0)
    for at in range(0, width, 128):
        count = min(128, width - at)
        turned = jnp.transpose(rows_ref[:, at : at + 128])
        out_ref[at : at + count, :] = turned[:count].astype(out_ref.dtype)


def place(arrived, width, rows):
    vmem = pl.BlockSpec(memory_space=pltpu.VMEM)
    return pl.pallas_call(
        place_kernel,
        in_specs=[vmem],
        out_specs=vmem,
        out_shape=jax.ShapeDtypeStruct((width, rows), arrived.dtype),
        scratch_shapes=[pltpu.VMEM((rows, WIDE), jnp.float32)],
        compiler_params=params(8),
        name="place",
    )(arrived)


def assemble_kernel(*refs):
    pieces, out_ref = refs[:-1], refs[-1]
    groups = len(pieces)
    group = lax.axis_index("pre")
    width, rows = pieces[0].shape
    step = 64

    def body(k, carry):
        part = pl.ds(pl.multiple_of(k * step, step), step)
        for shift, piece in zip((0, groups - 1, 1, 2), pieces):
            at = pl.multiple_of(lax.rem(group + shift, groups) * rows, rows)
            out_ref[part, pl.ds(at, rows)] = piece[part, :]
        return carry

    lax.fori_loop(0, width // step, body, 0)


def assemble(pieces):
    width, rows = pieces[0].shape
    vmem = pl.BlockSpec(memory_space=pltpu.VMEM)
    return pl.pallas_call(
        assemble_kernel,
        in_specs=[vmem] * len(pieces),
        out_specs=vmem,
        out_shape=jax.ShapeDtypeStruct((width, rows * len(pieces)), pieces[0].dtype),
        compiler_params=params(4),
        name="assemble",
    )(*pieces)


def fill_bias(owners, groups, shifts, lengths_ref, request_ref, position_ref, bias_ref, valid_ref):
    group, owner = lax.axis_index("pre"), lax.axis_index("dec")
    steps, batch = position_ref.shape
    heads = CUT_HEADS
    count = bias_ref.shape[1] // len(shifts)
    row = lax.broadcasted_iota(jnp.int32, (heads, count), 1)
    bases = [
        (lax.rem(group + shift, groups) * owners + owner) * count for shift in range(groups)
    ]

    def body(b, carry):
        request = request_ref[b]
        start = jnp.int32(0)
        for r in range(lengths_ref.shape[0] - 1):
            start = start + jnp.where(request > r, lengths_ref[r], 0)
        for s in range(steps):
            stop = start + position_ref[s, b]
            at = pl.ds(pl.multiple_of((s * batch + b) * heads, heads), heads)
            for c, shift in enumerate(shifts):
                base = bases[shift]
                bias_ref[at, c * count : (c + 1) * count] = jnp.where(
                    (row >= start - base) & (row < stop - base), 0.0, mask_value
                )
            if valid_ref is not None:
                seen = jnp.int32(0)
                for base in bases:
                    seen = seen + jnp.where((start < base + count) & (stop > base), 1, 0)
                valid_ref[at, :] = jnp.full((heads, 128), seen, jnp.int32)
        return carry

    lax.fori_loop(0, batch, body, 0)


def update_state(latent, rope, chunk_refs, bias_ref, state):
    rows = latent.shape[0]
    scores = []
    for c, chunk_ref in enumerate(chunk_refs):
        count = chunk_ref.shape[1]
        s = jnp.dot(latent, chunk_ref[:LAT, :], preferred_element_type=jnp.float32)
        s += jnp.dot(rope, chunk_ref[LAT:, :], preferred_element_type=jnp.float32)
        scores.append(s + bias_ref[:, c * count : (c + 1) * count])
    peaks = [jnp.max(s, axis=1, keepdims=True) for s in scores]
    if state is None:
        total = jnp.zeros((rows, 1), jnp.float32)
        mixed = jnp.zeros((rows, LAT), jnp.float32)
    else:
        old_peak, total, mixed = state
        peaks.append(old_peak)
    peak = functools.reduce(jnp.maximum, peaks)
    if state is not None:
        factor = jnp.exp2((old_peak - peak) * (score_scale * log2_e))
        total, mixed = total * factor, mixed * factor
    weights = [jnp.exp2((s - peak) * (score_scale * log2_e)) for s in scores]
    total += jnp.sum(functools.reduce(jnp.add, weights), axis=1, keepdims=True)
    for p, chunk_ref in zip(weights, chunk_refs):
        mixed += lax.dot_general(
            p.astype(jnp.bfloat16),
            chunk_ref[:LAT, :],
            (((1,), (1,)), ((), ())),
            preferred_element_type=jnp.float32,
        )
    return peak, total, mixed


def near_kernel(
    owners, groups, lengths_ref, request_ref, position_ref, latent_ref, rope_ref,
    k0, k1, k2, mixed_ref, stat_ref, bias_ref,
):
    items, heads, _ = latent_ref.shape
    rows = items * heads
    cut = pl.program_id(0)

    @pl.when(cut == 0)
    def _():
        fill_bias(
            owners, groups, (0, groups - 1, 1),
            lengths_ref, request_ref, position_ref, bias_ref, None,
        )

    latent = latent_ref[...].reshape(rows, LAT)
    rope = rope_ref[...].reshape(rows, ROPE)
    peak, total, mixed = update_state(latent, rope, (k0, k1, k2), bias_ref, None)
    mixed_ref[...] = mixed
    lane = lax.broadcasted_iota(jnp.int32, (rows, 128), 1)
    stat_ref[...] = jnp.where(lane == 0, peak, total)


def far_kernel(
    owners, groups, lengths_ref, request_ref, position_ref, latent_ref, rope_ref,
    k3, mixed_ref, stat_ref, w_ref, keep_ref, send_ref, out_ref, bias_ref, valid_ref,
):
    items, heads, _ = latent_ref.shape
    rows = items * heads
    all_heads = out_ref.shape[1] - PAD
    cut = pl.program_id(0)

    @pl.when(cut == 0)
    def _():
        fill_bias(
            owners, groups, (2,),
            lengths_ref, request_ref, position_ref, bias_ref, valid_ref,
        )
        out_ref[:, all_heads:, :] = jnp.zeros((items, PAD, 128), jnp.float32)

    latent = latent_ref[...].reshape(rows, LAT)
    rope = rope_ref[...].reshape(rows, ROPE)
    state = (stat_ref[:, 0:1], stat_ref[:, 1:2], mixed_ref[...])
    peak, total, mixed = update_state(latent, rope, (k3,), bias_ref, state)
    valid = valid_ref[:, 0:1] > 0
    mixed = mixed * jnp.where(valid, 1.0 / total, 0.0)
    level = jnp.where(valid, peak * score_scale + jnp.log(total), mask_value)
    upper = mixed.astype(jnp.bfloat16)
    lower = (mixed - upper.astype(jnp.float32)).astype(jnp.bfloat16)
    head = lax.broadcasted_iota(jnp.int32, (rows, 128), 0) % heads
    result = jnp.zeros((rows, 128), jnp.float32)
    for h in range(0, heads, 2):
        pair = jnp.concatenate([w_ref[h], w_ref[h + 1]], axis=1)
        y = jnp.dot(upper, pair, preferred_element_type=jnp.float32)
        y += jnp.dot(lower, pair, preferred_element_type=jnp.float32)
        result = jnp.where(head == h, y[:, :128], result)
        result = jnp.where(head == h + 1, y[:, 128:], result)
    at = pl.multiple_of(cut * heads, heads)
    out_ref[:, pl.ds(at, heads), :] = result.reshape(items, heads, 128)
    lane = lax.broadcasted_iota(jnp.int32, (rows, 128), 1)
    lines = jnp.where(lane == head + at, level, 0.0).reshape(items, heads, 128)
    lines = jnp.sum(lines, axis=1, keepdims=True)
    out_ref[:, all_heads:, :] += jnp.broadcast_to(lines, (items, PAD, 128))

    @pl.when(cut == pl.num_programs(0) - 1)
    def _():
        half = items // 2
        core = lax.axis_index("dec") & 1

        def hand(i, carry):
            keep_ref[i] = out_ref[core * half + i]
            send_ref[i] = out_ref[(1 - core) * half + i]
            return carry

        lax.fori_loop(0, half, hand, 0)


def attend(owners, lengths, row_request, step_position, latent, rope, chunks, w_up):
    items, heads, _ = latent.shape
    groups = len(chunks)
    cut = heads // CUT_HEADS
    rows = items * CUT_HEADS
    count = chunks[0].shape[1]
    smem = pl.BlockSpec(memory_space=pltpu.SMEM)
    query_specs = [
        pl.BlockSpec((items, CUT_HEADS, LAT), lambda i: (0, i, 0)),
        pl.BlockSpec((items, CUT_HEADS, ROPE), lambda i: (0, i, 0)),
    ]
    scalars = (lengths, row_request, step_position)
    state_specs = [
        pl.BlockSpec((rows, LAT), lambda i: (i, 0)),
        pl.BlockSpec((rows, 128), lambda i: (i, 0)),
    ]
    fixed = pl.BlockSpec(chunks[0].shape, lambda i: (0, 0))
    mixed, stat = pl.pallas_call(
        functools.partial(near_kernel, owners, groups),
        grid=(cut,),
        in_specs=[smem] * 3 + query_specs + [fixed] * 3,
        out_specs=state_specs,
        out_shape=[
            jax.ShapeDtypeStruct((cut * rows, LAT), jnp.float32),
            jax.ShapeDtypeStruct((cut * rows, 128), jnp.float32),
        ],
        scratch_shapes=[pltpu.VMEM((rows, 3 * count), jnp.float32)],
        compiler_params=params(20),
        name="attend_near",
    )(*scalars, latent, rope, *chunks[:3])
    out_shape = jax.ShapeDtypeStruct((items // 2, heads + PAD, 128), jnp.float32)
    out_spec = pl.BlockSpec(out_shape.shape, lambda i: (0, 0, 0))
    return pl.pallas_call(
        functools.partial(far_kernel, owners, groups),
        grid=(cut,),
        in_specs=[smem] * 3
        + query_specs
        + [fixed]
        + state_specs
        + [pl.BlockSpec((CUT_HEADS,) + w_up.shape[1:], lambda i: (i, 0, 0))],
        out_specs=[out_spec] * 2,
        out_shape=[out_shape] * 2,
        scratch_shapes=[
            pltpu.VMEM((items, heads + PAD, 128), jnp.float32),
            pltpu.VMEM((rows, count), jnp.float32),
            pltpu.VMEM((rows, 128), jnp.int32),
        ],
        compiler_params=params(48),
        name="attend_far",
    )(*scalars, latent, rope, chunks[3], mixed, stat, w_up)


def merge_step(levels):
    peak = functools.reduce(jnp.maximum, levels)
    scales = [jnp.exp(level - peak) for level in levels]
    total = functools.reduce(jnp.add, scales)
    return [scale / total for scale in scales], peak + jnp.log(total)


def spread_columns(line, heads):
    shape = line.shape[:-2] + (heads, line.shape[-1])
    axis = len(shape) - 1
    lane = lax.broadcasted_iota(jnp.int32, shape, axis)
    row = lax.broadcasted_iota(jnp.int32, shape, axis - 1)
    return jnp.sum(jnp.where(lane == row, line, 0.0), axis=axis, keepdims=True)


def pair_kernel(mine_ref, other_ref, out_ref):
    items, depth, _ = mine_ref.shape
    heads = depth - PAD
    step = 4

    def body(k, carry):
        at = pl.ds(k * step, step)
        parts = [mine_ref[at], other_ref[at]]
        scales, level = merge_step([part[:, heads:, :] for part in parts])
        result = sum(
            part[:, :heads, :] * spread_columns(scale[:, 0:1, :], heads)
            for part, scale in zip(parts, scales)
        )
        out_ref[at, :heads, :] = result
        out_ref[at, heads:, :] = level
        return carry

    lax.fori_loop(0, items // step, body, 0)


def merge_pair(mine, other):
    vmem = pl.BlockSpec(memory_space=pltpu.VMEM)
    return pl.pallas_call(
        pair_kernel,
        in_specs=[vmem] * 2,
        out_specs=vmem,
        out_shape=jax.ShapeDtypeStruct(mine.shape, mine.dtype),
        compiler_params=params(4),
        name="merge_pair",
    )(mine, other)


def merge_kernel(parts_ref, out_ref, scale_ref):
    sources, depth, lanes = parts_ref.shape
    heads = depth - PAD
    scales, _ = merge_step([parts_ref[k, heads:, :] for k in range(sources)])
    for k in range(sources):
        scale_ref[k] = scales[k]

    def body(k, so_far):
        return so_far + parts_ref[k, :heads, :] * spread_columns(scale_ref[k][0:1, :], heads)

    result = lax.fori_loop(
        0, sources, body, jnp.zeros((heads, lanes), jnp.float32), unroll=4
    ).astype(out_ref.dtype)
    for copy in range(out_ref.shape[0]):
        out_ref[copy] = result


def merge(parts):
    sources, depth, lanes = parts.shape
    vmem = pl.BlockSpec(memory_space=pltpu.VMEM)
    return pl.pallas_call(
        merge_kernel,
        in_specs=[vmem],
        out_specs=vmem,
        out_shape=jax.ShapeDtypeStruct((sources, depth - PAD, lanes), jnp.bfloat16),
        scratch_shapes=[pltpu.VMEM((sources, PAD, lanes), jnp.float32)],
        compiler_params=params(4),
        name="merge",
    )(parts)


def spread_kernel(mine_ref, other_ref, out_ref, wide_ref):
    half, heads, lanes = mine_ref.shape
    core = lax.axis_index("dec") & 1
    rows = half * heads
    for place_at, ref in ((core, mine_ref), (1 - core, other_ref)):
        at = pl.ds(pl.multiple_of(place_at * rows, rows), rows)
        wide_ref[at, :] = ref[...].astype(jnp.float32).reshape(rows, lanes)

    def body(h, carry):
        piece = wide_ref[pl.ds(h, 2 * half, stride=heads), :]
        at = pl.multiple_of(h * lanes, lanes)
        out_ref[:, pl.ds(at, lanes)] = piece.astype(out_ref.dtype)
        return carry

    lax.fori_loop(0, heads, body, 0, unroll=4)


def spread(mine, other):
    half, heads, lanes = mine.shape
    vmem = pl.BlockSpec(memory_space=pltpu.VMEM)
    return pl.pallas_call(
        spread_kernel,
        in_specs=[vmem] * 2,
        out_specs=vmem,
        out_shape=jax.ShapeDtypeStruct((2 * half, heads * lanes), mine.dtype),
        scratch_shapes=[pltpu.VMEM((2 * half * heads, lanes), jnp.float32)],
        compiler_params=params(4),
        name="spread",
    )(mine, other)


def around(piece, groups, owners, gate=None):
    core = lax.axis_index("dec") % 2
    before = lax.ppermute(piece, "pre", [(i, (i + 1) % groups) for i in range(groups)])
    after = lax.ppermute(piece, "pre", [(i, (i - 1) % groups) for i in range(groups)])
    if gate is not None:
        before, after, _ = lax.optimization_barrier((before, after, gate))
    forward = [
        (g * owners + d, (g + (1 if d % 2 == 0 else -1)) % groups * owners + d)
        for g in range(groups)
        for d in range(owners)
    ]
    far = lax.ppermute(jnp.where(core == 0, before, after), ("pre", "dec"), forward)
    return [piece, before, after, far]


def per_device(
    hidden,
    w_down,
    kv_gain,
    query_latent,
    query_rope,
    w_up_value,
    request_rows,
    row_request,
    step_position,
    destination,
):
    groups = lax.axis_size("pre")
    owners = lax.axis_size("dec")
    steps, batch, heads, _ = query_latent.shape
    items = steps * batch
    plane = [[2 * k + core for k in range(SIDE * SIDE)] for core in range(2)]
    sibling = [(d, d ^ 1) for d in range(owners)]

    produced = produce(owners, request_rows, hidden, w_down.T, kv_gain)
    chunks = around(produced, groups, owners)

    exchanged = functools.partial(
        lax.all_to_all, axis_name="dec", split_axis=0, concat_axis=0, tiled=True
    )
    keep, send = attend(
        owners,
        request_rows,
        row_request,
        step_position,
        query_latent.reshape(items, heads, -1),
        query_rope.reshape(items, heads, -1),
        chunks,
        w_up_value,
    )
    parts = merge_pair(keep, lax.ppermute(send, "dec", sibling))
    result = merge(exchanged(parts, axis_index_groups=plane))

    arrived = exchanged(pack(groups, owners, destination, produced))
    quarter = place(arrived, *produced.shape)
    kv_cache = assemble(around(quarter, groups, owners, result)).T

    result = exchanged(result, axis_index_groups=plane)
    result = spread(result, lax.ppermute(result, "dec", sibling))
    attention_out = result.reshape(steps, batch, -1)
    return (attention_out, kv_cache)


def solution(mesh):
    return jax.shard_map(
        per_device,
        mesh=mesh,
        in_specs=(
            P(("pre", "dec"), None),
            P(),
            P(),
            P(None, None, "pre", None),
            P(None, None, "pre", None),
            P("pre", None, None),
            P(),
            P(),
            P(),
            P(),
        ),
        out_specs=(P(None, None, "pre"), P("dec", None)),
        check_vma=False,
    )
```

```python
import functools
import math

import jax
import jax.numpy as jnp
import numpy as np
from jax import lax
from jax.experimental import pallas as pl
from jax.experimental.pallas import tpu as pltpu
from jax.sharding import PartitionSpec as P

LAT = 512
ROPE = 64
MOST = 2
PAD = 8
SIDE = 4
TURNS = (0, 3, 1, 2)
CUT_HEADS = 8
DEPTH = 1024

score_scale = 0.07216878364870323
mask_value = -1e30
norm_eps = 1e-06
log2_e = 1.4426950408889634


def frequencies():
    half = ROPE // 2
    pair_index = np.arange(half, dtype=np.float64)
    frequency = np.exp(pair_index * (-2.0 * math.log(10000.0) / ROPE)).astype(np.float32)
    return np.tile(frequency[:, None], (1, 128))


WIDE = 640


def shift_of(count):
    assert count & (count - 1) == 0
    return count.bit_length() - 1


def params(megabytes):
    return pltpu.CompilerParams(vmem_limit_bytes=megabytes * 1024 * 1024)


def produce_kernel(
    groups, owners, lengths_hbm, dest_hbm, hidden_hbm, w_hbm, gain_hbm, freq_hbm,
    out_ref, packed_ref, hidden_ref, w_ref, acc_ref, lengths_ref, dest_ref, gain_ref, freq_ref,
    turn_ref, column_ref, rows_ref, count_ref, slot_ref, sems, small_sems,
):
    pieces, rows, depth = hidden_ref.shape
    half = ROPE // 2
    small = [
        pltpu.make_async_copy(source, target, small_sems.at[k])
        for k, (source, target) in enumerate(
            (
                (lengths_hbm, lengths_ref),
                (dest_hbm, dest_ref),
                (gain_hbm, gain_ref),
                (freq_hbm, freq_ref),
            )
        )
    ]

    def copies(k):
        columns = pl.ds(pl.multiple_of(k * depth, depth), depth)
        return (
            pltpu.make_async_copy(hidden_hbm.at[:, columns], hidden_ref.at[k], sems.at[0, k]),
            pltpu.make_async_copy(w_hbm.at[:, columns], w_ref.at[k], sems.at[1, k]),
        )

    def begin(k, carry):
        for copy in copies(k):
            copy.start()
        return carry

    for copy in small:
        copy.start()
    lax.fori_loop(0, pieces, begin, 0)
    acc_ref[...] = jnp.zeros_like(acc_ref)
    packed_ref[...] = jnp.full(packed_ref.shape, -1.0, packed_ref.dtype)
    for copy in small:
        copy.wait()
    group = lax.axis_index("pre")
    device = group * owners + lax.axis_index("dec")
    block_rows = packed_ref.shape[1]
    blocks = rows // block_rows

    def clear(owner, carry):
        count_ref[owner] = 0
        return carry

    def choose(b, carry):
        owner = lax.shift_right_logical(dest_ref[device * blocks + b], shift_of(groups * owners))
        rank = count_ref[owner]
        count_ref[owner] = rank + 1
        slot_ref[b] = owner * MOST + rank
        return carry

    lax.fori_loop(0, owners, clear, 0)
    lax.fori_loop(0, blocks, choose, 0)
    row = device * rows + lax.broadcasted_iota(jnp.int32, (1, rows), 1)
    start = jnp.zeros((1, rows), jnp.int32)
    first_row = jnp.int32(0)
    for r in range(lengths_ref.shape[0] - 1):
        first_row = first_row + lengths_ref[r]
        start = jnp.where(row >= first_row, first_row, start)
    angles = freq_ref[:, 0:1] * (row - start).astype(jnp.float32)
    turn_ref[:half, :] = jnp.cos(angles)
    turn_ref[half:, :] = jnp.sin(angles)
    column_ref[...] = jnp.transpose(jnp.broadcast_to(gain_ref[...], (128, LAT)))

    def body(k, carry):
        for copy in copies(k):
            copy.wait()
        acc_ref[...] += lax.dot_general(
            w_ref[k],
            hidden_ref[k],
            (((1,), (1,)), ((), ())),
            preferred_element_type=jnp.float32,
        )
        return carry

    lax.fori_loop(0, pieces, body, 0)
    latent = acc_ref[:LAT, :]
    inverse_rms = lax.rsqrt(jnp.mean(latent * latent, axis=0, keepdims=True) + norm_eps)
    out_ref[:LAT, :] = (latent * inverse_rms * column_ref[:, 0:1]).astype(out_ref.dtype)
    cosine, sine = turn_ref[:half, :], turn_ref[half:, :]
    first = acc_ref[LAT : LAT + half, :]
    second = acc_ref[LAT + half :, :]
    turned = first * cosine - second * sine
    out_ref[LAT : LAT + half, :] = turned.astype(out_ref.dtype)
    turned = second * cosine + first * sine
    out_ref[LAT + half :, :] = turned.astype(out_ref.dtype)
    width = out_ref.shape[0]
    for at in range(0, width, 128):
        count = min(128, width - at)
        wide = out_ref[at : at + count, :].astype(jnp.float32)
        if count < 128:
            wide = jnp.concatenate([wide, jnp.zeros((128 - count, rows), jnp.float32)], axis=0)
        rows_ref[:, :, at : at + 128] = jnp.transpose(wide).reshape(blocks, block_rows, 128)
    lane = lax.broadcasted_iota(jnp.int32, (block_rows, WIDE), 1)

    def put(b, carry):
        place_at = (dest_ref[device * blocks + b] & (groups * owners - 1)) - group * owners
        block = jnp.where(lane < width, rows_ref[b], place_at.astype(jnp.float32))
        packed_ref[slot_ref[b]] = block.astype(packed_ref.dtype)
        return carry

    lax.fori_loop(0, blocks, put, 0, unroll=4)


def produce(groups, owners, lengths, destination, hidden, w_turned, gain):
    rows, width = hidden.shape
    row_width = w_turned.shape[0]
    pieces = width // DEPTH
    block_rows = rows // owners
    vmem = pl.BlockSpec(memory_space=pltpu.VMEM)
    return pl.pallas_call(
        functools.partial(produce_kernel, groups, owners),
        in_specs=[pl.BlockSpec(memory_space=pltpu.HBM)] * 6,
        out_specs=[vmem, vmem],
        out_shape=[
            jax.ShapeDtypeStruct((row_width, rows), jnp.bfloat16),
            jax.ShapeDtypeStruct((owners * MOST, block_rows, WIDE), jnp.bfloat16),
        ],
        scratch_shapes=[
            pltpu.VMEM((pieces, rows, DEPTH), jnp.bfloat16),
            pltpu.VMEM((pieces, row_width, DEPTH), jnp.bfloat16),
            pltpu.VMEM((row_width, rows), jnp.float32),
            pltpu.SMEM(lengths.shape, jnp.int32),
            pltpu.SMEM(destination.shape, jnp.int32),
            pltpu.VMEM((1, LAT), jnp.float32),
            pltpu.VMEM((ROPE // 2, 128), jnp.float32),
            pltpu.VMEM((ROPE, rows), jnp.float32),
            pltpu.VMEM((LAT, 128), jnp.float32),
            pltpu.VMEM((owners, block_rows, WIDE), jnp.float32),
            pltpu.SMEM((owners,), jnp.int32),
            pltpu.SMEM((owners,), jnp.int32),
            pltpu.SemaphoreType.DMA((2, pieces)),
            pltpu.SemaphoreType.DMA((4,)),
        ],
        name="produce",
    )(
        lengths,
        destination,
        hidden,
        w_turned,
        gain.reshape(1, -1),
        jnp.asarray(frequencies()),
    )


def place_kernel(arrived_ref, out_ref, rows_ref):
    blocks, block_rows, _ = arrived_ref.shape
    width, rows = out_ref.shape
    part = 128 // block_rows
    row = lax.broadcasted_iota(jnp.int32, (rows, 128), 0).astype(jnp.float32)
    lane = lax.broadcasted_iota(jnp.int32, (1, 128), 1)
    within = lax.rem(lane, block_rows).astype(jnp.float32)
    rows_ref[...] = jnp.zeros_like(rows_ref)

    def body(k, carry):
        source = arrived_ref[pl.ds(k * part, part)].astype(jnp.float32).reshape(128, WIDE)
        slot = jnp.transpose(source[:, WIDE - 128 :])[127:128, :]
        select = jnp.where(row == slot * block_rows + within, 1.0, 0.0).astype(jnp.bfloat16)
        rows_ref[...] += jnp.dot(
            select, source.astype(jnp.bfloat16), preferred_element_type=jnp.float32
        )
        return carry

    lax.fori_loop(0, blocks // part, body, 0)
    for at in range(0, width, 128):
        count = min(128, width - at)
        turned = jnp.transpose(rows_ref[:, at : at + 128])
        out_ref[at : at + count, :] = turned[:count].astype(out_ref.dtype)


def place(arrived, width, rows):
    vmem = pl.BlockSpec(memory_space=pltpu.VMEM)
    return pl.pallas_call(
        place_kernel,
        in_specs=[vmem],
        out_specs=vmem,
        out_shape=jax.ShapeDtypeStruct((width, rows), arrived.dtype),
        scratch_shapes=[pltpu.VMEM((rows, WIDE), jnp.float32)],
        compiler_params=params(8),
        name="place",
    )(arrived)


def assemble_kernel(*refs):
    pieces, out_ref = refs[:-1], refs[-1]
    groups = len(pieces)
    group = lax.axis_index("pre")
    width, rows = pieces[0].shape
    step = 64

    def body(k, carry):
        part = pl.ds(pl.multiple_of(k * step, step), step)
        for turn, piece in zip(TURNS, pieces):
            at = pl.multiple_of((group ^ turn) * rows, rows)
            out_ref[part, pl.ds(at, rows)] = piece[part, :]
        return carry

    lax.fori_loop(0, width // step, body, 0)


def assemble(pieces):
    width, rows = pieces[0].shape
    vmem = pl.BlockSpec(memory_space=pltpu.VMEM)
    return pl.pallas_call(
        assemble_kernel,
        in_specs=[vmem] * len(pieces),
        out_specs=vmem,
        out_shape=jax.ShapeDtypeStruct((width, rows * len(pieces)), pieces[0].dtype),
        compiler_params=params(4),
        name="assemble",
    )(*pieces)


def prepare_kernel(
    owners, groups, lengths_ref, request_ref, position_ref, own_hbm,
    bias_ref, valid_ref, own_ref, sem,
):
    copy = pltpu.make_async_copy(own_hbm, own_ref, sem)
    copy.start()
    steps, batch = position_ref.shape
    heads = CUT_HEADS
    count = own_ref.shape[1]
    group, owner = lax.axis_index("pre"), lax.axis_index("dec")
    row = lax.broadcasted_iota(jnp.int32, (heads, count), 1)
    bases = [((group ^ turn) * owners + owner) * count for turn in TURNS]

    def fill(b, carry):
        request = request_ref[b]
        start = jnp.int32(0)
        for r in range(lengths_ref.shape[0] - 1):
            start = start + jnp.where(request > r, lengths_ref[r], 0)
        for s in range(steps):
            stop = start + position_ref[s, b]
            at = pl.ds(pl.multiple_of((s * batch + b) * heads, heads), heads)
            seen = jnp.int32(0)
            for c, base in enumerate(bases):
                bias_ref[at, c * count : (c + 1) * count] = jnp.where(
                    (row >= start - base) & (row < stop - base), 0.0, mask_value
                )
                seen = seen + jnp.where((start < base + count) & (stop > base), 1, 0)
            valid_ref[at, :] = jnp.full((heads, 128), seen, jnp.int32)
        return carry

    lax.fori_loop(0, batch, fill, 0)
    copy.wait()


def prepare(owners, groups, lengths, row_request, step_position, own):
    rows = step_position.size * CUT_HEADS
    smem = pl.BlockSpec(memory_space=pltpu.SMEM)
    vmem = pl.BlockSpec(memory_space=pltpu.VMEM)
    return pl.pallas_call(
        functools.partial(prepare_kernel, owners, groups),
        in_specs=[smem] * 3 + [pl.BlockSpec(memory_space=pl.ANY)],
        out_specs=[vmem] * 3,
        out_shape=[
            jax.ShapeDtypeStruct((rows, groups * own.shape[1]), jnp.float32),
            jax.ShapeDtypeStruct((rows, 128), jnp.int32),
            jax.ShapeDtypeStruct(own.shape, own.dtype),
        ],
        scratch_shapes=[pltpu.SemaphoreType.DMA(())],
        compiler_params=params(8),
        name="prepare",
    )(lengths, row_request, step_position, own)


def attend_kernel(
    bias_ref, valid_ref, latent_ref, rope_ref, k0, k1, k2, k3, w_hbm,
    keep_ref, send_ref, out_ref, w_ref, sems,
):
    chunk_refs = (k0, k1, k2, k3)
    items, cuts, heads, _ = latent_ref.shape
    rows = items * heads
    all_heads = cuts * heads
    count = k0.shape[1]

    def weights_of(cut):
        part = pl.ds(cut * heads, heads)
        return pltpu.make_async_copy(w_hbm.at[part], w_ref.at[part], sems.at[cut])

    for cut in range(cuts):
        weights_of(cut).start()
    out_ref[:, all_heads:, :] = jnp.zeros((items, PAD, 128), jnp.float32)
    head = lax.broadcasted_iota(jnp.int32, (rows, 128), 0) % heads
    lane = lax.broadcasted_iota(jnp.int32, (rows, 128), 1)

    def body(cut, carry):
        latent = latent_ref[:, cut].reshape(rows, LAT)
        rope = rope_ref[:, cut].reshape(rows, ROPE)
        scores = []
        for c, chunk_ref in enumerate(chunk_refs):
            s = jnp.dot(latent, chunk_ref[:LAT, :], preferred_element_type=jnp.float32)
            s += jnp.dot(rope, chunk_ref[LAT:, :], preferred_element_type=jnp.float32)
            scores.append(s + bias_ref[:, c * count : (c + 1) * count])
        peak = jnp.max(functools.reduce(jnp.maximum, scores), axis=1, keepdims=True)
        weights = [jnp.exp2((s - peak) * (score_scale * log2_e)) for s in scores]
        total = jnp.sum(functools.reduce(jnp.add, weights), axis=1, keepdims=True)
        mixed = sum(
            lax.dot_general(
                p.astype(jnp.bfloat16),
                chunk_ref[:LAT, :],
                (((1,), (1,)), ((), ())),
                preferred_element_type=jnp.float32,
            )
            for p, chunk_ref in zip(weights, chunk_refs)
        )
        valid = valid_ref[:, 0:1] > 0
        mixed = mixed * jnp.where(valid, 1.0 / total, 0.0)
        level = jnp.where(valid, peak * score_scale + jnp.log(total), mask_value)
        upper = mixed.astype(jnp.bfloat16)
        lower = (mixed - upper.astype(jnp.float32)).astype(jnp.bfloat16)
        weights_of(cut).wait()
        result = jnp.zeros((rows, 128), jnp.float32)
        for h in range(0, heads, 2):
            pair = jnp.concatenate([w_ref[cut * heads + h], w_ref[cut * heads + h + 1]], axis=1)
            y = jnp.dot(upper, pair, preferred_element_type=jnp.float32)
            y += jnp.dot(lower, pair, preferred_element_type=jnp.float32)
            result = jnp.where(head == h, y[:, :128], result)
            result = jnp.where(head == h + 1, y[:, 128:], result)
        at = pl.multiple_of(cut * heads, heads)
        out_ref[:, pl.ds(at, heads), :] = result.reshape(items, heads, 128)
        lines = jnp.where(lane == head + at, level, 0.0).reshape(items, heads, 128)
        lines = jnp.sum(lines, axis=1, keepdims=True)
        out_ref[:, all_heads:, :] += jnp.broadcast_to(lines, (items, PAD, 128))
        return carry

    lax.fori_loop(0, cuts, body, 0)
    half = items // 2
    core = lax.axis_index("dec") & 1

    def hand(i, carry):
        keep_ref[i] = out_ref[core * half + i]
        send_ref[i] = out_ref[(1 - core) * half + i]
        return carry

    lax.fori_loop(0, half, hand, 0)


def attend(bias, valid, latent, rope, chunks, w_up):
    items, heads, _ = latent.shape
    cuts = heads // CUT_HEADS
    vmem = pl.BlockSpec(memory_space=pltpu.VMEM)
    out_shape = jax.ShapeDtypeStruct((items // 2, heads + PAD, 128), jnp.float32)
    return pl.pallas_call(
        attend_kernel,
        in_specs=[vmem] * 8 + [pl.BlockSpec(memory_space=pl.ANY)],
        out_specs=[vmem] * 2,
        out_shape=[out_shape] * 2,
        scratch_shapes=[
            pltpu.VMEM((items, heads + PAD, 128), jnp.float32),
            pltpu.VMEM(w_up.shape, w_up.dtype),
            pltpu.SemaphoreType.DMA((cuts,)),
        ],
        compiler_params=params(48),
        name="attend",
    )(
        bias,
        valid,
        latent.reshape(items, cuts, CUT_HEADS, -1),
        rope.reshape(items, cuts, CUT_HEADS, -1),
        *chunks,
        w_up,
    )


def merge_step(levels):
    peak = functools.reduce(jnp.maximum, levels)
    scales = [jnp.exp(level - peak) for level in levels]
    total = functools.reduce(jnp.add, scales)
    return [scale / total for scale in scales], peak + jnp.log(total)


def spread_columns(line, heads):
    shape = line.shape[:-2] + (heads, line.shape[-1])
    axis = len(shape) - 1
    lane = lax.broadcasted_iota(jnp.int32, shape, axis)
    row = lax.broadcasted_iota(jnp.int32, shape, axis - 1)
    return jnp.sum(jnp.where(lane == row, line, 0.0), axis=axis, keepdims=True)


def pair_kernel(mine_ref, other_ref, out_ref):
    items, depth, _ = mine_ref.shape
    heads = depth - PAD
    step = 4

    def body(k, carry):
        at = pl.ds(k * step, step)
        parts = [mine_ref[at], other_ref[at]]
        scales, level = merge_step([part[:, heads:, :] for part in parts])
        result = sum(
            part[:, :heads, :] * spread_columns(scale[:, 0:1, :], heads)
            for part, scale in zip(parts, scales)
        )
        out_ref[at, :heads, :] = result
        out_ref[at, heads:, :] = level
        return carry

    lax.fori_loop(0, items // step, body, 0)


def merge_pair(mine, other):
    vmem = pl.BlockSpec(memory_space=pltpu.VMEM)
    return pl.pallas_call(
        pair_kernel,
        in_specs=[vmem] * 2,
        out_specs=vmem,
        out_shape=jax.ShapeDtypeStruct(mine.shape, mine.dtype),
        compiler_params=params(4),
        name="merge_pair",
    )(mine, other)


def merge_kernel(parts_ref, out_ref, scale_ref):
    sources, depth, lanes = parts_ref.shape
    heads = depth - PAD
    scales, _ = merge_step([parts_ref[k, heads:, :] for k in range(sources)])
    for k in range(sources):
        scale_ref[k] = scales[k]

    def body(k, so_far):
        return so_far + parts_ref[k, :heads, :] * spread_columns(scale_ref[k][0:1, :], heads)

    result = lax.fori_loop(
        0, sources, body, jnp.zeros((heads, lanes), jnp.float32), unroll=4
    ).astype(out_ref.dtype)
    for copy in range(out_ref.shape[0]):
        out_ref[copy] = result


def merge(parts):
    sources, depth, lanes = parts.shape
    vmem = pl.BlockSpec(memory_space=pltpu.VMEM)
    return pl.pallas_call(
        merge_kernel,
        in_specs=[vmem],
        out_specs=vmem,
        out_shape=jax.ShapeDtypeStruct((sources, depth - PAD, lanes), jnp.bfloat16),
        scratch_shapes=[pltpu.VMEM((sources, PAD, lanes), jnp.float32)],
        compiler_params=params(4),
        name="merge",
    )(parts)


def spread_kernel(mine_ref, other_ref, out_ref, wide_ref):
    half, heads, lanes = mine_ref.shape
    core = lax.axis_index("dec") & 1
    rows = half * heads
    for place_at, ref in ((core, mine_ref), (1 - core, other_ref)):
        for k in range(half):
            at = pl.ds(pl.multiple_of(place_at * rows + (half - 1 - k) * heads, heads), heads)
            wide_ref[at, :] = ref[k].astype(jnp.float32)

    def body(h, carry):
        piece = wide_ref[pl.ds(h, 2 * half, stride=heads), :]
        at = pl.multiple_of(h * lanes, lanes)
        out_ref[:, pl.ds(at, lanes)] = piece.astype(out_ref.dtype)
        return carry

    lax.fori_loop(0, heads, body, 0, unroll=4)


def spread(mine, other):
    half, heads, lanes = mine.shape
    vmem = pl.BlockSpec(memory_space=pltpu.VMEM)
    return pl.pallas_call(
        spread_kernel,
        in_specs=[vmem] * 2,
        out_specs=vmem,
        out_shape=jax.ShapeDtypeStruct((2 * half, heads * lanes), mine.dtype),
        scratch_shapes=[pltpu.VMEM((2 * half * heads, lanes), jnp.float32)],
        compiler_params=params(4),
        name="spread",
    )(mine, other)


def exchange(piece, groups, turn):
    return lax.ppermute(piece, "pre", [(i, i ^ turn) for i in range(groups)])


def around(piece, groups, owners):
    core = lax.axis_index("dec") % 2
    first = exchange(piece, groups, 3)
    second = exchange(piece, groups, 1)
    forward = [
        (g * owners + d, (g ^ (1 if d % 2 == 0 else 3)) * owners + d)
        for g in range(groups)
        for d in range(owners)
    ]
    chosen = jnp.where(core == 0, first, second)
    far = lax.ppermute(chosen, ("pre", "dec"), forward)
    return [piece, first, second, far], chosen


def per_device(
    hidden,
    w_down,
    kv_gain,
    query_latent,
    query_rope,
    w_up_value,
    request_rows,
    row_request,
    step_position,
    destination,
):
    groups = lax.axis_size("pre")
    owners = lax.axis_size("dec")
    steps, batch, heads, _ = query_latent.shape
    items = steps * batch
    plane = [[2 * k + core for k in range(SIDE * SIDE)] for core in range(2)]
    reverse = [group[::-1] for group in plane]
    sibling = [(d, d ^ 1) for d in range(owners)]

    produced, packed = produce(
        groups, owners, request_rows, destination, hidden, w_down.T, kv_gain
    )
    chunks, chosen = around(produced, groups, owners)

    exchanged = functools.partial(
        lax.all_to_all, axis_name="dec", split_axis=0, concat_axis=0, tiled=True
    )
    lengths, _ = lax.optimization_barrier((request_rows, chosen))
    bias, valid, chunks[0] = prepare(
        owners, groups, lengths, row_request, step_position, produced
    )
    keep, send = attend(
        bias,
        valid,
        query_latent.reshape(items, heads, -1),
        query_rope.reshape(items, heads, -1),
        chunks,
        w_up_value,
    )
    arrived = exchanged(packed)
    quarter = place(arrived, *produced.shape)
    pieces = [quarter] + [exchange(quarter, groups, turn) for turn in TURNS[1:]]
    kv_cache = assemble(pieces).T

    keep, _ = lax.optimization_barrier((keep, quarter))
    parts = merge_pair(keep, lax.ppermute(send, "dec", sibling))
    result = merge(exchanged(parts, axis_index_groups=plane))
    result = exchanged(result, axis_index_groups=reverse)
    result = spread(result, lax.ppermute(result, "dec", sibling))
    attention_out = result.reshape(steps, batch, -1)
    return (attention_out, kv_cache)


def solution(mesh):
    return jax.shard_map(
        per_device,
        mesh=mesh,
        in_specs=(
            P(("pre", "dec"), None),
            P(),
            P(),
            P(None, None, "pre", None),
            P(None, None, "pre", None),
            P("pre", None, None),
            P(),
            P(),
            P(),
            P(),
        ),
        out_specs=(P(None, None, "pre"), P("dec", None)),
        check_vma=False,
    )
```

```python
import functools
import math

import jax
import jax.numpy as jnp
import numpy as np
from jax import lax
from jax.experimental import pallas as pl
from jax.experimental.pallas import tpu as pltpu
from jax.sharding import PartitionSpec as P

LAT = 512
ROPE = 64
MOST = 2
PAD = 8
SIDE = 4
TURNS = (0, 3, 1, 2)
CUT_HEADS = 8
DEPTH = 1024

score_scale = 0.07216878364870323
mask_value = -1e30
norm_eps = 1e-06
log2_e = 1.4426950408889634


def frequencies():
    half = ROPE // 2
    pair_index = np.arange(half, dtype=np.float64)
    frequency = np.exp(pair_index * (-2.0 * math.log(10000.0) / ROPE)).astype(np.float32)
    return np.tile(frequency[:, None], (1, 128))


WIDE = 640


def shift_of(count):
    assert count & (count - 1) == 0
    return count.bit_length() - 1


def params(megabytes):
    return pltpu.CompilerParams(vmem_limit_bytes=megabytes * 1024 * 1024)


def produce_kernel(
    groups, owners, lengths_hbm, dest_hbm, hidden_hbm, w_hbm, gain_hbm, freq_hbm,
    out_ref, packed_ref, hidden_ref, w_ref, acc_ref, lengths_ref, dest_ref, gain_ref, freq_ref,
    turn_ref, column_ref, rows_ref, count_ref, slot_ref, sems, small_sems,
):
    pieces, rows, depth = hidden_ref.shape
    half = ROPE // 2
    small = [
        pltpu.make_async_copy(source, target, small_sems.at[k])
        for k, (source, target) in enumerate(
            (
                (lengths_hbm, lengths_ref),
                (dest_hbm, dest_ref),
                (gain_hbm, gain_ref),
                (freq_hbm, freq_ref),
            )
        )
    ]

    def copies(k):
        columns = pl.ds(pl.multiple_of(k * depth, depth), depth)
        return (
            pltpu.make_async_copy(hidden_hbm.at[:, columns], hidden_ref.at[k], sems.at[0, k]),
            pltpu.make_async_copy(w_hbm.at[:, columns], w_ref.at[k], sems.at[1, k]),
        )

    def begin(k, carry):
        for copy in copies(k):
            copy.start()
        return carry

    for copy in small:
        copy.start()
    lax.fori_loop(0, pieces, begin, 0)
    acc_ref[...] = jnp.zeros_like(acc_ref)
    packed_ref[...] = jnp.full(packed_ref.shape, -1.0, packed_ref.dtype)
    for copy in small:
        copy.wait()
    group = lax.axis_index("pre")
    device = group * owners + lax.axis_index("dec")
    block_rows = packed_ref.shape[1]
    blocks = rows // block_rows

    def clear(owner, carry):
        count_ref[owner] = 0
        return carry

    def choose(b, carry):
        owner = lax.shift_right_logical(dest_ref[device * blocks + b], shift_of(groups * owners))
        rank = count_ref[owner]
        count_ref[owner] = rank + 1
        slot_ref[b] = owner * MOST + rank
        return carry

    lax.fori_loop(0, owners, clear, 0)
    lax.fori_loop(0, blocks, choose, 0)
    row = device * rows + lax.broadcasted_iota(jnp.int32, (1, rows), 1)
    start = jnp.zeros((1, rows), jnp.int32)
    first_row = jnp.int32(0)
    for r in range(lengths_ref.shape[0] - 1):
        first_row = first_row + lengths_ref[r]
        start = jnp.where(row >= first_row, first_row, start)
    angles = freq_ref[:, 0:1] * (row - start).astype(jnp.float32)
    turn_ref[:half, :] = jnp.cos(angles)
    turn_ref[half:, :] = jnp.sin(angles)
    column_ref[...] = jnp.transpose(jnp.broadcast_to(gain_ref[...], (128, LAT)))

    def body(k, carry):
        for copy in copies(k):
            copy.wait()
        acc_ref[...] += lax.dot_general(
            w_ref[k],
            hidden_ref[k],
            (((1,), (1,)), ((), ())),
            preferred_element_type=jnp.float32,
        )
        return carry

    lax.fori_loop(0, pieces, body, 0)
    latent = acc_ref[:LAT, :]
    inverse_rms = lax.rsqrt(jnp.mean(latent * latent, axis=0, keepdims=True) + norm_eps)
    out_ref[:LAT, :] = (latent * inverse_rms * column_ref[:, 0:1]).astype(out_ref.dtype)
    cosine, sine = turn_ref[:half, :], turn_ref[half:, :]
    first = acc_ref[LAT : LAT + half, :]
    second = acc_ref[LAT + half :, :]
    turned = first * cosine - second * sine
    out_ref[LAT : LAT + half, :] = turned.astype(out_ref.dtype)
    turned = second * cosine + first * sine
    out_ref[LAT + half :, :] = turned.astype(out_ref.dtype)
    width = out_ref.shape[0]
    for at in range(0, width, 128):
        count = min(128, width - at)
        wide = out_ref[at : at + count, :].astype(jnp.float32)
        if count < 128:
            wide = jnp.concatenate([wide, jnp.zeros((128 - count, rows), jnp.float32)], axis=0)
        rows_ref[:, :, at : at + 128] = jnp.transpose(wide).reshape(blocks, block_rows, 128)
    lane = lax.broadcasted_iota(jnp.int32, (block_rows, WIDE), 1)

    def put(b, carry):
        place_at = (dest_ref[device * blocks + b] & (groups * owners - 1)) - group * owners
        block = jnp.where(lane < width, rows_ref[b], place_at.astype(jnp.float32))
        packed_ref[slot_ref[b]] = block.astype(packed_ref.dtype)
        return carry

    lax.fori_loop(0, blocks, put, 0, unroll=4)


def produce(groups, owners, lengths, destination, hidden, w_turned, gain):
    rows, width = hidden.shape
    row_width = w_turned.shape[0]
    pieces = width // DEPTH
    block_rows = rows // owners
    vmem = pl.BlockSpec(memory_space=pltpu.VMEM)
    return pl.pallas_call(
        functools.partial(produce_kernel, groups, owners),
        in_specs=[pl.BlockSpec(memory_space=pltpu.HBM)] * 6,
        out_specs=[vmem, vmem],
        out_shape=[
            jax.ShapeDtypeStruct((row_width, rows), jnp.bfloat16),
            jax.ShapeDtypeStruct((owners * MOST, block_rows, WIDE), jnp.bfloat16),
        ],
        scratch_shapes=[
            pltpu.VMEM((pieces, rows, DEPTH), jnp.bfloat16),
            pltpu.VMEM((pieces, row_width, DEPTH), jnp.bfloat16),
            pltpu.VMEM((row_width, rows), jnp.float32),
            pltpu.SMEM(lengths.shape, jnp.int32),
            pltpu.SMEM(destination.shape, jnp.int32),
            pltpu.VMEM((1, LAT), jnp.float32),
            pltpu.VMEM((ROPE // 2, 128), jnp.float32),
            pltpu.VMEM((ROPE, rows), jnp.float32),
            pltpu.VMEM((LAT, 128), jnp.float32),
            pltpu.VMEM((owners, block_rows, WIDE), jnp.float32),
            pltpu.SMEM((owners,), jnp.int32),
            pltpu.SMEM((owners,), jnp.int32),
            pltpu.SemaphoreType.DMA((2, pieces)),
            pltpu.SemaphoreType.DMA((4,)),
        ],
        name="produce",
    )(
        lengths,
        destination,
        hidden,
        w_turned,
        gain.reshape(1, -1),
        jnp.asarray(frequencies()),
    )


def place_kernel(arrived_ref, out_ref, rows_ref):
    blocks, block_rows, _ = arrived_ref.shape
    width, rows = out_ref.shape
    part = 128 // block_rows
    row = lax.broadcasted_iota(jnp.int32, (rows, 128), 0).astype(jnp.float32)
    lane = lax.broadcasted_iota(jnp.int32, (1, 128), 1)
    within = lax.rem(lane, block_rows).astype(jnp.float32)
    rows_ref[...] = jnp.zeros_like(rows_ref)

    def body(k, carry):
        source = arrived_ref[pl.ds(k * part, part)].astype(jnp.float32).reshape(128, WIDE)
        slot = jnp.transpose(source[:, WIDE - 128 :])[127:128, :]
        select = jnp.where(row == slot * block_rows + within, 1.0, 0.0).astype(jnp.bfloat16)
        rows_ref[...] += jnp.dot(
            select, source.astype(jnp.bfloat16), preferred_element_type=jnp.float32
        )
        return carry

    lax.fori_loop(0, blocks // part, body, 0)
    for at in range(0, width, 128):
        count = min(128, width - at)
        turned = jnp.transpose(rows_ref[:, at : at + 128])
        out_ref[at : at + count, :] = turned[:count].astype(out_ref.dtype)


def place(arrived, width, rows):
    vmem = pl.BlockSpec(memory_space=pltpu.VMEM)
    return pl.pallas_call(
        place_kernel,
        in_specs=[vmem],
        out_specs=vmem,
        out_shape=jax.ShapeDtypeStruct((width, rows), arrived.dtype),
        scratch_shapes=[pltpu.VMEM((rows, WIDE), jnp.float32)],
        compiler_params=params(8),
        name="place",
    )(arrived)


def assemble_kernel(*refs):
    pieces, out_ref = refs[:-1], refs[-1]
    groups = len(pieces)
    group = lax.axis_index("pre")
    width, rows = pieces[0].shape
    step = 64

    def body(k, carry):
        part = pl.ds(pl.multiple_of(k * step, step), step)
        for turn, piece in zip(TURNS, pieces):
            at = pl.multiple_of((group ^ turn) * rows, rows)
            out_ref[part, pl.ds(at, rows)] = piece[part, :]
        return carry

    lax.fori_loop(0, width // step, body, 0)


def assemble(pieces):
    width, rows = pieces[0].shape
    vmem = pl.BlockSpec(memory_space=pltpu.VMEM)
    return pl.pallas_call(
        assemble_kernel,
        in_specs=[vmem] * len(pieces),
        out_specs=vmem,
        out_shape=jax.ShapeDtypeStruct((width, rows * len(pieces)), pieces[0].dtype),
        compiler_params=params(4),
        name="assemble",
    )(*pieces)


def prepare_kernel(
    owners, groups, lengths_ref, request_ref, position_ref, own_hbm,
    bias_ref, valid_ref, own_ref, sem,
):
    copy = pltpu.make_async_copy(own_hbm, own_ref, sem)
    copy.start()
    steps, batch = position_ref.shape
    heads = CUT_HEADS
    count = own_ref.shape[1]
    group, owner = lax.axis_index("pre"), lax.axis_index("dec")
    row = lax.broadcasted_iota(jnp.int32, (heads, count), 1)
    bases = [((group ^ turn) * owners + owner) * count for turn in TURNS]

    def fill(b, carry):
        request = request_ref[b]
        start = jnp.int32(0)
        for r in range(lengths_ref.shape[0] - 1):
            start = start + jnp.where(request > r, lengths_ref[r], 0)
        for s in range(steps):
            stop = start + position_ref[s, b]
            at = pl.ds(pl.multiple_of((s * batch + b) * heads, heads), heads)
            seen = jnp.int32(0)
            for c, base in enumerate(bases):
                bias_ref[at, c * count : (c + 1) * count] = jnp.where(
                    (row >= start - base) & (row < stop - base), 0.0, mask_value
                )
                seen = seen + jnp.where((start < base + count) & (stop > base), 1, 0)
            valid_ref[at, :] = jnp.full((heads, 128), seen, jnp.int32)
        return carry

    lax.fori_loop(0, batch, fill, 0)
    copy.wait()


def prepare(owners, groups, lengths, row_request, step_position, own):
    rows = step_position.size * CUT_HEADS
    smem = pl.BlockSpec(memory_space=pltpu.SMEM)
    vmem = pl.BlockSpec(memory_space=pltpu.VMEM)
    return pl.pallas_call(
        functools.partial(prepare_kernel, owners, groups),
        in_specs=[smem] * 3 + [pl.BlockSpec(memory_space=pl.ANY)],
        out_specs=[vmem] * 3,
        out_shape=[
            jax.ShapeDtypeStruct((rows, groups * own.shape[1]), jnp.float32),
            jax.ShapeDtypeStruct((rows, 128), jnp.int32),
            jax.ShapeDtypeStruct(own.shape, own.dtype),
        ],
        scratch_shapes=[pltpu.SemaphoreType.DMA(())],
        compiler_params=params(8),
        name="prepare",
    )(lengths, row_request, step_position, own)


def attend_kernel(
    bias_ref, valid_ref, latent_ref, rope_ref, k0, k1, k2, k3, w_hbm,
    keep_ref, send_ref, out_ref, w_ref, sems,
):
    chunk_refs = (k0, k1, k2, k3)
    items, cuts, heads, _ = latent_ref.shape
    rows = items * heads
    all_heads = cuts * heads
    count = k0.shape[1]

    def weights_of(cut):
        part = pl.ds(cut * heads, heads)
        return pltpu.make_async_copy(w_hbm.at[part], w_ref.at[part], sems.at[cut])

    for cut in range(cuts):
        weights_of(cut).start()
    out_ref[:, all_heads:, :] = jnp.zeros((items, PAD, 128), jnp.float32)
    head = lax.broadcasted_iota(jnp.int32, (rows, 128), 0) % heads
    lane = lax.broadcasted_iota(jnp.int32, (rows, 128), 1)

    def body(cut, carry):
        latent = latent_ref[:, cut].reshape(rows, LAT)
        rope = rope_ref[:, cut].reshape(rows, ROPE)
        scores = []
        for c, chunk_ref in enumerate(chunk_refs):
            s = jnp.dot(latent, chunk_ref[:LAT, :], preferred_element_type=jnp.float32)
            s += jnp.dot(rope, chunk_ref[LAT:, :], preferred_element_type=jnp.float32)
            scores.append(s + bias_ref[:, c * count : (c + 1) * count])
        peak = jnp.max(functools.reduce(jnp.maximum, scores), axis=1, keepdims=True)
        weights = [jnp.exp2((s - peak) * (score_scale * log2_e)) for s in scores]
        total = jnp.sum(functools.reduce(jnp.add, weights), axis=1, keepdims=True)
        mixed = sum(
            lax.dot_general(
                p.astype(jnp.bfloat16),
                chunk_ref[:LAT, :],
                (((1,), (1,)), ((), ())),
                preferred_element_type=jnp.float32,
            )
            for p, chunk_ref in zip(weights, chunk_refs)
        )
        valid = valid_ref[:, 0:1] > 0
        mixed = mixed * jnp.where(valid, 1.0 / total, 0.0)
        level = jnp.where(valid, peak * score_scale + jnp.log(total), mask_value)
        upper = mixed.astype(jnp.bfloat16)
        lower = (mixed - upper.astype(jnp.float32)).astype(jnp.bfloat16)
        weights_of(cut).wait()
        result = jnp.zeros((rows, 128), jnp.float32)
        both = jnp.concatenate([upper, lower], axis=0)
        for h in range(0, heads, 2):
            pair = jnp.concatenate([w_ref[cut * heads + h], w_ref[cut * heads + h + 1]], axis=1)
            y = jnp.dot(both, pair, preferred_element_type=jnp.float32)
            y = y[:rows] + y[rows:]
            result = jnp.where(head == h, y[:, :128], result)
            result = jnp.where(head == h + 1, y[:, 128:], result)
        at = pl.multiple_of(cut * heads, heads)
        out_ref[:, pl.ds(at, heads), :] = result.reshape(items, heads, 128)
        lines = jnp.where(lane == head + at, level, 0.0).reshape(items, heads, 128)
        lines = jnp.sum(lines, axis=1, keepdims=True)
        out_ref[:, all_heads:, :] += jnp.broadcast_to(lines, (items, PAD, 128))
        return carry

    lax.fori_loop(0, cuts, body, 0)
    half = items // 2
    core = lax.axis_index("dec") & 1

    def hand(i, carry):
        keep_ref[i] = out_ref[core * half + i]
        send_ref[i] = out_ref[(1 - core) * half + i]
        return carry

    lax.fori_loop(0, half, hand, 0)


def attend(bias, valid, latent, rope, chunks, w_up):
    items, heads, _ = latent.shape
    cuts = heads // CUT_HEADS
    vmem = pl.BlockSpec(memory_space=pltpu.VMEM)
    out_shape = jax.ShapeDtypeStruct((items // 2, heads + PAD, 128), jnp.float32)
    return pl.pallas_call(
        attend_kernel,
        in_specs=[vmem] * 8 + [pl.BlockSpec(memory_space=pl.ANY)],
        out_specs=[vmem] * 2,
        out_shape=[out_shape] * 2,
        scratch_shapes=[
            pltpu.VMEM((items, heads + PAD, 128), jnp.float32),
            pltpu.VMEM(w_up.shape, w_up.dtype),
            pltpu.SemaphoreType.DMA((cuts,)),
        ],
        compiler_params=params(48),
        name="attend",
    )(
        bias,
        valid,
        latent.reshape(items, cuts, CUT_HEADS, -1),
        rope.reshape(items, cuts, CUT_HEADS, -1),
        *chunks,
        w_up,
    )


def merge_step(levels):
    peak = functools.reduce(jnp.maximum, levels)
    scales = [jnp.exp(level - peak) for level in levels]
    total = functools.reduce(jnp.add, scales)
    return [scale / total for scale in scales], peak + jnp.log(total)


def spread_columns(line, heads):
    shape = line.shape[:-2] + (heads, line.shape[-1])
    axis = len(shape) - 1
    lane = lax.broadcasted_iota(jnp.int32, shape, axis)
    row = lax.broadcasted_iota(jnp.int32, shape, axis - 1)
    return jnp.sum(jnp.where(lane == row, line, 0.0), axis=axis, keepdims=True)


def pair_kernel(mine_ref, other_ref, out_ref):
    items, depth, _ = mine_ref.shape
    heads = depth - PAD
    step = 4

    def body(k, carry):
        at = pl.ds(k * step, step)
        parts = [mine_ref[at], other_ref[at]]
        scales, level = merge_step([part[:, heads:, :] for part in parts])
        result = sum(
            part[:, :heads, :] * spread_columns(scale[:, 0:1, :], heads)
            for part, scale in zip(parts, scales)
        )
        out_ref[at, :heads, :] = result
        out_ref[at, heads:, :] = level
        return carry

    lax.fori_loop(0, items // step, body, 0)


def merge_pair(mine, other):
    vmem = pl.BlockSpec(memory_space=pltpu.VMEM)
    return pl.pallas_call(
        pair_kernel,
        in_specs=[vmem] * 2,
        out_specs=vmem,
        out_shape=jax.ShapeDtypeStruct(mine.shape, mine.dtype),
        compiler_params=params(4),
        name="merge_pair",
    )(mine, other)


def merge_kernel(last, parts_ref, out_ref):
    sources, _, depth, _ = parts_ref.shape
    heads = depth - PAD
    scales, level = merge_step([parts_ref[k, :, heads:, :] for k in range(sources)])
    result = sum(
        parts_ref[k, :, :heads, :] * spread_columns(scales[k][:, 0:1, :], heads)
        for k in range(sources)
    ).astype(out_ref.dtype)
    for copy in range(out_ref.shape[0]):
        out_ref[copy, :, :heads, :] = result
        if not last:
            out_ref[copy, :, heads:, :] = level


def merge(parts, last):
    sources, items, depth, lanes = parts.shape
    vmem = pl.BlockSpec(memory_space=pltpu.VMEM)
    if last:
        out_shape = jax.ShapeDtypeStruct((SIDE, items, depth - PAD, lanes), jnp.bfloat16)
    else:
        out_shape = jax.ShapeDtypeStruct((SIDE, items, depth, lanes), jnp.float32)
    return pl.pallas_call(
        functools.partial(merge_kernel, last),
        in_specs=[vmem],
        out_specs=vmem,
        out_shape=out_shape,
        compiler_params=params(4),
        name="merge",
    )(parts)


def spread_kernel(mine_ref, other_ref, out_ref, wide_ref):
    half, heads, lanes = mine_ref.shape
    core = lax.axis_index("dec") & 1
    for place_at, ref in ((core, mine_ref), (1 - core, other_ref)):
        for k in range(half):
            at = pl.ds(pl.multiple_of((place_at * half + k) * heads, heads), heads)
            wide_ref[at, :] = ref[k].astype(jnp.float32)

    def body(h, carry):
        piece = wide_ref[pl.ds(h, 2 * half, stride=heads), :]
        at = pl.multiple_of(h * lanes, lanes)
        out_ref[:, pl.ds(at, lanes)] = piece.astype(out_ref.dtype)
        return carry

    lax.fori_loop(0, heads, body, 0, unroll=4)


def spread(mine, other):
    half, heads, lanes = mine.shape
    vmem = pl.BlockSpec(memory_space=pltpu.VMEM)
    return pl.pallas_call(
        spread_kernel,
        in_specs=[vmem] * 2,
        out_specs=vmem,
        out_shape=jax.ShapeDtypeStruct((2 * half, heads * lanes), mine.dtype),
        scratch_shapes=[pltpu.VMEM((2 * half * heads, lanes), jnp.float32)],
        compiler_params=params(4),
        name="spread",
    )(mine, other)


def exchange(piece, groups, turn):
    return lax.ppermute(piece, "pre", [(i, i ^ turn) for i in range(groups)])


def around(piece, groups, owners):
    core = lax.axis_index("dec") % 2
    first = exchange(piece, groups, 3)
    second = exchange(piece, groups, 1)
    forward = [
        (g * owners + d, (g ^ (1 if d % 2 == 0 else 3)) * owners + d)
        for g in range(groups)
        for d in range(owners)
    ]
    chosen = jnp.where(core == 0, first, second)
    far = lax.ppermute(chosen, ("pre", "dec"), forward)
    return [piece, first, second, far], chosen


def per_device(
    hidden,
    w_down,
    kv_gain,
    query_latent,
    query_rope,
    w_up_value,
    request_rows,
    row_request,
    step_position,
    destination,
):
    groups = lax.axis_size("pre")
    owners = lax.axis_size("dec")
    steps, batch, heads, _ = query_latent.shape
    items = steps * batch
    line_x = [
        [2 * (y * SIDE + x) + core for x in range(SIDE)] for y in range(SIDE) for core in range(2)
    ]
    line_y = [
        [2 * (y * SIDE + x) + core for y in range(SIDE)] for x in range(SIDE) for core in range(2)
    ]
    sibling = [(d, d ^ 1) for d in range(owners)]

    produced, packed = produce(
        groups, owners, request_rows, destination, hidden, w_down.T, kv_gain
    )
    chunks, chosen = around(produced, groups, owners)

    exchanged = functools.partial(
        lax.all_to_all, axis_name="dec", split_axis=0, concat_axis=0, tiled=True
    )
    lengths, _ = lax.optimization_barrier((request_rows, chosen))
    bias, valid, chunks[0] = prepare(
        owners, groups, lengths, row_request, step_position, produced
    )
    keep, send = attend(
        bias,
        valid,
        query_latent.reshape(items, heads, -1),
        query_rope.reshape(items, heads, -1),
        chunks,
        w_up_value,
    )
    arrived = exchanged(packed)
    quarter = place(arrived, *produced.shape)
    keep, _ = lax.optimization_barrier((keep, quarter))
    parts = merge_pair(keep, lax.ppermute(send, "dec", sibling))
    parts = exchanged(parts, axis_index_groups=line_x)
    parts = merge(parts.reshape((SIDE, SIDE) + parts.shape[1:]), False)
    late_quarter, _ = lax.optimization_barrier((quarter, parts))
    result = merge(exchanged(parts, axis_index_groups=line_y), True)
    result = exchanged(result, axis_index_groups=line_x)
    result = result.reshape((SIDE * SIDE,) + result.shape[2:])
    result = spread(result, lax.ppermute(result, "dec", sibling))

    pieces = [quarter] + [exchange(quarter, groups, turn) for turn in TURNS[1:3]]
    kv_cache = assemble(pieces + [exchange(late_quarter, groups, TURNS[3])]).T
    attention_out = result.reshape(steps, batch, -1)
    return (attention_out, kv_cache)


def solution(mesh):
    return jax.shard_map(
        per_device,
        mesh=mesh,
        in_specs=(
            P(("pre", "dec"), None),
            P(),
            P(),
            P(None, None, "pre", None),
            P(None, None, "pre", None),
            P("pre", None, None),
            P(),
            P(),
            P(),
            P(),
        ),
        out_specs=(P(None, None, "pre"), P("dec", None)),
        check_vma=False,
    )
```

```python
import functools
import math

import jax
import jax.numpy as jnp
import numpy as np
from jax import lax
from jax.experimental import pallas as pl
from jax.experimental.pallas import tpu as pltpu
from jax.sharding import PartitionSpec as P

LAT = 512
ROPE = 64
MOST = 2
PAD = 8
SIDE = 4
TURNS = (0, 3, 1, 2)
CUT_HEADS = 8
DEPTH = 1792

score_scale = 0.07216878364870323
mask_value = -1e30
norm_eps = 1e-06
log2_e = 1.4426950408889634


def frequencies():
    half = ROPE // 2
    pair_index = np.arange(half, dtype=np.float64)
    frequency = np.exp(pair_index * (-2.0 * math.log(10000.0) / ROPE)).astype(np.float32)
    return np.tile(frequency[:, None], (1, 128))


WIDE = 640


def shift_of(count):
    assert count & (count - 1) == 0
    return count.bit_length() - 1


def params(megabytes):
    return pltpu.CompilerParams(vmem_limit_bytes=megabytes * 1024 * 1024)


def produce_kernel(
    groups, owners, lengths_hbm, dest_hbm, hidden_hbm, w_hbm, gain_hbm, freq_hbm,
    out_ref, packed_ref, hidden_ref, w_ref, acc_ref, lengths_ref, dest_ref, gain_ref, freq_ref,
    turn_ref, column_ref, rows_ref, count_ref, slot_ref, sems, small_sems,
):
    pieces, rows, depth = hidden_ref.shape
    half = ROPE // 2
    small = [
        pltpu.make_async_copy(source, target, small_sems.at[k])
        for k, (source, target) in enumerate(
            (
                (lengths_hbm, lengths_ref),
                (dest_hbm, dest_ref),
                (gain_hbm, gain_ref),
                (freq_hbm, freq_ref),
            )
        )
    ]

    def copies(k):
        columns = pl.ds(pl.multiple_of(k * depth, depth), depth)
        return (
            pltpu.make_async_copy(hidden_hbm.at[:, columns], hidden_ref.at[k], sems.at[0, k]),
            pltpu.make_async_copy(w_hbm.at[:, columns], w_ref.at[k], sems.at[1, k]),
        )

    def begin(k, carry):
        for copy in copies(k):
            copy.start()
        return carry

    for copy in small:
        copy.start()
    lax.fori_loop(0, pieces, begin, 0)
    acc_ref[...] = jnp.zeros_like(acc_ref)
    packed_ref[...] = jnp.full(packed_ref.shape, -1.0, packed_ref.dtype)
    for copy in small:
        copy.wait()
    group = lax.axis_index("pre")
    device = group * owners + lax.axis_index("dec")
    block_rows = packed_ref.shape[1]
    blocks = rows // block_rows

    def clear(owner, carry):
        count_ref[owner] = 0
        return carry

    def choose(b, carry):
        owner = lax.shift_right_logical(dest_ref[device * blocks + b], shift_of(groups * owners))
        rank = count_ref[owner]
        count_ref[owner] = rank + 1
        slot_ref[b] = owner * MOST + rank
        return carry

    lax.fori_loop(0, owners, clear, 0)
    lax.fori_loop(0, blocks, choose, 0)
    row = device * rows + lax.broadcasted_iota(jnp.int32, (1, rows), 1)
    start = jnp.zeros((1, rows), jnp.int32)
    first_row = jnp.int32(0)
    for r in range(lengths_ref.shape[0] - 1):
        first_row = first_row + lengths_ref[r]
        start = jnp.where(row >= first_row, first_row, start)
    angles = freq_ref[:, 0:1] * (row - start).astype(jnp.float32)
    turn_ref[:half, :] = jnp.cos(angles)
    turn_ref[half:, :] = jnp.sin(angles)
    column_ref[...] = jnp.transpose(jnp.broadcast_to(gain_ref[...], (128, LAT)))

    def body(k, carry):
        for copy in copies(k):
            copy.wait()
        acc_ref[...] += lax.dot_general(
            w_ref[k],
            hidden_ref[k],
            (((1,), (1,)), ((), ())),
            preferred_element_type=jnp.float32,
        )
        return carry

    lax.fori_loop(0, pieces, body, 0)
    latent = acc_ref[:LAT, :]
    inverse_rms = lax.rsqrt(jnp.mean(latent * latent, axis=0, keepdims=True) + norm_eps)
    out_ref[:LAT, :] = (latent * inverse_rms * column_ref[:, 0:1]).astype(out_ref.dtype)
    cosine, sine = turn_ref[:half, :], turn_ref[half:, :]
    first = acc_ref[LAT : LAT + half, :]
    second = acc_ref[LAT + half :, :]
    turned = first * cosine - second * sine
    out_ref[LAT : LAT + half, :] = turned.astype(out_ref.dtype)
    turned = second * cosine + first * sine
    out_ref[LAT + half :, :] = turned.astype(out_ref.dtype)
    width = out_ref.shape[0]
    for at in range(0, width, 128):
        count = min(128, width - at)
        wide = out_ref[at : at + count, :].astype(jnp.float32)
        if count < 128:
            wide = jnp.concatenate([wide, jnp.zeros((128 - count, rows), jnp.float32)], axis=0)
        rows_ref[:, :, at : at + 128] = jnp.transpose(wide).reshape(blocks, block_rows, 128)
    lane = lax.broadcasted_iota(jnp.int32, (block_rows, WIDE), 1)

    def put(b, carry):
        place_at = (dest_ref[device * blocks + b] & (groups * owners - 1)) - group * owners
        block = jnp.where(lane < width, rows_ref[b], place_at.astype(jnp.float32))
        packed_ref[slot_ref[b]] = block.astype(packed_ref.dtype)
        return carry

    lax.fori_loop(0, blocks, put, 0, unroll=4)


def produce(groups, owners, lengths, destination, hidden, w_turned, gain):
    rows, width = hidden.shape
    row_width = w_turned.shape[0]
    pieces = width // DEPTH
    block_rows = rows // owners
    vmem = pl.BlockSpec(memory_space=pltpu.VMEM)
    return pl.pallas_call(
        functools.partial(produce_kernel, groups, owners),
        in_specs=[pl.BlockSpec(memory_space=pltpu.HBM)] * 6,
        out_specs=[vmem, vmem],
        out_shape=[
            jax.ShapeDtypeStruct((row_width, rows), jnp.bfloat16),
            jax.ShapeDtypeStruct((owners * MOST, block_rows, WIDE), jnp.bfloat16),
        ],
        scratch_shapes=[
            pltpu.VMEM((pieces, rows, DEPTH), jnp.bfloat16),
            pltpu.VMEM((pieces, row_width, DEPTH), jnp.bfloat16),
            pltpu.VMEM((row_width, rows), jnp.float32),
            pltpu.SMEM(lengths.shape, jnp.int32),
            pltpu.SMEM(destination.shape, jnp.int32),
            pltpu.VMEM((1, LAT), jnp.float32),
            pltpu.VMEM((ROPE // 2, 128), jnp.float32),
            pltpu.VMEM((ROPE, rows), jnp.float32),
            pltpu.VMEM((LAT, 128), jnp.float32),
            pltpu.VMEM((owners, block_rows, WIDE), jnp.float32),
            pltpu.SMEM((owners,), jnp.int32),
            pltpu.SMEM((owners,), jnp.int32),
            pltpu.SemaphoreType.DMA((2, pieces)),
            pltpu.SemaphoreType.DMA((4,)),
        ],
        name="produce",
    )(
        lengths,
        destination,
        hidden,
        w_turned,
        gain.reshape(1, -1),
        jnp.asarray(frequencies()),
    )


def place_kernel(arrived_ref, out_ref, rows_ref):
    blocks, block_rows, _ = arrived_ref.shape
    width, rows = out_ref.shape
    part = 128 // block_rows
    row = lax.broadcasted_iota(jnp.int32, (rows, 128), 0).astype(jnp.float32)
    lane = lax.broadcasted_iota(jnp.int32, (1, 128), 1)
    within = lax.rem(lane, block_rows).astype(jnp.float32)
    rows_ref[...] = jnp.zeros_like(rows_ref)

    def body(k, carry):
        source = arrived_ref[pl.ds(k * part, part)].astype(jnp.float32).reshape(128, WIDE)
        slot = jnp.transpose(source[:, WIDE - 128 :])[127:128, :]
        select = jnp.where(row == slot * block_rows + within, 1.0, 0.0).astype(jnp.bfloat16)
        rows_ref[...] += jnp.dot(
            select, source.astype(jnp.bfloat16), preferred_element_type=jnp.float32
        )
        return carry

    lax.fori_loop(0, blocks // part, body, 0)
    for at in range(0, width, 128):
        count = min(128, width - at)
        turned = jnp.transpose(rows_ref[:, at : at + 128])
        out_ref[at : at + count, :] = turned[:count].astype(out_ref.dtype)


def place(arrived, width, rows):
    vmem = pl.BlockSpec(memory_space=pltpu.VMEM)
    return pl.pallas_call(
        place_kernel,
        in_specs=[vmem],
        out_specs=vmem,
        out_shape=jax.ShapeDtypeStruct((width, rows), arrived.dtype),
        scratch_shapes=[pltpu.VMEM((rows, WIDE), jnp.float32)],
        compiler_params=params(8),
        name="place",
    )(arrived)


def prepare_kernel(
    owners, groups, lengths_ref, request_ref, position_ref, own_hbm,
    bias_ref, valid_ref, own_ref, sem,
):
    copy = pltpu.make_async_copy(own_hbm, own_ref, sem)
    copy.start()
    steps, batch = position_ref.shape
    heads = CUT_HEADS
    count = own_ref.shape[1]
    group, owner = lax.axis_index("pre"), lax.axis_index("dec")
    row = lax.broadcasted_iota(jnp.int32, (heads, count), 1)
    bases = [((group ^ turn) * owners + owner) * count for turn in TURNS]

    def fill(b, carry):
        request = request_ref[b]
        start = jnp.int32(0)
        for r in range(lengths_ref.shape[0] - 1):
            start = start + jnp.where(request > r, lengths_ref[r], 0)
        for s in range(steps):
            stop = start + position_ref[s, b]
            at = pl.ds(pl.multiple_of((s * batch + b) * heads, heads), heads)
            seen = jnp.int32(0)
            for c, base in enumerate(bases):
                bias_ref[at, c * count : (c + 1) * count] = jnp.where(
                    (row >= start - base) & (row < stop - base), 0.0, mask_value
                )
                seen = seen + jnp.where((start < base + count) & (stop > base), 1, 0)
            valid_ref[at, :] = jnp.full((heads, 128), seen, jnp.int32)
        return carry

    lax.fori_loop(0, batch, fill, 0)
    copy.wait()


def prepare(owners, groups, lengths, row_request, step_position, own):
    rows = step_position.size * CUT_HEADS
    smem = pl.BlockSpec(memory_space=pltpu.SMEM)
    vmem = pl.BlockSpec(memory_space=pltpu.VMEM)
    return pl.pallas_call(
        functools.partial(prepare_kernel, owners, groups),
        in_specs=[smem] * 3 + [pl.BlockSpec(memory_space=pl.ANY)],
        out_specs=[vmem] * 3,
        out_shape=[
            jax.ShapeDtypeStruct((rows, groups * own.shape[1]), jnp.float32),
            jax.ShapeDtypeStruct((rows, 128), jnp.int32),
            jax.ShapeDtypeStruct(own.shape, own.dtype),
        ],
        scratch_shapes=[pltpu.SemaphoreType.DMA(())],
        compiler_params=params(8),
        name="prepare",
    )(lengths, row_request, step_position, own)


def attend_kernel(
    bias_ref, valid_ref, latent_ref, rope_ref, k0, k1, k2, k3, w_hbm,
    keep_ref, send_ref, out_ref, w_ref, sems,
):
    chunk_refs = (k0, k1, k2, k3)
    items, cuts, heads, _ = latent_ref.shape
    rows = items * heads
    all_heads = cuts * heads
    count = k0.shape[1]

    def weights_of(cut):
        part = pl.ds(cut * heads, heads)
        return pltpu.make_async_copy(w_hbm.at[part], w_ref.at[part], sems.at[cut])

    for cut in range(cuts):
        weights_of(cut).start()
    out_ref[:, all_heads:, :] = jnp.zeros((items, PAD, 128), jnp.float32)
    head = lax.broadcasted_iota(jnp.int32, (rows, 128), 0) % heads
    lane = lax.broadcasted_iota(jnp.int32, (rows, 128), 1)

    def body(cut, carry):
        latent = latent_ref[:, cut].reshape(rows, LAT)
        rope = rope_ref[:, cut].reshape(rows, ROPE)
        scores = []
        for c, chunk_ref in enumerate(chunk_refs):
            s = jnp.dot(latent, chunk_ref[:LAT, :], preferred_element_type=jnp.float32)
            s += jnp.dot(rope, chunk_ref[LAT:, :], preferred_element_type=jnp.float32)
            scores.append(s + bias_ref[:, c * count : (c + 1) * count])
        peak = jnp.max(functools.reduce(jnp.maximum, scores), axis=1, keepdims=True)
        weights = [jnp.exp2((s - peak) * (score_scale * log2_e)) for s in scores]
        total = jnp.sum(functools.reduce(jnp.add, weights), axis=1, keepdims=True)
        mixed = sum(
            lax.dot_general(
                p.astype(jnp.bfloat16),
                chunk_ref[:LAT, :],
                (((1,), (1,)), ((), ())),
                preferred_element_type=jnp.float32,
            )
            for p, chunk_ref in zip(weights, chunk_refs)
        )
        valid = valid_ref[:, 0:1] > 0
        mixed = mixed * jnp.where(valid, 1.0 / total, 0.0)
        level = jnp.where(valid, peak * score_scale + jnp.log(total), mask_value)
        upper = mixed.astype(jnp.bfloat16)
        lower = (mixed - upper.astype(jnp.float32)).astype(jnp.bfloat16)
        weights_of(cut).wait()
        result = jnp.zeros((rows, 128), jnp.float32)
        both = jnp.concatenate([upper, lower], axis=0)
        for h in range(0, heads, 2):
            pair = jnp.concatenate([w_ref[cut * heads + h], w_ref[cut * heads + h + 1]], axis=1)
            y = jnp.dot(both, pair, preferred_element_type=jnp.float32)
            y = y[:rows] + y[rows:]
            result = jnp.where(head == h, y[:, :128], result)
            result = jnp.where(head == h + 1, y[:, 128:], result)
        at = pl.multiple_of(cut * heads, heads)
        out_ref[:, pl.ds(at, heads), :] = result.reshape(items, heads, 128)
        lines = jnp.where(lane == head + at, level, 0.0).reshape(items, heads, 128)
        lines = jnp.sum(lines, axis=1, keepdims=True)
        out_ref[:, all_heads:, :] += jnp.broadcast_to(lines, (items, PAD, 128))
        return carry

    lax.fori_loop(0, cuts, body, 0, unroll=2)
    half = items // 2
    core = lax.axis_index("dec") & 1

    def hand(i, carry):
        keep_ref[i] = out_ref[core * half + half - 1 - i]
        send_ref[i] = out_ref[(1 - core) * half + half - 1 - i]
        return carry

    lax.fori_loop(0, half, hand, 0)


def attend(bias, valid, latent, rope, chunks, w_up):
    items, heads, _ = latent.shape
    cuts = heads // CUT_HEADS
    vmem = pl.BlockSpec(memory_space=pltpu.VMEM)
    out_shape = jax.ShapeDtypeStruct((items // 2, heads + PAD, 128), jnp.float32)
    return pl.pallas_call(
        attend_kernel,
        in_specs=[vmem] * 8 + [pl.BlockSpec(memory_space=pl.ANY)],
        out_specs=[vmem] * 2,
        out_shape=[out_shape] * 2,
        scratch_shapes=[
            pltpu.VMEM((items, heads + PAD, 128), jnp.float32),
            pltpu.VMEM(w_up.shape, w_up.dtype),
            pltpu.SemaphoreType.DMA((cuts,)),
        ],
        compiler_params=params(48),
        name="attend",
    )(
        bias,
        valid,
        latent.reshape(items, cuts, CUT_HEADS, -1),
        rope.reshape(items, cuts, CUT_HEADS, -1),
        *chunks,
        w_up,
    )


def merge_step(levels):
    peak = functools.reduce(jnp.maximum, levels)
    scales = [jnp.exp(level - peak) for level in levels]
    total = functools.reduce(jnp.add, scales)
    return [scale / total for scale in scales], peak + jnp.log(total)


def spread_columns(line, heads):
    shape = line.shape[:-2] + (heads, line.shape[-1])
    axis = len(shape) - 1
    lane = lax.broadcasted_iota(jnp.int32, shape, axis)
    row = lax.broadcasted_iota(jnp.int32, shape, axis - 1)
    return jnp.sum(jnp.where(lane == row, line, 0.0), axis=axis, keepdims=True)


def pair_kernel(mine_ref, other_ref, out_ref):
    items, depth, _ = mine_ref.shape
    heads = depth - PAD
    step = 4

    def body(k, carry):
        at = pl.ds(k * step, step)
        parts = [mine_ref[at], other_ref[at]]
        scales, level = merge_step([part[:, heads:, :] for part in parts])
        result = sum(
            part[:, :heads, :] * spread_columns(scale[:, 0:1, :], heads)
            for part, scale in zip(parts, scales)
        )
        out_ref[at, :heads, :] = result
        out_ref[at, heads:, :] = level
        return carry

    lax.fori_loop(0, items // step, body, 0)


def merge_pair(mine, other):
    vmem = pl.BlockSpec(memory_space=pltpu.VMEM)
    return pl.pallas_call(
        pair_kernel,
        in_specs=[vmem] * 2,
        out_specs=vmem,
        out_shape=jax.ShapeDtypeStruct(mine.shape, mine.dtype),
        compiler_params=params(4),
        name="merge_pair",
    )(mine, other)


def merge_kernel(parts_ref, out_ref, scale_ref):
    sources, depth, lanes = parts_ref.shape
    heads = depth - PAD
    scales, _ = merge_step([parts_ref[k, heads:, :] for k in range(sources)])
    for k in range(sources):
        scale_ref[k] = scales[k]

    def body(k, so_far):
        return so_far + parts_ref[k, :heads, :] * spread_columns(scale_ref[k][0:1, :], heads)

    result = lax.fori_loop(
        0, sources, body, jnp.zeros((heads, lanes), jnp.float32), unroll=4
    ).astype(out_ref.dtype)
    for copy in range(out_ref.shape[0]):
        out_ref[copy] = result


def merge(parts):
    sources, depth, lanes = parts.shape
    vmem = pl.BlockSpec(memory_space=pltpu.VMEM)
    return pl.pallas_call(
        merge_kernel,
        in_specs=[vmem],
        out_specs=vmem,
        out_shape=jax.ShapeDtypeStruct((sources, depth - PAD, lanes), jnp.bfloat16),
        scratch_shapes=[pltpu.VMEM((sources, PAD, lanes), jnp.float32)],
        compiler_params=params(4),
        name="merge",
    )(parts)


def finish_kernel(mine_ref, other_ref, p0, p1, p2, p3, out_ref, cache_hbm, wide_ref, sems):
    group = lax.axis_index("pre")
    copies = []
    for k, (turn, piece) in enumerate(zip(TURNS, (p0, p1, p2, p3))):
        rows = piece.shape[1]
        at = pl.multiple_of((group ^ turn) * rows, rows)
        copies.append(
            pltpu.make_async_copy(piece, cache_hbm.at[:, pl.ds(at, rows)], sems.at[k])
        )
    for copy in copies:
        copy.start()
    half, heads, lanes = mine_ref.shape
    core = lax.axis_index("dec") & 1

    def widen(k, carry):
        for place_at, ref in ((core, mine_ref), (1 - core, other_ref)):
            item = place_at * half + half - 1 - k
            at = pl.ds(pl.multiple_of(item * heads, heads), heads)
            wide_ref[at, :] = ref[k].astype(jnp.float32)
        return carry

    lax.fori_loop(0, half, widen, 0, unroll=4)

    def body(h, carry):
        piece = wide_ref[pl.ds(h, 2 * half, stride=heads), :]
        at = pl.multiple_of(h * lanes, lanes)
        out_ref[:, pl.ds(at, lanes)] = piece.astype(out_ref.dtype)
        return carry

    lax.fori_loop(0, heads, body, 0, unroll=4)
    for copy in copies:
        copy.wait()


def finish(mine, other, pieces):
    half, heads, lanes = mine.shape
    width, rows = pieces[0].shape
    vmem = pl.BlockSpec(memory_space=pltpu.VMEM)
    return pl.pallas_call(
        finish_kernel,
        in_specs=[vmem] * 6,
        out_specs=[vmem, pl.BlockSpec(memory_space=pl.ANY)],
        out_shape=[
            jax.ShapeDtypeStruct((2 * half, heads * lanes), mine.dtype),
            jax.ShapeDtypeStruct((width, rows * len(pieces)), pieces[0].dtype),
        ],
        scratch_shapes=[
            pltpu.VMEM((2 * half * heads, lanes), jnp.float32),
            pltpu.SemaphoreType.DMA((len(pieces),)),
        ],
        compiler_params=params(6),
        name="finish",
    )(mine, other, *pieces)


def exchange(piece, groups, turn):
    return lax.ppermute(piece, "pre", [(i, i ^ turn) for i in range(groups)])


def around(piece, groups, owners):
    core = lax.axis_index("dec") % 2
    first = exchange(piece, groups, 3)
    second = exchange(piece, groups, 1)
    forward = [
        (g * owners + d, (g ^ (1 if d % 2 == 0 else 3)) * owners + d)
        for g in range(groups)
        for d in range(owners)
    ]
    chosen = jnp.where(core == 0, first, second)
    far = lax.ppermute(chosen, ("pre", "dec"), forward)
    return [piece, first, second, far], chosen


def per_device(
    hidden,
    w_down,
    kv_gain,
    query_latent,
    query_rope,
    w_up_value,
    request_rows,
    row_request,
    step_position,
    destination,
):
    groups = lax.axis_size("pre")
    owners = lax.axis_size("dec")
    steps, batch, heads, _ = query_latent.shape
    items = steps * batch
    plane = [[2 * k + core for k in reversed(range(SIDE * SIDE))] for core in range(2)]
    sibling = [(d, d ^ 1) for d in range(owners)]

    produced, packed = produce(
        groups, owners, request_rows, destination, hidden, w_down.T, kv_gain
    )
    chunks, chosen = around(produced, groups, owners)

    exchanged = functools.partial(
        lax.all_to_all, axis_name="dec", split_axis=0, concat_axis=0, tiled=True
    )
    lengths, _ = lax.optimization_barrier((request_rows, chosen))
    bias, valid, chunks[0] = prepare(
        owners, groups, lengths, row_request, step_position, produced
    )
    keep, send = attend(
        bias,
        valid,
        query_latent.reshape(items, heads, -1),
        query_rope.reshape(items, heads, -1),
        chunks,
        w_up_value,
    )
    arrived = exchanged(packed)
    quarter = place(arrived, *produced.shape)
    pieces = [quarter] + [exchange(quarter, groups, turn) for turn in TURNS[1:]]

    keep, _ = lax.optimization_barrier((keep, quarter))
    parts = merge_pair(keep, lax.ppermute(send, "dec", sibling))
    result = merge(exchanged(parts, axis_index_groups=plane))
    result = exchanged(result, axis_index_groups=plane)
    result, kv_cache = finish(result, lax.ppermute(result, "dec", sibling), pieces)
    attention_out = result.reshape(steps, batch, -1)
    kv_cache = kv_cache.T
    return (attention_out, kv_cache)


def solution(mesh):
    return jax.shard_map(
        per_device,
        mesh=mesh,
        in_specs=(
            P(("pre", "dec"), None),
            P(),
            P(),
            P(None, None, "pre", None),
            P(None, None, "pre", None),
            P("pre", None, None),
            P(),
            P(),
            P(),
            P(),
        ),
        out_specs=(P(None, None, "pre"), P("dec", None)),
        check_vma=False,
    )
```

```python
import functools
import math

import jax
import jax.numpy as jnp
import numpy as np
from jax import lax
from jax.experimental import pallas as pl
from jax.experimental.pallas import tpu as pltpu
from jax.sharding import PartitionSpec as P

LAT = 512
ROPE = 64
MOST = 2
PAD = 8
SIDE = 4
TURNS = (0, 3, 1, 2)
CUT_HEADS = 8
DEPTH = 1792

score_scale = 0.07216878364870323
mask_value = -1e30
norm_eps = 1e-06
log2_e = 1.4426950408889634


def frequencies():
    half = ROPE // 2
    pair_index = np.arange(half, dtype=np.float64)
    frequency = np.exp(pair_index * (-2.0 * math.log(10000.0) / ROPE)).astype(np.float32)
    return np.tile(frequency[:, None], (1, 128))


WIDE = 640


def shift_of(count):
    assert count & (count - 1) == 0
    return count.bit_length() - 1


def params(megabytes):
    return pltpu.CompilerParams(vmem_limit_bytes=megabytes * 1024 * 1024)


def produce_kernel(
    groups, owners, lengths_hbm, dest_hbm, hidden_hbm, w_hbm, gain_hbm, freq_hbm,
    out_ref, packed_ref, hidden_ref, w_ref, acc_ref, lengths_ref, dest_ref, gain_ref, freq_ref,
    turn_ref, column_ref, rows_ref, count_ref, slot_ref, sems, small_sems,
):
    pieces, rows, depth = hidden_ref.shape
    half = ROPE // 2
    small = [
        pltpu.make_async_copy(source, target, small_sems.at[k])
        for k, (source, target) in enumerate(
            (
                (lengths_hbm, lengths_ref),
                (dest_hbm, dest_ref),
                (gain_hbm, gain_ref),
                (freq_hbm, freq_ref),
            )
        )
    ]

    def copies(k):
        columns = pl.ds(pl.multiple_of(k * depth, depth), depth)
        return (
            pltpu.make_async_copy(hidden_hbm.at[:, columns], hidden_ref.at[k], sems.at[0, k]),
            pltpu.make_async_copy(w_hbm.at[:, columns], w_ref.at[k], sems.at[1, k]),
        )

    def begin(k, carry):
        for copy in copies(k):
            copy.start()
        return carry

    for copy in small:
        copy.start()
    lax.fori_loop(0, pieces, begin, 0)
    acc_ref[...] = jnp.zeros_like(acc_ref)
    packed_ref[...] = jnp.full(packed_ref.shape, -1.0, packed_ref.dtype)
    for copy in small:
        copy.wait()
    group = lax.axis_index("pre")
    device = group * owners + lax.axis_index("dec")
    block_rows = packed_ref.shape[1]
    blocks = rows // block_rows

    def clear(owner, carry):
        count_ref[owner] = 0
        return carry

    def choose(b, carry):
        owner = lax.shift_right_logical(dest_ref[device * blocks + b], shift_of(groups * owners))
        rank = count_ref[owner]
        count_ref[owner] = rank + 1
        slot_ref[b] = owner * MOST + rank
        return carry

    lax.fori_loop(0, owners, clear, 0)
    lax.fori_loop(0, blocks, choose, 0)
    row = device * rows + lax.broadcasted_iota(jnp.int32, (1, rows), 1)
    start = jnp.zeros((1, rows), jnp.int32)
    first_row = jnp.int32(0)
    for r in range(lengths_ref.shape[0] - 1):
        first_row = first_row + lengths_ref[r]
        start = jnp.where(row >= first_row, first_row, start)
    angles = freq_ref[:, 0:1] * (row - start).astype(jnp.float32)
    turn_ref[:half, :] = jnp.cos(angles)
    turn_ref[half:, :] = jnp.sin(angles)
    column_ref[...] = jnp.transpose(jnp.broadcast_to(gain_ref[...], (128, LAT)))

    def body(k, carry):
        for copy in copies(k):
            copy.wait()
        acc_ref[...] += lax.dot_general(
            w_ref[k],
            hidden_ref[k],
            (((1,), (1,)), ((), ())),
            preferred_element_type=jnp.float32,
        )
        return carry

    lax.fori_loop(0, pieces, body, 0)
    latent = acc_ref[:LAT, :]
    inverse_rms = lax.rsqrt(jnp.mean(latent * latent, axis=0, keepdims=True) + norm_eps)
    out_ref[:LAT, :] = (latent * inverse_rms * column_ref[:, 0:1]).astype(out_ref.dtype)
    cosine, sine = turn_ref[:half, :], turn_ref[half:, :]
    first = acc_ref[LAT : LAT + half, :]
    second = acc_ref[LAT + half :, :]
    turned = first * cosine - second * sine
    out_ref[LAT : LAT + half, :] = turned.astype(out_ref.dtype)
    turned = second * cosine + first * sine
    out_ref[LAT + half :, :] = turned.astype(out_ref.dtype)
    width = out_ref.shape[0]
    for at in range(0, width, 128):
        count = min(128, width - at)
        wide = out_ref[at : at + count, :].astype(jnp.float32)
        if count < 128:
            wide = jnp.concatenate([wide, jnp.zeros((128 - count, rows), jnp.float32)], axis=0)
        rows_ref[:, :, at : at + 128] = jnp.transpose(wide).reshape(blocks, block_rows, 128)
    lane = lax.broadcasted_iota(jnp.int32, (block_rows, WIDE), 1)

    def put(b, carry):
        place_at = (dest_ref[device * blocks + b] & (groups * owners - 1)) - group * owners
        block = jnp.where(lane < width, rows_ref[b], place_at.astype(jnp.float32))
        packed_ref[slot_ref[b]] = block.astype(packed_ref.dtype)
        return carry

    lax.fori_loop(0, blocks, put, 0, unroll=4)


def produce(groups, owners, lengths, destination, hidden, w_turned, gain):
    rows, width = hidden.shape
    row_width = w_turned.shape[0]
    pieces = width // DEPTH
    block_rows = rows // owners
    vmem = pl.BlockSpec(memory_space=pltpu.VMEM)
    return pl.pallas_call(
        functools.partial(produce_kernel, groups, owners),
        in_specs=[pl.BlockSpec(memory_space=pltpu.HBM)] * 6,
        out_specs=[vmem, vmem],
        out_shape=[
            jax.ShapeDtypeStruct((row_width, rows), jnp.bfloat16),
            jax.ShapeDtypeStruct((owners * MOST, block_rows, WIDE), jnp.bfloat16),
        ],
        scratch_shapes=[
            pltpu.VMEM((pieces, rows, DEPTH), jnp.bfloat16),
            pltpu.VMEM((pieces, row_width, DEPTH), jnp.bfloat16),
            pltpu.VMEM((row_width, rows), jnp.float32),
            pltpu.SMEM(lengths.shape, jnp.int32),
            pltpu.SMEM(destination.shape, jnp.int32),
            pltpu.VMEM((1, LAT), jnp.float32),
            pltpu.VMEM((ROPE // 2, 128), jnp.float32),
            pltpu.VMEM((ROPE, rows), jnp.float32),
            pltpu.VMEM((LAT, 128), jnp.float32),
            pltpu.VMEM((owners, block_rows, WIDE), jnp.float32),
            pltpu.SMEM((owners,), jnp.int32),
            pltpu.SMEM((owners,), jnp.int32),
            pltpu.SemaphoreType.DMA((2, pieces)),
            pltpu.SemaphoreType.DMA((4,)),
        ],
        name="produce",
    )(
        lengths,
        destination,
        hidden,
        w_turned,
        gain.reshape(1, -1),
        jnp.asarray(frequencies()),
    )


def place_kernel(arrived_ref, out_ref, rows_ref):
    blocks, block_rows, _ = arrived_ref.shape
    width, rows = out_ref.shape
    part = 128 // block_rows
    row = lax.broadcasted_iota(jnp.int32, (rows, 128), 0).astype(jnp.float32)
    lane = lax.broadcasted_iota(jnp.int32, (1, 128), 1)
    within = lax.rem(lane, block_rows).astype(jnp.float32)
    rows_ref[...] = jnp.zeros_like(rows_ref)

    def body(k, carry):
        source = arrived_ref[pl.ds(k * part, part)].astype(jnp.float32).reshape(128, WIDE)
        slot = jnp.transpose(source[:, WIDE - 128 :])[127:128, :]
        select = jnp.where(row == slot * block_rows + within, 1.0, 0.0).astype(jnp.bfloat16)
        rows_ref[...] += jnp.dot(
            select, source.astype(jnp.bfloat16), preferred_element_type=jnp.float32
        )
        return carry

    lax.fori_loop(0, blocks // part, body, 0)
    for at in range(0, width, 128):
        count = min(128, width - at)
        turned = jnp.transpose(rows_ref[:, at : at + 128])
        out_ref[at : at + count, :] = turned[:count].astype(out_ref.dtype)


def place(arrived, width, rows):
    vmem = pl.BlockSpec(memory_space=pltpu.VMEM)
    return pl.pallas_call(
        place_kernel,
        in_specs=[vmem],
        out_specs=vmem,
        out_shape=jax.ShapeDtypeStruct((width, rows), arrived.dtype),
        scratch_shapes=[pltpu.VMEM((rows, WIDE), jnp.float32)],
        compiler_params=params(8),
        name="place",
    )(arrived)


def prepare_kernel(
    owners, lengths_ref, request_ref, position_ref, own_hbm,
    near_ref, far_ref, valid_ref, own_ref, sem,
):
    copy = pltpu.make_async_copy(own_hbm, own_ref, sem)
    copy.start()
    steps, batch = position_ref.shape
    heads = CUT_HEADS
    count = own_ref.shape[1]
    group, owner = lax.axis_index("pre"), lax.axis_index("dec")
    row = lax.broadcasted_iota(jnp.int32, (heads, count), 1)
    bases = [((group ^ turn) * owners + owner) * count for turn in TURNS]

    def fill(b, carry):
        request = request_ref[b]
        start = jnp.int32(0)
        for r in range(lengths_ref.shape[0] - 1):
            start = start + jnp.where(request > r, lengths_ref[r], 0)
        for s in range(steps):
            stop = start + position_ref[s, b]
            at = pl.ds(pl.multiple_of((s * batch + b) * heads, heads), heads)
            seen = jnp.int32(0)
            for c, base in enumerate(bases):
                bias = jnp.where((row >= start - base) & (row < stop - base), 0.0, mask_value)
                if c < len(bases) - 1:
                    near_ref[at, c * count : (c + 1) * count] = bias
                else:
                    far_ref[at, :] = bias
                seen = seen + jnp.where((start < base + count) & (stop > base), 1, 0)
            valid_ref[at, :] = jnp.full((heads, 128), seen, jnp.int32)
        return carry

    lax.fori_loop(0, batch, fill, 0)
    copy.wait()


def prepare(owners, groups, lengths, row_request, step_position, own):
    rows = step_position.size * CUT_HEADS
    smem = pl.BlockSpec(memory_space=pltpu.SMEM)
    vmem = pl.BlockSpec(memory_space=pltpu.VMEM)
    return pl.pallas_call(
        functools.partial(prepare_kernel, owners),
        in_specs=[smem] * 3 + [pl.BlockSpec(memory_space=pl.ANY)],
        out_specs=[vmem] * 4,
        out_shape=[
            jax.ShapeDtypeStruct((rows, (groups - 1) * own.shape[1]), jnp.float32),
            jax.ShapeDtypeStruct((rows, own.shape[1]), jnp.float32),
            jax.ShapeDtypeStruct((rows, 128), jnp.int32),
            jax.ShapeDtypeStruct(own.shape, own.dtype),
        ],
        scratch_shapes=[pltpu.SemaphoreType.DMA(())],
        compiler_params=params(8),
        name="prepare",
    )(lengths, row_request, step_position, own)


def scores_of(latent_ref, rope_ref, cut, chunk_refs, bias_ref):
    items, _, heads, _ = latent_ref.shape
    rows = items * heads
    latent = latent_ref[:, cut].reshape(rows, LAT)
    rope = rope_ref[:, cut].reshape(rows, ROPE)
    scores = []
    for c, chunk_ref in enumerate(chunk_refs):
        count = chunk_ref.shape[1]
        s = jnp.dot(latent, chunk_ref[:LAT, :], preferred_element_type=jnp.float32)
        s += jnp.dot(rope, chunk_ref[LAT:, :], preferred_element_type=jnp.float32)
        scores.append(s + bias_ref[:, c * count : (c + 1) * count])
    return scores


def weigh(scores, peak, chunk_refs):
    weights = [jnp.exp2((s - peak) * (score_scale * log2_e)) for s in scores]
    total = jnp.sum(functools.reduce(jnp.add, weights), axis=1, keepdims=True)
    mixed = sum(
        lax.dot_general(
            p.astype(jnp.bfloat16),
            chunk_ref[:LAT, :],
            (((1,), (1,)), ((), ())),
            preferred_element_type=jnp.float32,
        )
        for p, chunk_ref in zip(weights, chunk_refs)
    )
    return total, mixed


def near_kernel(bias_ref, latent_ref, rope_ref, k0, k1, k2, mixed_ref, stat_ref):
    chunk_refs = (k0, k1, k2)
    cuts, rows, _ = mixed_ref.shape
    lane = lax.broadcasted_iota(jnp.int32, (rows, 128), 1)

    def body(cut, carry):
        scores = scores_of(latent_ref, rope_ref, cut, chunk_refs, bias_ref)
        peak = jnp.max(functools.reduce(jnp.maximum, scores), axis=1, keepdims=True)
        total, mixed = weigh(scores, peak, chunk_refs)
        mixed_ref[cut] = mixed
        stat_ref[cut] = jnp.where(lane == 0, peak, total)
        return carry

    lax.fori_loop(0, cuts, body, 0, unroll=2)


def far_kernel(
    bias_ref, valid_ref, latent_ref, rope_ref, k3, mixed_ref, stat_ref, w_hbm,
    keep_ref, send_ref, out_ref, w_ref, sems,
):
    items, cuts, heads, _ = latent_ref.shape
    rows = items * heads
    all_heads = cuts * heads

    def weights_of(cut):
        part = pl.ds(cut * heads, heads)
        return pltpu.make_async_copy(w_hbm.at[part], w_ref.at[part], sems.at[cut])

    for cut in range(cuts):
        weights_of(cut).start()
    out_ref[:, all_heads:, :] = jnp.zeros((items, PAD, 128), jnp.float32)
    head = lax.broadcasted_iota(jnp.int32, (rows, 128), 0) % heads
    lane = lax.broadcasted_iota(jnp.int32, (rows, 128), 1)

    def body(cut, carry):
        scores = scores_of(latent_ref, rope_ref, cut, (k3,), bias_ref)
        old_peak, old_total = stat_ref[cut, :, 0:1], stat_ref[cut, :, 1:2]
        peak = jnp.maximum(old_peak, jnp.max(scores[0], axis=1, keepdims=True))
        factor = jnp.exp2((old_peak - peak) * (score_scale * log2_e))
        total, mixed = weigh(scores, peak, (k3,))
        total += old_total * factor
        valid = valid_ref[:, 0:1] > 0
        inverse = jnp.where(valid, 1.0 / total, 0.0)
        mixed = mixed * inverse + mixed_ref[cut] * (factor * inverse)
        level = jnp.where(valid, peak * score_scale + jnp.log(total), mask_value)
        upper = mixed.astype(jnp.bfloat16)
        lower = (mixed - upper.astype(jnp.float32)).astype(jnp.bfloat16)
        weights_of(cut).wait()
        result = jnp.zeros((rows, 128), jnp.float32)
        both = jnp.concatenate([upper, lower], axis=0)
        for h in range(0, heads, 2):
            pair = jnp.concatenate([w_ref[cut * heads + h], w_ref[cut * heads + h + 1]], axis=1)
            y = jnp.dot(both, pair, preferred_element_type=jnp.float32)
            y = y[:rows] + y[rows:]
            result = jnp.where(head == h, y[:, :128], result)
            result = jnp.where(head == h + 1, y[:, 128:], result)
        at = pl.multiple_of(cut * heads, heads)
        out_ref[:, pl.ds(at, heads), :] = result.reshape(items, heads, 128)
        lines = jnp.where(lane == head + at, level, 0.0).reshape(items, heads, 128)
        lines = jnp.sum(lines, axis=1, keepdims=True)
        out_ref[:, all_heads:, :] += jnp.broadcast_to(lines, (items, PAD, 128))
        return carry

    lax.fori_loop(0, cuts, body, 0, unroll=2)
    half = items // 2
    core = lax.axis_index("dec") & 1

    def hand(i, carry):
        keep_ref[i] = out_ref[core * half + half - 1 - i]
        send_ref[i] = out_ref[(1 - core) * half + half - 1 - i]
        return carry

    lax.fori_loop(0, half, hand, 0)


def attend(near_bias, far_bias, valid, latent, rope, chunks, w_up):
    items, heads, _ = latent.shape
    cuts = heads // CUT_HEADS
    rows = items * CUT_HEADS
    latent = latent.reshape(items, cuts, CUT_HEADS, -1)
    rope = rope.reshape(items, cuts, CUT_HEADS, -1)
    vmem = pl.BlockSpec(memory_space=pltpu.VMEM)
    mixed, stat = pl.pallas_call(
        near_kernel,
        in_specs=[vmem] * 6,
        out_specs=[vmem] * 2,
        out_shape=[
            jax.ShapeDtypeStruct((cuts, rows, LAT), jnp.float32),
            jax.ShapeDtypeStruct((cuts, rows, 128), jnp.float32),
        ],
        compiler_params=params(20),
        name="attend_near",
    )(near_bias, latent, rope, *chunks[:3])
    out_shape = jax.ShapeDtypeStruct((items // 2, heads + PAD, 128), jnp.float32)
    return pl.pallas_call(
        far_kernel,
        in_specs=[vmem] * 7 + [pl.BlockSpec(memory_space=pl.ANY)],
        out_specs=[vmem] * 2,
        out_shape=[out_shape] * 2,
        scratch_shapes=[
            pltpu.VMEM((items, heads + PAD, 128), jnp.float32),
            pltpu.VMEM(w_up.shape, w_up.dtype),
            pltpu.SemaphoreType.DMA((cuts,)),
        ],
        compiler_params=params(47),
        name="attend_far",
    )(far_bias, valid, latent, rope, chunks[3], mixed, stat, w_up)


def merge_step(levels):
    peak = functools.reduce(jnp.maximum, levels)
    scales = [jnp.exp(level - peak) for level in levels]
    total = functools.reduce(jnp.add, scales)
    return [scale / total for scale in scales], peak + jnp.log(total)


def spread_columns(line, heads):
    shape = line.shape[:-2] + (heads, line.shape[-1])
    axis = len(shape) - 1
    lane = lax.broadcasted_iota(jnp.int32, shape, axis)
    row = lax.broadcasted_iota(jnp.int32, shape, axis - 1)
    return jnp.sum(jnp.where(lane == row, line, 0.0), axis=axis, keepdims=True)


def pair_kernel(mine_ref, other_ref, out_ref):
    items, depth, _ = mine_ref.shape
    heads = depth - PAD
    step = 4

    def body(k, carry):
        at = pl.ds(k * step, step)
        parts = [mine_ref[at], other_ref[at]]
        scales, level = merge_step([part[:, heads:, :] for part in parts])
        result = sum(
            part[:, :heads, :] * spread_columns(scale[:, 0:1, :], heads)
            for part, scale in zip(parts, scales)
        )
        out_ref[at, :heads, :] = result
        out_ref[at, heads:, :] = level
        return carry

    lax.fori_loop(0, items // step, body, 0)


def merge_pair(mine, other):
    vmem = pl.BlockSpec(memory_space=pltpu.VMEM)
    return pl.pallas_call(
        pair_kernel,
        in_specs=[vmem] * 2,
        out_specs=vmem,
        out_shape=jax.ShapeDtypeStruct(mine.shape, mine.dtype),
        compiler_params=params(4),
        name="merge_pair",
    )(mine, other)


def merge_kernel(parts_ref, out_ref, scale_ref):
    sources, depth, lanes = parts_ref.shape
    heads = depth - PAD
    scales, _ = merge_step([parts_ref[k, heads:, :] for k in range(sources)])
    for k in range(sources):
        scale_ref[k] = scales[k]

    def body(k, so_far):
        return so_far + parts_ref[k, :heads, :] * spread_columns(scale_ref[k][0:1, :], heads)

    result = lax.fori_loop(
        0, sources, body, jnp.zeros((heads, lanes), jnp.float32), unroll=4
    ).astype(out_ref.dtype)
    for copy in range(out_ref.shape[0]):
        out_ref[copy] = result


def merge(parts):
    sources, depth, lanes = parts.shape
    vmem = pl.BlockSpec(memory_space=pltpu.VMEM)
    return pl.pallas_call(
        merge_kernel,
        in_specs=[vmem],
        out_specs=vmem,
        out_shape=jax.ShapeDtypeStruct((sources, depth - PAD, lanes), jnp.bfloat16),
        scratch_shapes=[pltpu.VMEM((sources, PAD, lanes), jnp.float32)],
        compiler_params=params(4),
        name="merge",
    )(parts)


def finish_kernel(mine_ref, other_ref, p0, p1, p2, p3, out_ref, cache_hbm, wide_ref, sems):
    group = lax.axis_index("pre")
    copies = []
    for k, (turn, piece) in enumerate(zip(TURNS, (p0, p1, p2, p3))):
        rows = piece.shape[1]
        at = pl.multiple_of((group ^ turn) * rows, rows)
        copies.append(
            pltpu.make_async_copy(piece, cache_hbm.at[:, pl.ds(at, rows)], sems.at[k])
        )
    for copy in copies:
        copy.start()
    half, heads, lanes = mine_ref.shape
    core = lax.axis_index("dec") & 1

    def widen(k, carry):
        for place_at, ref in ((core, mine_ref), (1 - core, other_ref)):
            item = place_at * half + half - 1 - k
            at = pl.ds(pl.multiple_of(item * heads, heads), heads)
            wide_ref[at, :] = ref[k].astype(jnp.float32)
        return carry

    lax.fori_loop(0, half, widen, 0, unroll=4)

    def body(h, carry):
        piece = wide_ref[pl.ds(h, 2 * half, stride=heads), :]
        at = pl.multiple_of(h * lanes, lanes)
        out_ref[:, pl.ds(at, lanes)] = piece.astype(out_ref.dtype)
        return carry

    lax.fori_loop(0, heads, body, 0, unroll=4)
    for copy in copies:
        copy.wait()


def finish(mine, other, pieces):
    half, heads, lanes = mine.shape
    width, rows = pieces[0].shape
    vmem = pl.BlockSpec(memory_space=pltpu.VMEM)
    return pl.pallas_call(
        finish_kernel,
        in_specs=[vmem] * 6,
        out_specs=[vmem, pl.BlockSpec(memory_space=pl.ANY)],
        out_shape=[
            jax.ShapeDtypeStruct((2 * half, heads * lanes), mine.dtype),
            jax.ShapeDtypeStruct((width, rows * len(pieces)), pieces[0].dtype),
        ],
        scratch_shapes=[
            pltpu.VMEM((2 * half * heads, lanes), jnp.float32),
            pltpu.SemaphoreType.DMA((len(pieces),)),
        ],
        compiler_params=params(6),
        name="finish",
    )(mine, other, *pieces)


def exchange(piece, groups, turn):
    return lax.ppermute(piece, "pre", [(i, i ^ turn) for i in range(groups)])


def around(piece, groups, owners):
    core = lax.axis_index("dec") % 2
    first = exchange(piece, groups, 3)
    second = exchange(piece, groups, 1)
    forward = [
        (g * owners + d, (g ^ (1 if d % 2 == 0 else 3)) * owners + d)
        for g in range(groups)
        for d in range(owners)
    ]
    chosen = jnp.where(core == 0, first, second)
    far = lax.ppermute(chosen, ("pre", "dec"), forward)
    return [piece, first, second, far], chosen


def per_device(
    hidden,
    w_down,
    kv_gain,
    query_latent,
    query_rope,
    w_up_value,
    request_rows,
    row_request,
    step_position,
    destination,
):
    groups = lax.axis_size("pre")
    owners = lax.axis_size("dec")
    steps, batch, heads, _ = query_latent.shape
    items = steps * batch
    plane = [[2 * k + core for k in reversed(range(SIDE * SIDE))] for core in range(2)]
    sibling = [(d, d ^ 1) for d in range(owners)]

    produced, packed = produce(
        groups, owners, request_rows, destination, hidden, w_down.T, kv_gain
    )
    chunks, chosen = around(produced, groups, owners)

    exchanged = functools.partial(
        lax.all_to_all, axis_name="dec", split_axis=0, concat_axis=0, tiled=True
    )
    lengths, _ = lax.optimization_barrier((request_rows, chosen))
    near_bias, far_bias, valid, chunks[0] = prepare(
        owners, groups, lengths, row_request, step_position, produced
    )
    keep, send = attend(
        near_bias,
        far_bias,
        valid,
        query_latent.reshape(items, heads, -1),
        query_rope.reshape(items, heads, -1),
        chunks,
        w_up_value,
    )
    arrived = exchanged(packed)
    quarter = place(arrived, *produced.shape)
    pieces = [quarter] + [exchange(quarter, groups, turn) for turn in TURNS[1:]]

    keep, _ = lax.optimization_barrier((keep, quarter))
    parts = merge_pair(keep, lax.ppermute(send, "dec", sibling))
    result = merge(exchanged(parts, axis_index_groups=plane))
    result = exchanged(result, axis_index_groups=plane)
    result, kv_cache = finish(result, lax.ppermute(result, "dec", sibling), pieces)
    attention_out = result.reshape(steps, batch, -1)
    kv_cache = kv_cache.T
    return (attention_out, kv_cache)


def solution(mesh):
    return jax.shard_map(
        per_device,
        mesh=mesh,
        in_specs=(
            P(("pre", "dec"), None),
            P(),
            P(),
            P(None, None, "pre", None),
            P(None, None, "pre", None),
            P("pre", None, None),
            P(),
            P(),
            P(),
            P(),
        ),
        out_specs=(P(None, None, "pre"), P("dec", None)),
        check_vma=False,
    )
```

```python
import functools
import math

import jax
import jax.numpy as jnp
import numpy as np
from jax import lax
from jax.experimental import pallas as pl
from jax.experimental.pallas import tpu as pltpu
from jax.sharding import PartitionSpec as P

LAT = 512
ROPE = 64
MOST = 2
PAD = 8
SIDE = 4
TURNS = (0, 3, 1, 2)
CUT_HEADS = 8
DEPTH = 1792

score_scale = 0.07216878364870323
mask_value = -1e30
norm_eps = 1e-06
log2_e = 1.4426950408889634


def frequencies():
    half = ROPE // 2
    pair_index = np.arange(half, dtype=np.float64)
    frequency = np.exp(pair_index * (-2.0 * math.log(10000.0) / ROPE)).astype(np.float32)
    return np.tile(frequency[:, None], (1, 128))


WIDE = 640


def shift_of(count):
    assert count & (count - 1) == 0
    return count.bit_length() - 1


def params(megabytes):
    return pltpu.CompilerParams(vmem_limit_bytes=megabytes * 1024 * 1024)


def produce_kernel(
    groups, owners, lengths_hbm, dest_hbm, hidden_hbm, w_hbm, gain_hbm, freq_hbm,
    out_ref, packed_ref, hidden_ref, w_ref, acc_ref, lengths_ref, dest_ref, gain_ref, freq_ref,
    turn_ref, column_ref, rows_ref, count_ref, slot_ref, sems, small_sems,
):
    pieces, rows, depth = hidden_ref.shape
    half = ROPE // 2
    small = [
        pltpu.make_async_copy(source, target, small_sems.at[k])
        for k, (source, target) in enumerate(
            (
                (lengths_hbm, lengths_ref),
                (dest_hbm, dest_ref),
                (gain_hbm, gain_ref),
                (freq_hbm, freq_ref),
            )
        )
    ]

    def copies(k):
        columns = pl.ds(pl.multiple_of(k * depth, depth), depth)
        return (
            pltpu.make_async_copy(hidden_hbm.at[:, columns], hidden_ref.at[k], sems.at[0, k]),
            pltpu.make_async_copy(w_hbm.at[:, columns], w_ref.at[k], sems.at[1, k]),
        )

    def begin(k, carry):
        for copy in copies(k):
            copy.start()
        return carry

    for copy in small:
        copy.start()
    lax.fori_loop(0, pieces, begin, 0)
    acc_ref[...] = jnp.zeros_like(acc_ref)
    packed_ref[...] = jnp.full(packed_ref.shape, -1.0, packed_ref.dtype)
    for copy in small:
        copy.wait()
    group = lax.axis_index("pre")
    device = group * owners + lax.axis_index("dec")
    block_rows = packed_ref.shape[1]
    blocks = rows // block_rows

    def clear(owner, carry):
        count_ref[owner] = 0
        return carry

    def choose(b, carry):
        owner = lax.shift_right_logical(dest_ref[device * blocks + b], shift_of(groups * owners))
        rank = count_ref[owner]
        count_ref[owner] = rank + 1
        slot_ref[b] = owner * MOST + rank
        return carry

    lax.fori_loop(0, owners, clear, 0)
    lax.fori_loop(0, blocks, choose, 0)
    row = device * rows + lax.broadcasted_iota(jnp.int32, (1, rows), 1)
    start = jnp.zeros((1, rows), jnp.int32)
    first_row = jnp.int32(0)
    for r in range(lengths_ref.shape[0] - 1):
        first_row = first_row + lengths_ref[r]
        start = jnp.where(row >= first_row, first_row, start)
    angles = freq_ref[:, 0:1] * (row - start).astype(jnp.float32)
    turn_ref[:half, :] = jnp.cos(angles)
    turn_ref[half:, :] = jnp.sin(angles)
    column_ref[...] = jnp.transpose(jnp.broadcast_to(gain_ref[...], (128, LAT)))

    def body(k, carry):
        for copy in copies(k):
            copy.wait()
        acc_ref[...] += lax.dot_general(
            w_ref[k],
            hidden_ref[k],
            (((1,), (1,)), ((), ())),
            preferred_element_type=jnp.float32,
        )
        return carry

    lax.fori_loop(0, pieces, body, 0)
    latent = acc_ref[:LAT, :]
    inverse_rms = lax.rsqrt(jnp.mean(latent * latent, axis=0, keepdims=True) + norm_eps)
    out_ref[:LAT, :] = (latent * inverse_rms * column_ref[:, 0:1]).astype(out_ref.dtype)
    cosine, sine = turn_ref[:half, :], turn_ref[half:, :]
    first = acc_ref[LAT : LAT + half, :]
    second = acc_ref[LAT + half :, :]
    turned = first * cosine - second * sine
    out_ref[LAT : LAT + half, :] = turned.astype(out_ref.dtype)
    turned = second * cosine + first * sine
    out_ref[LAT + half :, :] = turned.astype(out_ref.dtype)
    width = out_ref.shape[0]
    for at in range(0, width, 128):
        count = min(128, width - at)
        wide = out_ref[at : at + count, :].astype(jnp.float32)
        if count < 128:
            wide = jnp.concatenate([wide, jnp.zeros((128 - count, rows), jnp.float32)], axis=0)
        rows_ref[:, :, at : at + 128] = jnp.transpose(wide).reshape(blocks, block_rows, 128)
    lane = lax.broadcasted_iota(jnp.int32, (block_rows, WIDE), 1)

    def put(b, carry):
        place_at = (dest_ref[device * blocks + b] & (groups * owners - 1)) - group * owners
        block = jnp.where(lane < width, rows_ref[b], place_at.astype(jnp.float32))
        packed_ref[slot_ref[b]] = block.astype(packed_ref.dtype)
        return carry

    lax.fori_loop(0, blocks, put, 0, unroll=4)


def produce(groups, owners, lengths, destination, hidden, w_turned, gain):
    rows, width = hidden.shape
    row_width = w_turned.shape[0]
    pieces = width // DEPTH
    block_rows = rows // owners
    vmem = pl.BlockSpec(memory_space=pltpu.VMEM)
    return pl.pallas_call(
        functools.partial(produce_kernel, groups, owners),
        in_specs=[pl.BlockSpec(memory_space=pltpu.HBM)] * 6,
        out_specs=[vmem, vmem],
        out_shape=[
            jax.ShapeDtypeStruct((row_width, rows), jnp.bfloat16),
            jax.ShapeDtypeStruct((owners * MOST, block_rows, WIDE), jnp.bfloat16),
        ],
        scratch_shapes=[
            pltpu.VMEM((pieces, rows, DEPTH), jnp.bfloat16),
            pltpu.VMEM((pieces, row_width, DEPTH), jnp.bfloat16),
            pltpu.VMEM((row_width, rows), jnp.float32),
            pltpu.SMEM(lengths.shape, jnp.int32),
            pltpu.SMEM(destination.shape, jnp.int32),
            pltpu.VMEM((1, LAT), jnp.float32),
            pltpu.VMEM((ROPE // 2, 128), jnp.float32),
            pltpu.VMEM((ROPE, rows), jnp.float32),
            pltpu.VMEM((LAT, 128), jnp.float32),
            pltpu.VMEM((owners, block_rows, WIDE), jnp.float32),
            pltpu.SMEM((owners,), jnp.int32),
            pltpu.SMEM((owners,), jnp.int32),
            pltpu.SemaphoreType.DMA((2, pieces)),
            pltpu.SemaphoreType.DMA((4,)),
        ],
        name="produce",
    )(
        lengths,
        destination,
        hidden,
        w_turned,
        gain.reshape(1, -1),
        jnp.asarray(frequencies()),
    )


def place_kernel(arrived_ref, out_ref, rows_ref):
    blocks, block_rows, _ = arrived_ref.shape
    width, rows = out_ref.shape
    part = 128 // block_rows
    row = lax.broadcasted_iota(jnp.int32, (rows, 128), 0).astype(jnp.float32)
    lane = lax.broadcasted_iota(jnp.int32, (1, 128), 1)
    within = lax.rem(lane, block_rows).astype(jnp.float32)
    rows_ref[...] = jnp.zeros_like(rows_ref)

    def body(k, carry):
        source = arrived_ref[pl.ds(k * part, part)].astype(jnp.float32).reshape(128, WIDE)
        slot = jnp.transpose(source[:, WIDE - 128 :])[127:128, :]
        select = jnp.where(row == slot * block_rows + within, 1.0, 0.0).astype(jnp.bfloat16)
        rows_ref[...] += jnp.dot(
            select, source.astype(jnp.bfloat16), preferred_element_type=jnp.float32
        )
        return carry

    lax.fori_loop(0, blocks // part, body, 0)
    for at in range(0, width, 128):
        count = min(128, width - at)
        turned = jnp.transpose(rows_ref[:, at : at + 128])
        out_ref[at : at + count, :] = turned[:count].astype(out_ref.dtype)


def place(arrived, width, rows):
    vmem = pl.BlockSpec(memory_space=pltpu.VMEM)
    return pl.pallas_call(
        place_kernel,
        in_specs=[vmem],
        out_specs=vmem,
        out_shape=jax.ShapeDtypeStruct((width, rows), arrived.dtype),
        scratch_shapes=[pltpu.VMEM((rows, WIDE), jnp.float32)],
        compiler_params=params(8),
        name="place",
    )(arrived)


def prepare_kernel(
    owners, lengths_ref, request_ref, position_ref, own_hbm,
    near_ref, far_ref, valid_ref, own_ref, sem,
):
    copy = pltpu.make_async_copy(own_hbm, own_ref, sem)
    copy.start()
    steps, batch = position_ref.shape
    heads = CUT_HEADS
    count = own_ref.shape[1]
    group, owner = lax.axis_index("pre"), lax.axis_index("dec")
    row = lax.broadcasted_iota(jnp.int32, (heads, count), 1)
    bases = [((group ^ turn) * owners + owner) * count for turn in TURNS]

    def fill(b, carry):
        request = request_ref[b]
        start = jnp.int32(0)
        for r in range(lengths_ref.shape[0] - 1):
            start = start + jnp.where(request > r, lengths_ref[r], 0)
        for s in range(steps):
            stop = start + position_ref[s, b]
            at = pl.ds(pl.multiple_of((s * batch + b) * heads, heads), heads)
            seen = jnp.int32(0)
            for c, base in enumerate(bases):
                bias = jnp.where((row >= start - base) & (row < stop - base), 0.0, mask_value)
                if c < len(bases) - 1:
                    near_ref[at, c * count : (c + 1) * count] = bias
                else:
                    far_ref[at, :] = bias
                seen = seen + jnp.where((start < base + count) & (stop > base), 1, 0)
            valid_ref[at, :] = jnp.full((heads, 128), seen, jnp.int32)
        return carry

    lax.fori_loop(0, batch, fill, 0)
    copy.wait()


def prepare(owners, groups, lengths, row_request, step_position, own):
    rows = step_position.size * CUT_HEADS
    smem = pl.BlockSpec(memory_space=pltpu.SMEM)
    vmem = pl.BlockSpec(memory_space=pltpu.VMEM)
    return pl.pallas_call(
        functools.partial(prepare_kernel, owners),
        in_specs=[smem] * 3 + [pl.BlockSpec(memory_space=pl.ANY)],
        out_specs=[vmem] * 4,
        out_shape=[
            jax.ShapeDtypeStruct((rows, (groups - 1) * own.shape[1]), jnp.float32),
            jax.ShapeDtypeStruct((rows, own.shape[1]), jnp.float32),
            jax.ShapeDtypeStruct((rows, 128), jnp.int32),
            jax.ShapeDtypeStruct(own.shape, own.dtype),
        ],
        scratch_shapes=[pltpu.SemaphoreType.DMA(())],
        compiler_params=params(8),
        name="prepare",
    )(lengths, row_request, step_position, own)


def scores_of(latent_ref, rope_ref, cut, chunk_refs, bias_ref):
    items, _, heads, _ = latent_ref.shape
    rows = items * heads
    latent = latent_ref[:, cut].reshape(rows, LAT)
    rope = rope_ref[:, cut].reshape(rows, ROPE)
    scores = []
    for c, chunk_ref in enumerate(chunk_refs):
        count = chunk_ref.shape[1]
        s = jnp.dot(latent, chunk_ref[:LAT, :], preferred_element_type=jnp.float32)
        s += jnp.dot(rope, chunk_ref[LAT:, :], preferred_element_type=jnp.float32)
        scores.append(s + bias_ref[:, c * count : (c + 1) * count])
    return scores


def weigh(scores, peak, chunk_refs):
    weights = [jnp.exp2((s - peak) * (score_scale * log2_e)) for s in scores]
    total = jnp.sum(functools.reduce(jnp.add, weights), axis=1, keepdims=True)
    mixed = sum(
        lax.dot_general(
            p.astype(jnp.bfloat16),
            chunk_ref[:LAT, :],
            (((1,), (1,)), ((), ())),
            preferred_element_type=jnp.float32,
        )
        for p, chunk_ref in zip(weights, chunk_refs)
    )
    return total, mixed


def near_kernel(bias_ref, latent_ref, rope_ref, k0, k1, k2, mixed_ref, stat_ref):
    chunk_refs = (k0, k1, k2)
    cuts, rows, _ = mixed_ref.shape
    lane = lax.broadcasted_iota(jnp.int32, (rows, 128), 1)

    def body(cut, carry):
        scores = scores_of(latent_ref, rope_ref, cut, chunk_refs, bias_ref)
        peak = jnp.max(functools.reduce(jnp.maximum, scores), axis=1, keepdims=True)
        total, mixed = weigh(scores, peak, chunk_refs)
        mixed_ref[cut] = mixed
        stat_ref[cut] = jnp.where(lane == 0, peak, total)
        return carry

    lax.fori_loop(0, cuts, body, 0, unroll=2)


def apart(value):
    rows, width = value.shape
    tiles = value.reshape(rows // 16, 2, 8, width)
    first, second = tiles[:, 0], tiles[:, 1]
    upper_part = lax.broadcasted_iota(jnp.int32, first.shape, 1) < 4
    low = jnp.where(upper_part, first, pltpu.roll(second, 4, 1))
    high = jnp.where(upper_part, pltpu.roll(first, 4, 1), second)
    return low.reshape(rows // 2, width), high.reshape(rows // 2, width)


def together(low, high):
    rows, width = low.shape
    low = low.reshape(rows // 8, 8, width)
    high = high.reshape(rows // 8, 8, width)
    upper_part = lax.broadcasted_iota(jnp.int32, low.shape, 1) < 4
    first = jnp.where(upper_part, low, pltpu.roll(high, 4, 1))
    second = jnp.where(upper_part, pltpu.roll(low, 4, 1), high)
    return jnp.stack([first, second], axis=1).reshape(2 * rows, width)


def far_kernel(
    bias_ref, valid_ref, latent_ref, rope_ref, k3, mixed_ref, stat_ref, w_hbm,
    keep_ref, send_ref, out_ref, w_ref, sems,
):
    items, cuts, heads, _ = latent_ref.shape
    rows = items * heads
    all_heads = cuts * heads

    def weights_of(cut):
        part = pl.ds(cut * heads, heads)
        return pltpu.make_async_copy(w_hbm.at[part], w_ref.at[part], sems.at[cut])

    for cut in range(cuts):
        weights_of(cut).start()
    out_ref[:, all_heads:, :] = jnp.zeros((items, PAD, 128), jnp.float32)
    head = lax.broadcasted_iota(jnp.int32, (rows, 128), 0) % heads
    lane = lax.broadcasted_iota(jnp.int32, (rows, 128), 1)
    half_heads = heads // 2
    head_of_half = lax.broadcasted_iota(jnp.int32, (rows // 2, 128), 0) % half_heads

    def body(cut, carry):
        scores = scores_of(latent_ref, rope_ref, cut, (k3,), bias_ref)
        old_peak, old_total = stat_ref[cut, :, 0:1], stat_ref[cut, :, 1:2]
        peak = jnp.maximum(old_peak, jnp.max(scores[0], axis=1, keepdims=True))
        factor = jnp.exp2((old_peak - peak) * (score_scale * log2_e))
        total, mixed = weigh(scores, peak, (k3,))
        total += old_total * factor
        valid = valid_ref[:, 0:1] > 0
        inverse = jnp.where(valid, 1.0 / total, 0.0)
        mixed = mixed * inverse + mixed_ref[cut] * (factor * inverse)
        level = jnp.where(valid, peak * score_scale + jnp.log(total), mask_value)
        low, high = apart(mixed)
        weights_of(cut).wait()
        pieces = []
        for first, part in ((0, low), (half_heads, high)):
            upper = part.astype(jnp.bfloat16)
            lower = (part - upper.astype(jnp.float32)).astype(jnp.bfloat16)
            both = jnp.concatenate([upper, lower], axis=0)
            piece = jnp.zeros((rows // 2, 128), jnp.float32)
            for h in range(0, half_heads, 2):
                at = cut * heads + first + h
                pair = jnp.concatenate([w_ref[at], w_ref[at + 1]], axis=1)
                y = jnp.dot(both, pair, preferred_element_type=jnp.float32)
                y = y[: rows // 2] + y[rows // 2 :]
                piece = jnp.where(head_of_half == h, y[:, :128], piece)
                piece = jnp.where(head_of_half == h + 1, y[:, 128:], piece)
            pieces.append(piece)
        result = together(*pieces)
        at = pl.multiple_of(cut * heads, heads)
        out_ref[:, pl.ds(at, heads), :] = result.reshape(items, heads, 128)
        lines = jnp.where(lane == head + at, level, 0.0).reshape(items, heads, 128)
        lines = jnp.sum(lines, axis=1, keepdims=True)
        out_ref[:, all_heads:, :] += jnp.broadcast_to(lines, (items, PAD, 128))
        return carry

    lax.fori_loop(0, cuts, body, 0, unroll=2)
    half = items // 2
    core = lax.axis_index("dec") & 1

    def hand(i, carry):
        keep_ref[i] = out_ref[core * half + half - 1 - i]
        send_ref[i] = out_ref[(1 - core) * half + half - 1 - i]
        return carry

    lax.fori_loop(0, half, hand, 0)


def attend(near_bias, far_bias, valid, latent, rope, chunks, w_up):
    items, heads, _ = latent.shape
    cuts = heads // CUT_HEADS
    rows = items * CUT_HEADS
    latent = latent.reshape(items, cuts, CUT_HEADS, -1)
    rope = rope.reshape(items, cuts, CUT_HEADS, -1)
    vmem = pl.BlockSpec(memory_space=pltpu.VMEM)
    mixed, stat = pl.pallas_call(
        near_kernel,
        in_specs=[vmem] * 6,
        out_specs=[vmem] * 2,
        out_shape=[
            jax.ShapeDtypeStruct((cuts, rows, LAT), jnp.float32),
            jax.ShapeDtypeStruct((cuts, rows, 128), jnp.float32),
        ],
        compiler_params=params(20),
        name="attend_near",
    )(near_bias, latent, rope, *chunks[:3])
    out_shape = jax.ShapeDtypeStruct((items // 2, heads + PAD, 128), jnp.float32)
    return pl.pallas_call(
        far_kernel,
        in_specs=[vmem] * 7 + [pl.BlockSpec(memory_space=pl.ANY)],
        out_specs=[vmem] * 2,
        out_shape=[out_shape] * 2,
        scratch_shapes=[
            pltpu.VMEM((items, heads + PAD, 128), jnp.float32),
            pltpu.VMEM(w_up.shape, w_up.dtype),
            pltpu.SemaphoreType.DMA((cuts,)),
        ],
        compiler_params=params(47),
        name="attend_far",
    )(far_bias, valid, latent, rope, chunks[3], mixed, stat, w_up)


def merge_step(levels):
    peak = functools.reduce(jnp.maximum, levels)
    scales = [jnp.exp(level - peak) for level in levels]
    total = functools.reduce(jnp.add, scales)
    return [scale / total for scale in scales], peak + jnp.log(total)


def spread_columns(line, heads):
    shape = line.shape[:-2] + (heads, line.shape[-1])
    axis = len(shape) - 1
    lane = lax.broadcasted_iota(jnp.int32, shape, axis)
    row = lax.broadcasted_iota(jnp.int32, shape, axis - 1)
    return jnp.sum(jnp.where(lane == row, line, 0.0), axis=axis, keepdims=True)


def pair_kernel(mine_ref, other_ref, out_ref):
    items, depth, _ = mine_ref.shape
    heads = depth - PAD
    step = 4

    def body(k, carry):
        at = pl.ds(k * step, step)
        parts = [mine_ref[at], other_ref[at]]
        scales, level = merge_step([part[:, heads:, :] for part in parts])
        result = sum(
            part[:, :heads, :] * spread_columns(scale[:, 0:1, :], heads)
            for part, scale in zip(parts, scales)
        )
        out_ref[at, :heads, :] = result
        out_ref[at, heads:, :] = level
        return carry

    lax.fori_loop(0, items // step, body, 0)


def merge_pair(mine, other):
    vmem = pl.BlockSpec(memory_space=pltpu.VMEM)
    return pl.pallas_call(
        pair_kernel,
        in_specs=[vmem] * 2,
        out_specs=vmem,
        out_shape=jax.ShapeDtypeStruct(mine.shape, mine.dtype),
        compiler_params=params(4),
        name="merge_pair",
    )(mine, other)


def merge_kernel(parts_ref, out_ref, scale_ref):
    sources, depth, lanes = parts_ref.shape
    heads = depth - PAD
    scales, _ = merge_step([parts_ref[k, heads:, :] for k in range(sources)])
    for k in range(sources):
        scale_ref[k] = scales[k]

    def body(k, so_far):
        return so_far + parts_ref[k, :heads, :] * spread_columns(scale_ref[k][0:1, :], heads)

    result = lax.fori_loop(
        0, sources, body, jnp.zeros((heads, lanes), jnp.float32), unroll=4
    ).astype(out_ref.dtype)
    for copy in range(out_ref.shape[0]):
        out_ref[copy] = result


def merge(parts):
    sources, depth, lanes = parts.shape
    vmem = pl.BlockSpec(memory_space=pltpu.VMEM)
    return pl.pallas_call(
        merge_kernel,
        in_specs=[vmem],
        out_specs=vmem,
        out_shape=jax.ShapeDtypeStruct((sources, depth - PAD, lanes), jnp.bfloat16),
        scratch_shapes=[pltpu.VMEM((sources, PAD, lanes), jnp.float32)],
        compiler_params=params(4),
        name="merge",
    )(parts)


def finish_kernel(mine_ref, other_ref, p0, p1, p2, p3, out_ref, cache_hbm, wide_ref, sems):
    group = lax.axis_index("pre")
    copies = []
    for k, (turn, piece) in enumerate(zip(TURNS, (p0, p1, p2, p3))):
        rows = piece.shape[1]
        at = pl.multiple_of((group ^ turn) * rows, rows)
        copies.append(
            pltpu.make_async_copy(piece, cache_hbm.at[:, pl.ds(at, rows)], sems.at[k])
        )
    for copy in copies:
        copy.start()
    half, heads, lanes = mine_ref.shape
    core = lax.axis_index("dec") & 1

    def widen(k, carry):
        for place_at, ref in ((core, mine_ref), (1 - core, other_ref)):
            item = place_at * half + half - 1 - k
            at = pl.ds(pl.multiple_of(item * heads, heads), heads)
            wide_ref[at, :] = ref[k].astype(jnp.float32)
        return carry

    lax.fori_loop(0, half, widen, 0, unroll=4)

    def body(h, carry):
        piece = wide_ref[pl.ds(h, 2 * half, stride=heads), :]
        at = pl.multiple_of(h * lanes, lanes)
        out_ref[:, pl.ds(at, lanes)] = piece.astype(out_ref.dtype)
        return carry

    lax.fori_loop(0, heads, body, 0, unroll=4)
    for copy in copies:
        copy.wait()


def finish(mine, other, pieces):
    half, heads, lanes = mine.shape
    width, rows = pieces[0].shape
    vmem = pl.BlockSpec(memory_space=pltpu.VMEM)
    return pl.pallas_call(
        finish_kernel,
        in_specs=[vmem] * 6,
        out_specs=[vmem, pl.BlockSpec(memory_space=pl.ANY)],
        out_shape=[
            jax.ShapeDtypeStruct((2 * half, heads * lanes), mine.dtype),
            jax.ShapeDtypeStruct((width, rows * len(pieces)), pieces[0].dtype),
        ],
        scratch_shapes=[
            pltpu.VMEM((2 * half * heads, lanes), jnp.float32),
            pltpu.SemaphoreType.DMA((len(pieces),)),
        ],
        compiler_params=params(6),
        name="finish",
    )(mine, other, *pieces)


def exchange(piece, groups, turn):
    return lax.ppermute(piece, "pre", [(i, i ^ turn) for i in range(groups)])


def around(piece, groups, owners):
    core = lax.axis_index("dec") % 2
    first = exchange(piece, groups, 3)
    second = exchange(piece, groups, 1)
    forward = [
        (g * owners + d, (g ^ (1 if d % 2 == 0 else 3)) * owners + d)
        for g in range(groups)
        for d in range(owners)
    ]
    chosen = jnp.where(core == 0, first, second)
    far = lax.ppermute(chosen, ("pre", "dec"), forward)
    return [piece, first, second, far], chosen


def per_device(
    hidden,
    w_down,
    kv_gain,
    query_latent,
    query_rope,
    w_up_value,
    request_rows,
    row_request,
    step_position,
    destination,
):
    groups = lax.axis_size("pre")
    owners = lax.axis_size("dec")
    steps, batch, heads, _ = query_latent.shape
    items = steps * batch
    plane = [[2 * k + core for k in reversed(range(SIDE * SIDE))] for core in range(2)]
    sibling = [(d, d ^ 1) for d in range(owners)]

    produced, packed = produce(
        groups, owners, request_rows, destination, hidden, w_down.T, kv_gain
    )
    chunks, chosen = around(produced, groups, owners)

    exchanged = functools.partial(
        lax.all_to_all, axis_name="dec", split_axis=0, concat_axis=0, tiled=True
    )
    lengths, _ = lax.optimization_barrier((request_rows, chosen))
    near_bias, far_bias, valid, chunks[0] = prepare(
        owners, groups, lengths, row_request, step_position, produced
    )
    keep, send = attend(
        near_bias,
        far_bias,
        valid,
        query_latent.reshape(items, heads, -1),
        query_rope.reshape(items, heads, -1),
        chunks,
        w_up_value,
    )
    arrived = exchanged(packed)
    quarter = place(arrived, *produced.shape)
    pieces = [quarter] + [exchange(quarter, groups, turn) for turn in TURNS[1:]]

    keep, _ = lax.optimization_barrier((keep, quarter))
    parts = merge_pair(keep, lax.ppermute(send, "dec", sibling))
    result = merge(exchanged(parts, axis_index_groups=plane))
    result = exchanged(result, axis_index_groups=plane)
    result, kv_cache = finish(result, lax.ppermute(result, "dec", sibling), pieces)
    attention_out = result.reshape(steps, batch, -1)
    kv_cache = kv_cache.T
    return (attention_out, kv_cache)


def solution(mesh):
    return jax.shard_map(
        per_device,
        mesh=mesh,
        in_specs=(
            P(("pre", "dec"), None),
            P(),
            P(),
            P(None, None, "pre", None),
            P(None, None, "pre", None),
            P("pre", None, None),
            P(),
            P(),
            P(),
            P(),
        ),
        out_specs=(P(None, None, "pre"), P("dec", None)),
        check_vma=False,
    )
```

```python
import functools
import math

import jax
import jax.numpy as jnp
import numpy as np
from jax import lax
from jax.experimental import pallas as pl
from jax.experimental.pallas import tpu as pltpu
from jax.sharding import PartitionSpec as P

LAT = 512
ROPE = 64
MOST = 2
PAD = 8
SIDE = 4
TURNS = (0, 3, 1, 2)
CUT_HEADS = 8
DEPTH = 1792

score_scale = 0.07216878364870323
mask_value = -1e30
norm_eps = 1e-06
log2_e = 1.4426950408889634


def frequencies():
    half = ROPE // 2
    pair_index = np.arange(half, dtype=np.float64)
    frequency = np.exp(pair_index * (-2.0 * math.log(10000.0) / ROPE)).astype(np.float32)
    return np.tile(frequency[:, None], (1, 128))


WIDE = 640


def shift_of(count):
    assert count & (count - 1) == 0
    return count.bit_length() - 1


def params(megabytes):
    return pltpu.CompilerParams(vmem_limit_bytes=megabytes * 1024 * 1024)


def produce_kernel(
    groups, owners, lengths_hbm, dest_hbm, hidden_hbm, w_hbm, gain_hbm, freq_hbm,
    out_ref, packed_ref, hidden_ref, w_ref, acc_ref, lengths_ref, dest_ref, gain_ref, freq_ref,
    turn_ref, column_ref, rows_ref, count_ref, slot_ref, sems, small_sems,
):
    pieces, rows, depth = hidden_ref.shape
    half = ROPE // 2
    small = [
        pltpu.make_async_copy(source, target, small_sems.at[k])
        for k, (source, target) in enumerate(
            (
                (lengths_hbm, lengths_ref),
                (dest_hbm, dest_ref),
                (gain_hbm, gain_ref),
                (freq_hbm, freq_ref),
            )
        )
    ]

    def copies(k):
        columns = pl.ds(pl.multiple_of(k * depth, depth), depth)
        return (
            pltpu.make_async_copy(hidden_hbm.at[:, columns], hidden_ref.at[k], sems.at[0, k]),
            pltpu.make_async_copy(w_hbm.at[:, columns], w_ref.at[k], sems.at[1, k]),
        )

    def begin(k, carry):
        for copy in copies(k):
            copy.start()
        return carry

    for copy in small:
        copy.start()
    lax.fori_loop(0, pieces, begin, 0)
    acc_ref[...] = jnp.zeros_like(acc_ref)
    packed_ref[...] = jnp.full(packed_ref.shape, -1.0, packed_ref.dtype)
    for copy in small:
        copy.wait()
    group = lax.axis_index("pre")
    device = group * owners + lax.axis_index("dec")
    block_rows = packed_ref.shape[1]
    blocks = rows // block_rows

    def clear(owner, carry):
        count_ref[owner] = 0
        return carry

    def choose(b, carry):
        owner = lax.shift_right_logical(dest_ref[device * blocks + b], shift_of(groups * owners))
        rank = count_ref[owner]
        count_ref[owner] = rank + 1
        slot_ref[b] = owner * MOST + rank
        return carry

    lax.fori_loop(0, owners, clear, 0)
    lax.fori_loop(0, blocks, choose, 0)
    row = device * rows + lax.broadcasted_iota(jnp.int32, (1, rows), 1)
    start = jnp.zeros((1, rows), jnp.int32)
    first_row = jnp.int32(0)
    for r in range(lengths_ref.shape[0] - 1):
        first_row = first_row + lengths_ref[r]
        start = jnp.where(row >= first_row, first_row, start)
    angles = freq_ref[:, 0:1] * (row - start).astype(jnp.float32)
    turn_ref[:half, :] = jnp.cos(angles)
    turn_ref[half:, :] = jnp.sin(angles)
    column_ref[...] = jnp.transpose(jnp.broadcast_to(gain_ref[...], (128, LAT)))

    def body(k, carry):
        for copy in copies(k):
            copy.wait()
        acc_ref[...] += lax.dot_general(
            w_ref[k],
            hidden_ref[k],
            (((1,), (1,)), ((), ())),
            preferred_element_type=jnp.float32,
        )
        return carry

    lax.fori_loop(0, pieces, body, 0)
    latent = acc_ref[:LAT, :]
    inverse_rms = lax.rsqrt(jnp.mean(latent * latent, axis=0, keepdims=True) + norm_eps)
    out_ref[:LAT, :] = (latent * inverse_rms * column_ref[:, 0:1]).astype(out_ref.dtype)
    cosine, sine = turn_ref[:half, :], turn_ref[half:, :]
    first = acc_ref[LAT : LAT + half, :]
    second = acc_ref[LAT + half :, :]
    turned = first * cosine - second * sine
    out_ref[LAT : LAT + half, :] = turned.astype(out_ref.dtype)
    turned = second * cosine + first * sine
    out_ref[LAT + half :, :] = turned.astype(out_ref.dtype)
    width = out_ref.shape[0]
    for at in range(0, width, 128):
        count = min(128, width - at)
        wide = out_ref[at : at + count, :].astype(jnp.float32)
        if count < 128:
            wide = jnp.concatenate([wide, jnp.zeros((128 - count, rows), jnp.float32)], axis=0)
        rows_ref[:, :, at : at + 128] = jnp.transpose(wide).reshape(blocks, block_rows, 128)
    lane = lax.broadcasted_iota(jnp.int32, (block_rows, WIDE), 1)

    def put(b, carry):
        place_at = (dest_ref[device * blocks + b] & (groups * owners - 1)) - group * owners
        block = jnp.where(lane < width, rows_ref[b], place_at.astype(jnp.float32))
        packed_ref[slot_ref[b]] = block.astype(packed_ref.dtype)
        return carry

    lax.fori_loop(0, blocks, put, 0, unroll=4)


def produce(groups, owners, lengths, destination, hidden, w_turned, gain):
    rows, width = hidden.shape
    row_width = w_turned.shape[0]
    pieces = width // DEPTH
    block_rows = rows // owners
    vmem = pl.BlockSpec(memory_space=pltpu.VMEM)
    return pl.pallas_call(
        functools.partial(produce_kernel, groups, owners),
        in_specs=[pl.BlockSpec(memory_space=pltpu.HBM)] * 6,
        out_specs=[vmem, vmem],
        out_shape=[
            jax.ShapeDtypeStruct((row_width, rows), jnp.bfloat16),
            jax.ShapeDtypeStruct((owners * MOST, block_rows, WIDE), jnp.bfloat16),
        ],
        scratch_shapes=[
            pltpu.VMEM((pieces, rows, DEPTH), jnp.bfloat16),
            pltpu.VMEM((pieces, row_width, DEPTH), jnp.bfloat16),
            pltpu.VMEM((row_width, rows), jnp.float32),
            pltpu.SMEM(lengths.shape, jnp.int32),
            pltpu.SMEM(destination.shape, jnp.int32),
            pltpu.VMEM((1, LAT), jnp.float32),
            pltpu.VMEM((ROPE // 2, 128), jnp.float32),
            pltpu.VMEM((ROPE, rows), jnp.float32),
            pltpu.VMEM((LAT, 128), jnp.float32),
            pltpu.VMEM((owners, block_rows, WIDE), jnp.float32),
            pltpu.SMEM((owners,), jnp.int32),
            pltpu.SMEM((owners,), jnp.int32),
            pltpu.SemaphoreType.DMA((2, pieces)),
            pltpu.SemaphoreType.DMA((4,)),
        ],
        name="produce",
    )(
        lengths,
        destination,
        hidden,
        w_turned,
        gain.reshape(1, -1),
        jnp.asarray(frequencies()),
    )


def place_kernel(arrived_ref, out_ref, rows_ref):
    blocks, block_rows, _ = arrived_ref.shape
    width, rows = out_ref.shape
    part = 128 // block_rows
    row = lax.broadcasted_iota(jnp.int32, (rows, 128), 0).astype(jnp.float32)
    lane = lax.broadcasted_iota(jnp.int32, (1, 128), 1)
    within = lax.rem(lane, block_rows).astype(jnp.float32)
    rows_ref[...] = jnp.zeros_like(rows_ref)

    def body(k, carry):
        source = arrived_ref[pl.ds(k * part, part)].astype(jnp.float32).reshape(128, WIDE)
        slot = jnp.transpose(source[:, WIDE - 128 :])[127:128, :]
        select = jnp.where(row == slot * block_rows + within, 1.0, 0.0).astype(jnp.bfloat16)
        rows_ref[...] += jnp.dot(
            select, source.astype(jnp.bfloat16), preferred_element_type=jnp.float32
        )
        return carry

    lax.fori_loop(0, blocks // part, body, 0)
    for at in range(0, width, 128):
        count = min(128, width - at)
        turned = jnp.transpose(rows_ref[:, at : at + 128])
        out_ref[at : at + count, :] = turned[:count].astype(out_ref.dtype)


def place(arrived, width, rows):
    vmem = pl.BlockSpec(memory_space=pltpu.VMEM)
    return pl.pallas_call(
        place_kernel,
        in_specs=[vmem],
        out_specs=vmem,
        out_shape=jax.ShapeDtypeStruct((width, rows), arrived.dtype),
        scratch_shapes=[pltpu.VMEM((rows, WIDE), jnp.float32)],
        compiler_params=params(8),
        name="place",
    )(arrived)


def prepare_kernel(
    owners, lengths_ref, request_ref, position_ref, own_hbm,
    near_ref, far_ref, valid_ref, own_ref, sem,
):
    copy = pltpu.make_async_copy(own_hbm, own_ref, sem)
    copy.start()
    steps, batch = position_ref.shape
    heads = CUT_HEADS
    count = own_ref.shape[1]
    group, owner = lax.axis_index("pre"), lax.axis_index("dec")
    row = lax.broadcasted_iota(jnp.int32, (heads, count), 1)
    bases = [((group ^ turn) * owners + owner) * count for turn in TURNS]

    def fill(b, carry):
        request = request_ref[b]
        start = jnp.int32(0)
        for r in range(lengths_ref.shape[0] - 1):
            start = start + jnp.where(request > r, lengths_ref[r], 0)
        for s in range(steps):
            stop = start + position_ref[s, b]
            at = pl.ds(pl.multiple_of((s * batch + b) * heads, heads), heads)
            seen = jnp.int32(0)
            for c, base in enumerate(bases):
                bias = jnp.where((row >= start - base) & (row < stop - base), 0.0, mask_value)
                if c < len(bases) - 1:
                    near_ref[at, c * count : (c + 1) * count] = bias
                else:
                    far_ref[at, :] = bias
                seen = seen + jnp.where((start < base + count) & (stop > base), 1, 0)
            valid_ref[at, :] = jnp.full((heads, 128), seen, jnp.int32)
        return carry

    lax.fori_loop(0, batch, fill, 0)
    copy.wait()


def prepare(owners, groups, lengths, row_request, step_position, own):
    rows = step_position.size * CUT_HEADS
    smem = pl.BlockSpec(memory_space=pltpu.SMEM)
    vmem = pl.BlockSpec(memory_space=pltpu.VMEM)
    return pl.pallas_call(
        functools.partial(prepare_kernel, owners),
        in_specs=[smem] * 3 + [pl.BlockSpec(memory_space=pl.ANY)],
        out_specs=[vmem] * 4,
        out_shape=[
            jax.ShapeDtypeStruct((rows, (groups - 1) * own.shape[1]), jnp.float32),
            jax.ShapeDtypeStruct((rows, own.shape[1]), jnp.float32),
            jax.ShapeDtypeStruct((rows, 128), jnp.int32),
            jax.ShapeDtypeStruct(own.shape, own.dtype),
        ],
        scratch_shapes=[pltpu.SemaphoreType.DMA(())],
        compiler_params=params(8),
        name="prepare",
    )(lengths, row_request, step_position, own)


def scores_of(latent_ref, rope_ref, cut, chunk_refs, bias_ref):
    items, _, heads, _ = latent_ref.shape
    rows = items * heads
    latent = latent_ref[:, cut].reshape(rows, LAT)
    rope = rope_ref[:, cut].reshape(rows, ROPE)
    scores = []
    for c, chunk_ref in enumerate(chunk_refs):
        count = chunk_ref.shape[1]
        s = jnp.dot(latent, chunk_ref[:LAT, :], preferred_element_type=jnp.float32)
        s += jnp.dot(rope, chunk_ref[LAT:, :], preferred_element_type=jnp.float32)
        scores.append(s + bias_ref[:, c * count : (c + 1) * count])
    return scores


def weigh(scores, peak, chunk_refs):
    weights = [jnp.exp2((s - peak) * (score_scale * log2_e)) for s in scores]
    total = jnp.sum(functools.reduce(jnp.add, weights), axis=1, keepdims=True)
    mixed = sum(
        lax.dot_general(
            p.astype(jnp.bfloat16),
            chunk_ref[:LAT, :],
            (((1,), (1,)), ((), ())),
            preferred_element_type=jnp.float32,
        )
        for p, chunk_ref in zip(weights, chunk_refs)
    )
    return total, mixed


def near_kernel(
    bias_ref, latent_ref, rope_ref, k0, k1, k2, w_hbm, mixed_ref, stat_ref, w_ref, sem
):
    copy = pltpu.make_async_copy(w_hbm, w_ref, sem)
    copy.start()
    chunk_refs = (k0, k1, k2)
    cuts, rows, _ = mixed_ref.shape
    lane = lax.broadcasted_iota(jnp.int32, (rows, 128), 1)

    def body(cut, carry):
        scores = scores_of(latent_ref, rope_ref, cut, chunk_refs, bias_ref)
        peak = jnp.max(functools.reduce(jnp.maximum, scores), axis=1, keepdims=True)
        total, mixed = weigh(scores, peak, chunk_refs)
        mixed_ref[cut] = mixed
        stat_ref[cut] = jnp.where(lane == 0, peak, total)
        return carry

    lax.fori_loop(0, cuts, body, 0, unroll=2)
    copy.wait()


def apart(value):
    rows, width = value.shape
    tiles = value.reshape(rows // 16, 2, 8, width)
    first, second = tiles[:, 0], tiles[:, 1]
    upper_part = lax.broadcasted_iota(jnp.int32, first.shape, 1) < 4
    low = jnp.where(upper_part, first, pltpu.roll(second, 4, 1))
    high = jnp.where(upper_part, pltpu.roll(first, 4, 1), second)
    return low.reshape(rows // 2, width), high.reshape(rows // 2, width)


def together(low, high):
    rows, width = low.shape
    low = low.reshape(rows // 8, 8, width)
    high = high.reshape(rows // 8, 8, width)
    upper_part = lax.broadcasted_iota(jnp.int32, low.shape, 1) < 4
    first = jnp.where(upper_part, low, pltpu.roll(high, 4, 1))
    second = jnp.where(upper_part, pltpu.roll(low, 4, 1), high)
    return jnp.stack([first, second], axis=1).reshape(2 * rows, width)


def far_kernel(
    bias_ref, valid_ref, latent_ref, rope_ref, k3, mixed_ref, stat_ref, w_ref,
    keep_ref, send_ref, out_ref,
):
    items, cuts, heads, _ = latent_ref.shape
    rows = items * heads
    all_heads = cuts * heads

    out_ref[:, all_heads:, :] = jnp.zeros((items, PAD, 128), jnp.float32)
    head = lax.broadcasted_iota(jnp.int32, (rows, 128), 0) % heads
    lane = lax.broadcasted_iota(jnp.int32, (rows, 128), 1)
    half_heads = heads // 2
    head_of_half = lax.broadcasted_iota(jnp.int32, (rows // 2, 128), 0) % half_heads

    def body(cut, carry):
        scores = scores_of(latent_ref, rope_ref, cut, (k3,), bias_ref)
        old_peak, old_total = stat_ref[cut, :, 0:1], stat_ref[cut, :, 1:2]
        peak = jnp.maximum(old_peak, jnp.max(scores[0], axis=1, keepdims=True))
        factor = jnp.exp2((old_peak - peak) * (score_scale * log2_e))
        total, mixed = weigh(scores, peak, (k3,))
        total += old_total * factor
        valid = valid_ref[:, 0:1] > 0
        inverse = jnp.where(valid, 1.0 / total, 0.0)
        mixed = mixed * inverse + mixed_ref[cut] * (factor * inverse)
        level = jnp.where(valid, peak * score_scale + jnp.log(total), mask_value)
        low, high = apart(mixed)
        pieces = []
        for first, part in ((0, low), (half_heads, high)):
            upper = part.astype(jnp.bfloat16)
            lower = (part - upper.astype(jnp.float32)).astype(jnp.bfloat16)
            both = jnp.concatenate([upper, lower], axis=0)
            piece = jnp.zeros((rows // 2, 128), jnp.float32)
            for h in range(0, half_heads, 2):
                at = cut * heads + first + h
                pair = jnp.concatenate([w_ref[at], w_ref[at + 1]], axis=1)
                y = jnp.dot(both, pair, preferred_element_type=jnp.float32)
                y = y[: rows // 2] + y[rows // 2 :]
                piece = jnp.where(head_of_half == h, y[:, :128], piece)
                piece = jnp.where(head_of_half == h + 1, y[:, 128:], piece)
            pieces.append(piece)
        result = together(*pieces)
        at = pl.multiple_of(cut * heads, heads)
        out_ref[:, pl.ds(at, heads), :] = result.reshape(items, heads, 128)
        lines = jnp.where(lane == head + at, level, 0.0).reshape(items, heads, 128)
        lines = jnp.sum(lines, axis=1, keepdims=True)
        out_ref[:, all_heads:, :] += jnp.broadcast_to(lines, (items, PAD, 128))
        return carry

    lax.fori_loop(0, cuts, body, 0, unroll=2)
    half = items // 2
    core = lax.axis_index("dec") & 1

    def hand(i, carry):
        keep_ref[i] = out_ref[core * half + half - 1 - i]
        send_ref[i] = out_ref[(1 - core) * half + half - 1 - i]
        return carry

    lax.fori_loop(0, half, hand, 0)


def attend(near_bias, far_bias, valid, latent, rope, chunks, w_up):
    items, heads, _ = latent.shape
    cuts = heads // CUT_HEADS
    rows = items * CUT_HEADS
    latent = latent.reshape(items, cuts, CUT_HEADS, -1)
    rope = rope.reshape(items, cuts, CUT_HEADS, -1)
    vmem = pl.BlockSpec(memory_space=pltpu.VMEM)
    mixed, stat, w_near = pl.pallas_call(
        near_kernel,
        in_specs=[vmem] * 6 + [pl.BlockSpec(memory_space=pl.ANY)],
        out_specs=[vmem] * 3,
        out_shape=[
            jax.ShapeDtypeStruct((cuts, rows, LAT), jnp.float32),
            jax.ShapeDtypeStruct((cuts, rows, 128), jnp.float32),
            jax.ShapeDtypeStruct(w_up.shape, w_up.dtype),
        ],
        scratch_shapes=[pltpu.SemaphoreType.DMA(())],
        compiler_params=params(42),
        name="attend_near",
    )(near_bias, latent, rope, *chunks[:3], w_up)
    out_shape = jax.ShapeDtypeStruct((items // 2, heads + PAD, 128), jnp.float32)
    return pl.pallas_call(
        far_kernel,
        in_specs=[vmem] * 8,
        out_specs=[vmem] * 2,
        out_shape=[out_shape] * 2,
        scratch_shapes=[pltpu.VMEM((items, heads + PAD, 128), jnp.float32)],
        compiler_params=params(20),
        name="attend_far",
    )(far_bias, valid, latent, rope, chunks[3], mixed, stat, w_near)


def merge_step(levels):
    peak = functools.reduce(jnp.maximum, levels)
    scales = [jnp.exp(level - peak) for level in levels]
    total = functools.reduce(jnp.add, scales)
    return [scale / total for scale in scales], peak + jnp.log(total)


def spread_columns(line, heads):
    shape = line.shape[:-2] + (heads, line.shape[-1])
    axis = len(shape) - 1
    lane = lax.broadcasted_iota(jnp.int32, shape, axis)
    row = lax.broadcasted_iota(jnp.int32, shape, axis - 1)
    return jnp.sum(jnp.where(lane == row, line, 0.0), axis=axis, keepdims=True)


def pair_kernel(mine_ref, other_ref, out_ref):
    items, depth, _ = mine_ref.shape
    heads = depth - PAD
    step = 4

    def body(k, carry):
        at = pl.ds(k * step, step)
        parts = [mine_ref[at], other_ref[at]]
        scales, level = merge_step([part[:, heads:, :] for part in parts])
        result = sum(
            part[:, :heads, :] * spread_columns(scale[:, 0:1, :], heads)
            for part, scale in zip(parts, scales)
        )
        out_ref[at, :heads, :] = result
        out_ref[at, heads:, :] = level
        return carry

    lax.fori_loop(0, items // step, body, 0)


def merge_pair(mine, other):
    vmem = pl.BlockSpec(memory_space=pltpu.VMEM)
    return pl.pallas_call(
        pair_kernel,
        in_specs=[vmem] * 2,
        out_specs=vmem,
        out_shape=jax.ShapeDtypeStruct(mine.shape, mine.dtype),
        compiler_params=params(4),
        name="merge_pair",
    )(mine, other)


def merge_kernel(parts_ref, out_ref, scale_ref):
    sources, depth, lanes = parts_ref.shape
    heads = depth - PAD
    scales, _ = merge_step([parts_ref[k, heads:, :] for k in range(sources)])
    for k in range(sources):
        scale_ref[k] = scales[k]

    def body(k, so_far):
        return so_far + parts_ref[k, :heads, :] * spread_columns(scale_ref[k][0:1, :], heads)

    result = lax.fori_loop(
        0, sources, body, jnp.zeros((heads, lanes), jnp.float32), unroll=4
    ).astype(out_ref.dtype)
    for copy in range(out_ref.shape[0]):
        out_ref[copy] = result


def merge(parts):
    sources, depth, lanes = parts.shape
    vmem = pl.BlockSpec(memory_space=pltpu.VMEM)
    return pl.pallas_call(
        merge_kernel,
        in_specs=[vmem],
        out_specs=vmem,
        out_shape=jax.ShapeDtypeStruct((sources, depth - PAD, lanes), jnp.bfloat16),
        scratch_shapes=[pltpu.VMEM((sources, PAD, lanes), jnp.float32)],
        compiler_params=params(4),
        name="merge",
    )(parts)


def finish_kernel(mine_ref, other_ref, p0, p1, p2, p3, out_ref, cache_hbm, wide_ref, sems):
    group = lax.axis_index("pre")
    copies = []
    for k, (turn, piece) in enumerate(zip(TURNS, (p0, p1, p2, p3))):
        rows = piece.shape[1]
        at = pl.multiple_of((group ^ turn) * rows, rows)
        copies.append(
            pltpu.make_async_copy(piece, cache_hbm.at[:, pl.ds(at, rows)], sems.at[k])
        )
    for copy in copies:
        copy.start()
    half, heads, lanes = mine_ref.shape
    core = lax.axis_index("dec") & 1

    def widen(k, carry):
        for place_at, ref in ((core, mine_ref), (1 - core, other_ref)):
            item = place_at * half + half - 1 - k
            at = pl.ds(pl.multiple_of(item * heads, heads), heads)
            wide_ref[at, :] = ref[k].astype(jnp.float32)
        return carry

    lax.fori_loop(0, half, widen, 0, unroll=4)

    def body(h, carry):
        piece = wide_ref[pl.ds(h, 2 * half, stride=heads), :]
        at = pl.multiple_of(h * lanes, lanes)
        out_ref[:, pl.ds(at, lanes)] = piece.astype(out_ref.dtype)
        return carry

    lax.fori_loop(0, heads, body, 0, unroll=4)
    for copy in copies:
        copy.wait()


def finish(mine, other, pieces):
    half, heads, lanes = mine.shape
    width, rows = pieces[0].shape
    vmem = pl.BlockSpec(memory_space=pltpu.VMEM)
    return pl.pallas_call(
        finish_kernel,
        in_specs=[vmem] * 6,
        out_specs=[vmem, pl.BlockSpec(memory_space=pl.ANY)],
        out_shape=[
            jax.ShapeDtypeStruct((2 * half, heads * lanes), mine.dtype),
            jax.ShapeDtypeStruct((width, rows * len(pieces)), pieces[0].dtype),
        ],
        scratch_shapes=[
            pltpu.VMEM((2 * half * heads, lanes), jnp.float32),
            pltpu.SemaphoreType.DMA((len(pieces),)),
        ],
        compiler_params=params(6),
        name="finish",
    )(mine, other, *pieces)


def exchange(piece, groups, turn):
    return lax.ppermute(piece, "pre", [(i, i ^ turn) for i in range(groups)])


def around(piece, groups, owners):
    core = lax.axis_index("dec") % 2
    first = exchange(piece, groups, 3)
    second = exchange(piece, groups, 1)
    forward = [
        (g * owners + d, (g ^ (1 if d % 2 == 0 else 3)) * owners + d)
        for g in range(groups)
        for d in range(owners)
    ]
    chosen = jnp.where(core == 0, first, second)
    far = lax.ppermute(chosen, ("pre", "dec"), forward)
    return [piece, first, second, far], chosen


def per_device(
    hidden,
    w_down,
    kv_gain,
    query_latent,
    query_rope,
    w_up_value,
    request_rows,
    row_request,
    step_position,
    destination,
):
    groups = lax.axis_size("pre")
    owners = lax.axis_size("dec")
    steps, batch, heads, _ = query_latent.shape
    items = steps * batch
    plane = [[2 * k + core for k in reversed(range(SIDE * SIDE))] for core in range(2)]
    sibling = [(d, d ^ 1) for d in range(owners)]

    produced, packed = produce(
        groups, owners, request_rows, destination, hidden, w_down.T, kv_gain
    )
    chunks, chosen = around(produced, groups, owners)

    exchanged = functools.partial(
        lax.all_to_all, axis_name="dec", split_axis=0, concat_axis=0, tiled=True
    )
    lengths, _ = lax.optimization_barrier((request_rows, chosen))
    near_bias, far_bias, valid, chunks[0] = prepare(
        owners, groups, lengths, row_request, step_position, produced
    )
    keep, send = attend(
        near_bias,
        far_bias,
        valid,
        query_latent.reshape(items, heads, -1),
        query_rope.reshape(items, heads, -1),
        chunks,
        w_up_value,
    )
    arrived = exchanged(packed)
    quarter = place(arrived, *produced.shape)
    pieces = [quarter] + [exchange(quarter, groups, turn) for turn in TURNS[1:]]

    parts = merge_pair(keep, lax.ppermute(send, "dec", sibling))
    result = merge(exchanged(parts, axis_index_groups=plane))
    result = exchanged(result, axis_index_groups=plane)
    result, kv_cache = finish(result, lax.ppermute(result, "dec", sibling), pieces)
    attention_out = result.reshape(steps, batch, -1)
    kv_cache = kv_cache.T
    return (attention_out, kv_cache)


def solution(mesh):
    return jax.shard_map(
        per_device,
        mesh=mesh,
        in_specs=(
            P(("pre", "dec"), None),
            P(),
            P(),
            P(None, None, "pre", None),
            P(None, None, "pre", None),
            P("pre", None, None),
            P(),
            P(),
            P(),
            P(),
        ),
        out_specs=(P(None, None, "pre"), P("dec", None)),
        check_vma=False,
    )
```

```python
import functools
import math

import jax
import jax.numpy as jnp
import numpy as np
from jax import lax
from jax.experimental import pallas as pl
from jax.experimental.pallas import tpu as pltpu
from jax.sharding import PartitionSpec as P

LAT = 512
ROPE = 64
MOST = 2
PAD = 8
SIDE = 4
TURNS = (0, 3, 1, 2)
CUT_HEADS = 8
DEPTH = 1792

score_scale = 0.07216878364870323
mask_value = -1e30
norm_eps = 1e-06
log2_e = 1.4426950408889634


def frequencies():
    half = ROPE // 2
    pair_index = np.arange(half, dtype=np.float64)
    frequency = np.exp(pair_index * (-2.0 * math.log(10000.0) / ROPE)).astype(np.float32)
    return np.tile(frequency[:, None], (1, 128))


WIDE = 640


def shift_of(count):
    assert count & (count - 1) == 0
    return count.bit_length() - 1


def params(megabytes):
    return pltpu.CompilerParams(vmem_limit_bytes=megabytes * 1024 * 1024)


def produce_kernel(
    groups, owners, lengths_hbm, dest_hbm, hidden_hbm, w_hbm, gain_hbm, freq_hbm,
    out_ref, packed_ref, hidden_ref, w_ref, acc_ref, lengths_ref, dest_ref, gain_ref, freq_ref,
    turn_ref, column_ref, rows_ref, count_ref, slot_ref, sems, small_sems,
):
    pieces, rows, depth = hidden_ref.shape
    half = ROPE // 2
    small = [
        pltpu.make_async_copy(source, target, small_sems.at[k])
        for k, (source, target) in enumerate(
            (
                (lengths_hbm, lengths_ref),
                (dest_hbm, dest_ref),
                (gain_hbm, gain_ref),
                (freq_hbm, freq_ref),
            )
        )
    ]

    def copies(k):
        columns = pl.ds(pl.multiple_of(k * depth, depth), depth)
        return (
            pltpu.make_async_copy(hidden_hbm.at[:, columns], hidden_ref.at[k], sems.at[0, k]),
            pltpu.make_async_copy(w_hbm.at[:, columns], w_ref.at[k], sems.at[1, k]),
        )

    def begin(k, carry):
        for copy in copies(k):
            copy.start()
        return carry

    for copy in small:
        copy.start()
    lax.fori_loop(0, pieces, begin, 0)
    acc_ref[...] = jnp.zeros_like(acc_ref)
    packed_ref[...] = jnp.full(packed_ref.shape, -1.0, packed_ref.dtype)
    for copy in small:
        copy.wait()
    group = lax.axis_index("pre")
    device = group * owners + lax.axis_index("dec")
    block_rows = packed_ref.shape[1]
    blocks = rows // block_rows

    def clear(owner, carry):
        count_ref[owner] = 0
        return carry

    def choose(b, carry):
        owner = lax.shift_right_logical(dest_ref[device * blocks + b], shift_of(groups * owners))
        rank = count_ref[owner]
        count_ref[owner] = rank + 1
        slot_ref[b] = (owners - 1 - owner) * MOST + rank
        return carry

    lax.fori_loop(0, owners, clear, 0)
    lax.fori_loop(0, blocks, choose, 0)
    row = device * rows + lax.broadcasted_iota(jnp.int32, (1, rows), 1)
    start = jnp.zeros((1, rows), jnp.int32)
    first_row = jnp.int32(0)
    for r in range(lengths_ref.shape[0] - 1):
        first_row = first_row + lengths_ref[r]
        start = jnp.where(row >= first_row, first_row, start)
    angles = freq_ref[:, 0:1] * (row - start).astype(jnp.float32)
    turn_ref[:half, :] = jnp.cos(angles)
    turn_ref[half:, :] = jnp.sin(angles)
    column_ref[...] = jnp.transpose(jnp.broadcast_to(gain_ref[...], (128, LAT)))

    def body(k, carry):
        for copy in copies(k):
            copy.wait()
        acc_ref[...] += lax.dot_general(
            w_ref[k],
            hidden_ref[k],
            (((1,), (1,)), ((), ())),
            preferred_element_type=jnp.float32,
        )
        return carry

    lax.fori_loop(0, pieces, body, 0)
    latent = acc_ref[:LAT, :]
    inverse_rms = lax.rsqrt(jnp.mean(latent * latent, axis=0, keepdims=True) + norm_eps)
    out_ref[:LAT, :] = (latent * inverse_rms * column_ref[:, 0:1]).astype(out_ref.dtype)
    cosine, sine = turn_ref[:half, :], turn_ref[half:, :]
    first = acc_ref[LAT : LAT + half, :]
    second = acc_ref[LAT + half :, :]
    turned = first * cosine - second * sine
    out_ref[LAT : LAT + half, :] = turned.astype(out_ref.dtype)
    turned = second * cosine + first * sine
    out_ref[LAT + half :, :] = turned.astype(out_ref.dtype)
    width = out_ref.shape[0]
    for at in range(0, width, 128):
        count = min(128, width - at)
        wide = out_ref[at : at + count, :].astype(jnp.float32)
        if count < 128:
            wide = jnp.concatenate([wide, jnp.zeros((128 - count, rows), jnp.float32)], axis=0)
        rows_ref[:, :, at : at + 128] = jnp.transpose(wide).reshape(blocks, block_rows, 128)
    lane = lax.broadcasted_iota(jnp.int32, (block_rows, WIDE), 1)

    def put(b, carry):
        place_at = (dest_ref[device * blocks + b] & (groups * owners - 1)) - group * owners
        block = jnp.where(lane < width, rows_ref[b], place_at.astype(jnp.float32))
        packed_ref[slot_ref[b]] = block.astype(packed_ref.dtype)
        return carry

    lax.fori_loop(0, blocks, put, 0, unroll=4)


def produce(groups, owners, lengths, destination, hidden, w_turned, gain):
    rows, width = hidden.shape
    row_width = w_turned.shape[0]
    pieces = width // DEPTH
    block_rows = rows // owners
    vmem = pl.BlockSpec(memory_space=pltpu.VMEM)
    return pl.pallas_call(
        functools.partial(produce_kernel, groups, owners),
        in_specs=[pl.BlockSpec(memory_space=pltpu.HBM)] * 6,
        out_specs=[vmem, vmem],
        out_shape=[
            jax.ShapeDtypeStruct((row_width, rows), jnp.bfloat16),
            jax.ShapeDtypeStruct((owners * MOST, block_rows, WIDE), jnp.bfloat16),
        ],
        scratch_shapes=[
            pltpu.VMEM((pieces, rows, DEPTH), jnp.bfloat16),
            pltpu.VMEM((pieces, row_width, DEPTH), jnp.bfloat16),
            pltpu.VMEM((row_width, rows), jnp.float32),
            pltpu.SMEM(lengths.shape, jnp.int32),
            pltpu.SMEM(destination.shape, jnp.int32),
            pltpu.VMEM((1, LAT), jnp.float32),
            pltpu.VMEM((ROPE // 2, 128), jnp.float32),
            pltpu.VMEM((ROPE, rows), jnp.float32),
            pltpu.VMEM((LAT, 128), jnp.float32),
            pltpu.VMEM((owners, block_rows, WIDE), jnp.float32),
            pltpu.SMEM((owners,), jnp.int32),
            pltpu.SMEM((owners,), jnp.int32),
            pltpu.SemaphoreType.DMA((2, pieces)),
            pltpu.SemaphoreType.DMA((4,)),
        ],
        name="produce",
    )(
        lengths,
        destination,
        hidden,
        w_turned,
        gain.reshape(1, -1),
        jnp.asarray(frequencies()),
    )


def place_kernel(arrived_ref, out_ref, rows_ref):
    blocks, block_rows, _ = arrived_ref.shape
    width, rows = out_ref.shape
    depth = 256
    part = depth // block_rows
    row = lax.broadcasted_iota(jnp.int32, (rows, depth), 0).astype(jnp.float32)
    lane = lax.broadcasted_iota(jnp.int32, (1, depth), 1)
    within = lax.rem(lane, block_rows).astype(jnp.float32)
    for k in range(blocks // part):
        source = arrived_ref[k * part : (k + 1) * part].astype(jnp.float32).reshape(depth, WIDE)
        slot = jnp.transpose(source[:, WIDE - 128 :])[127:128, :]
        select = jnp.where(row == slot * block_rows + within, 1.0, 0.0).astype(jnp.bfloat16)
        placed = jnp.dot(select, source.astype(jnp.bfloat16), preferred_element_type=jnp.float32)
        if k == 0:
            rows_ref[...] = placed
        else:
            rows_ref[...] += placed
    for at in range(0, width, 128):
        count = min(128, width - at)
        turned = jnp.transpose(rows_ref[:, at : at + 128])
        out_ref[at : at + count, :] = turned[:count].astype(out_ref.dtype)


def place(arrived, width, rows):
    vmem = pl.BlockSpec(memory_space=pltpu.VMEM)
    return pl.pallas_call(
        place_kernel,
        in_specs=[vmem],
        out_specs=vmem,
        out_shape=jax.ShapeDtypeStruct((width, rows), arrived.dtype),
        scratch_shapes=[pltpu.VMEM((rows, WIDE), jnp.float32)],
        compiler_params=params(8),
        name="place",
    )(arrived)


def prepare_kernel(
    owners, lengths_ref, request_ref, position_ref, own_hbm,
    near_ref, far_ref, valid_ref, own_ref, sem,
):
    copy = pltpu.make_async_copy(own_hbm, own_ref, sem)
    copy.start()
    steps, batch = position_ref.shape
    heads = CUT_HEADS
    count = own_ref.shape[1]
    group, owner = lax.axis_index("pre"), lax.axis_index("dec")
    row = lax.broadcasted_iota(jnp.int32, (heads, count), 1)
    bases = [((group ^ turn) * owners + owner) * count for turn in TURNS]

    def fill(b, carry):
        request = request_ref[b]
        start = jnp.int32(0)
        for r in range(lengths_ref.shape[0] - 1):
            start = start + jnp.where(request > r, lengths_ref[r], 0)
        for s in range(steps):
            stop = start + position_ref[s, b]
            at = pl.ds(pl.multiple_of((s * batch + b) * heads, heads), heads)
            seen = jnp.int32(0)
            for c, base in enumerate(bases):
                bias = jnp.where((row >= start - base) & (row < stop - base), 0.0, mask_value)
                if c < len(bases) - 1:
                    near_ref[at, c * count : (c + 1) * count] = bias
                else:
                    far_ref[at, :] = bias
                seen = seen + jnp.where((start < base + count) & (stop > base), 1, 0)
            valid_ref[at, :] = jnp.full((heads, 128), seen, jnp.int32)
        return carry

    lax.fori_loop(0, batch, fill, 0)
    copy.wait()


def prepare(owners, groups, lengths, row_request, step_position, own):
    rows = step_position.size * CUT_HEADS
    smem = pl.BlockSpec(memory_space=pltpu.SMEM)
    vmem = pl.BlockSpec(memory_space=pltpu.VMEM)
    return pl.pallas_call(
        functools.partial(prepare_kernel, owners),
        in_specs=[smem] * 3 + [pl.BlockSpec(memory_space=pl.ANY)],
        out_specs=[vmem] * 4,
        out_shape=[
            jax.ShapeDtypeStruct((rows, (groups - 1) * own.shape[1]), jnp.float32),
            jax.ShapeDtypeStruct((rows, own.shape[1]), jnp.float32),
            jax.ShapeDtypeStruct((rows, 128), jnp.int32),
            jax.ShapeDtypeStruct(own.shape, own.dtype),
        ],
        scratch_shapes=[pltpu.SemaphoreType.DMA(())],
        compiler_params=params(8),
        name="prepare",
    )(lengths, row_request, step_position, own)


def scores_of(latent_ref, rope_ref, cut, chunk_refs, bias_ref):
    items, _, heads, _ = latent_ref.shape
    rows = items * heads
    latent = latent_ref[:, cut].reshape(rows, LAT)
    rope = rope_ref[:, cut].reshape(rows, ROPE)
    scores = []
    for c, chunk_ref in enumerate(chunk_refs):
        count = chunk_ref.shape[1]
        s = jnp.dot(latent, chunk_ref[:LAT, :], preferred_element_type=jnp.float32)
        s += jnp.dot(rope, chunk_ref[LAT:, :], preferred_element_type=jnp.float32)
        scores.append(s + bias_ref[:, c * count : (c + 1) * count])
    return scores


def weigh(scores, peak, chunk_refs):
    weights = [jnp.exp2((s - peak) * (score_scale * log2_e)) for s in scores]
    total = jnp.sum(functools.reduce(jnp.add, weights), axis=1, keepdims=True)
    mixed = sum(
        lax.dot_general(
            p.astype(jnp.bfloat16),
            chunk_ref[:LAT, :],
            (((1,), (1,)), ((), ())),
            preferred_element_type=jnp.float32,
        )
        for p, chunk_ref in zip(weights, chunk_refs)
    )
    return total, mixed


def near_kernel(
    bias_ref, latent_ref, rope_ref, k0, k1, k2, w_hbm, mixed_ref, stat_ref, w_ref, sem
):
    copy = pltpu.make_async_copy(w_hbm, w_ref, sem)
    copy.start()
    chunk_refs = (k0, k1, k2)
    cuts, rows, _ = mixed_ref.shape
    lane = lax.broadcasted_iota(jnp.int32, (rows, 128), 1)

    def body(cut, carry):
        scores = scores_of(latent_ref, rope_ref, cut, chunk_refs, bias_ref)
        peak = jnp.max(functools.reduce(jnp.maximum, scores), axis=1, keepdims=True)
        total, mixed = weigh(scores, peak, chunk_refs)
        mixed_ref[cut] = mixed
        stat_ref[cut] = jnp.where(lane == 0, peak, total)
        return carry

    lax.fori_loop(0, cuts, body, 0, unroll=2)
    copy.wait()


def apart(value):
    rows, width = value.shape
    tiles = value.reshape(rows // 16, 2, 8, width)
    first, second = tiles[:, 0], tiles[:, 1]
    upper_part = lax.broadcasted_iota(jnp.int32, first.shape, 1) < 4
    low = jnp.where(upper_part, first, pltpu.roll(second, 4, 1))
    high = jnp.where(upper_part, pltpu.roll(first, 4, 1), second)
    return low.reshape(rows // 2, width), high.reshape(rows // 2, width)


def together(low, high):
    rows, width = low.shape
    low = low.reshape(rows // 8, 8, width)
    high = high.reshape(rows // 8, 8, width)
    upper_part = lax.broadcasted_iota(jnp.int32, low.shape, 1) < 4
    first = jnp.where(upper_part, low, pltpu.roll(high, 4, 1))
    second = jnp.where(upper_part, pltpu.roll(low, 4, 1), high)
    return jnp.stack([first, second], axis=1).reshape(2 * rows, width)


def far_kernel(
    bias_ref, valid_ref, latent_ref, rope_ref, k3, mixed_ref, stat_ref, w_ref,
    keep_ref, send_ref, out_ref,
):
    items, cuts, heads, _ = latent_ref.shape
    rows = items * heads
    all_heads = cuts * heads

    out_ref[:, all_heads:, :] = jnp.zeros((items, PAD, 128), jnp.float32)
    head = lax.broadcasted_iota(jnp.int32, (rows, 128), 0) % heads
    lane = lax.broadcasted_iota(jnp.int32, (rows, 128), 1)
    half_heads = heads // 2
    head_of_half = lax.broadcasted_iota(jnp.int32, (rows // 2, 128), 0) % half_heads

    def body(cut, carry):
        scores = scores_of(latent_ref, rope_ref, cut, (k3,), bias_ref)
        old_peak, old_total = stat_ref[cut, :, 0:1], stat_ref[cut, :, 1:2]
        peak = jnp.maximum(old_peak, jnp.max(scores[0], axis=1, keepdims=True))
        factor = jnp.exp2((old_peak - peak) * (score_scale * log2_e))
        total, mixed = weigh(scores, peak, (k3,))
        total += old_total * factor
        valid = valid_ref[:, 0:1] > 0
        inverse = jnp.where(valid, 1.0 / total, 0.0)
        mixed = mixed * inverse + mixed_ref[cut] * (factor * inverse)
        level = jnp.where(valid, peak * score_scale + jnp.log(total), mask_value)
        low, high = apart(mixed)
        pieces = []
        for first, part in ((0, low), (half_heads, high)):
            upper = part.astype(jnp.bfloat16)
            lower = (part - upper.astype(jnp.float32)).astype(jnp.bfloat16)
            both = jnp.concatenate([upper, lower], axis=0)
            piece = jnp.zeros((rows // 2, 128), jnp.float32)
            for h in range(0, half_heads, 2):
                at = cut * heads + first + h
                pair = jnp.concatenate([w_ref[at], w_ref[at + 1]], axis=1)
                y = jnp.dot(both, pair, preferred_element_type=jnp.float32)
                y = y[: rows // 2] + y[rows // 2 :]
                piece = jnp.where(head_of_half == h, y[:, :128], piece)
                piece = jnp.where(head_of_half == h + 1, y[:, 128:], piece)
            pieces.append(piece)
        result = together(*pieces)
        at = pl.multiple_of(cut * heads, heads)
        out_ref[:, pl.ds(at, heads), :] = result.reshape(items, heads, 128)
        lines = jnp.where(lane == head + at, level, 0.0).reshape(items, heads, 128)
        lines = jnp.sum(lines, axis=1, keepdims=True)
        out_ref[:, all_heads:, :] += jnp.broadcast_to(lines, (items, PAD, 128))
        return carry

    lax.fori_loop(0, cuts, body, 0, unroll=2)
    half = items // 2
    core = lax.axis_index("dec") & 1

    def hand(i, carry):
        keep_ref[i] = out_ref[core * half + half - 1 - i]
        send_ref[i] = out_ref[(1 - core) * half + half - 1 - i]
        return carry

    lax.fori_loop(0, half, hand, 0)


def attend(near_bias, far_bias, valid, latent, rope, chunks, w_up):
    items, heads, _ = latent.shape
    cuts = heads // CUT_HEADS
    rows = items * CUT_HEADS
    latent = latent.reshape(items, cuts, CUT_HEADS, -1)
    rope = rope.reshape(items, cuts, CUT_HEADS, -1)
    vmem = pl.BlockSpec(memory_space=pltpu.VMEM)
    mixed, stat, w_near = pl.pallas_call(
        near_kernel,
        in_specs=[vmem] * 6 + [pl.BlockSpec(memory_space=pl.ANY)],
        out_specs=[vmem] * 3,
        out_shape=[
            jax.ShapeDtypeStruct((cuts, rows, LAT), jnp.float32),
            jax.ShapeDtypeStruct((cuts, rows, 128), jnp.float32),
            jax.ShapeDtypeStruct(w_up.shape, w_up.dtype),
        ],
        scratch_shapes=[pltpu.SemaphoreType.DMA(())],
        compiler_params=params(42),
        name="attend_near",
    )(near_bias, latent, rope, *chunks[:3], w_up)
    out_shape = jax.ShapeDtypeStruct((items // 2, heads + PAD, 128), jnp.float32)
    return pl.pallas_call(
        far_kernel,
        in_specs=[vmem] * 8,
        out_specs=[vmem] * 2,
        out_shape=[out_shape] * 2,
        scratch_shapes=[pltpu.VMEM((items, heads + PAD, 128), jnp.float32)],
        compiler_params=params(20),
        name="attend_far",
    )(far_bias, valid, latent, rope, chunks[3], mixed, stat, w_near)


def merge_step(levels):
    peak = functools.reduce(jnp.maximum, levels)
    scales = [jnp.exp(level - peak) for level in levels]
    total = functools.reduce(jnp.add, scales)
    return [scale / total for scale in scales], peak + jnp.log(total)


def spread_columns(line, heads):
    shape = line.shape[:-2] + (heads, line.shape[-1])
    axis = len(shape) - 1
    lane = lax.broadcasted_iota(jnp.int32, shape, axis)
    row = lax.broadcasted_iota(jnp.int32, shape, axis - 1)
    return jnp.sum(jnp.where(lane == row, line, 0.0), axis=axis, keepdims=True)


def pair_kernel(mine_ref, other_ref, out_ref):
    items, depth, _ = mine_ref.shape
    heads = depth - PAD
    step = 4

    def body(k, carry):
        at = pl.ds(k * step, step)
        parts = [mine_ref[at], other_ref[at]]
        scales, level = merge_step([part[:, heads:, :] for part in parts])
        result = sum(
            part[:, :heads, :] * spread_columns(scale[:, 0:1, :], heads)
            for part, scale in zip(parts, scales)
        )
        out_ref[at, :heads, :] = result
        out_ref[at, heads:, :] = level
        return carry

    lax.fori_loop(0, items // step, body, 0)


def merge_pair(mine, other):
    vmem = pl.BlockSpec(memory_space=pltpu.VMEM)
    return pl.pallas_call(
        pair_kernel,
        in_specs=[vmem] * 2,
        out_specs=vmem,
        out_shape=jax.ShapeDtypeStruct(mine.shape, mine.dtype),
        compiler_params=params(4),
        name="merge_pair",
    )(mine, other)


def merge_kernel(parts_ref, out_ref, scale_ref):
    sources, depth, lanes = parts_ref.shape
    heads = depth - PAD
    scales, _ = merge_step([parts_ref[k, heads:, :] for k in range(sources)])
    for k in range(sources):
        scale_ref[k] = scales[k]

    def body(k, so_far):
        return so_far + parts_ref[k, :heads, :] * spread_columns(scale_ref[k][0:1, :], heads)

    result = lax.fori_loop(
        0, sources, body, jnp.zeros((heads, lanes), jnp.float32), unroll=4
    ).astype(out_ref.dtype)
    for copy in range(out_ref.shape[0]):
        out_ref[copy] = result


def merge(parts):
    sources, depth, lanes = parts.shape
    vmem = pl.BlockSpec(memory_space=pltpu.VMEM)
    return pl.pallas_call(
        merge_kernel,
        in_specs=[vmem],
        out_specs=vmem,
        out_shape=jax.ShapeDtypeStruct((sources, depth - PAD, lanes), jnp.bfloat16),
        scratch_shapes=[pltpu.VMEM((sources, PAD, lanes), jnp.float32)],
        compiler_params=params(4),
        name="merge",
    )(parts)


def finish_kernel(mine_ref, other_ref, p0, p1, p2, p3, out_ref, cache_hbm, wide_ref, sems):
    group = lax.axis_index("pre")
    copies = []
    for k, (turn, piece) in enumerate(zip(TURNS, (p0, p1, p2, p3))):
        rows = piece.shape[1]
        at = pl.multiple_of((group ^ turn) * rows, rows)
        copies.append(
            pltpu.make_async_copy(piece, cache_hbm.at[:, pl.ds(at, rows)], sems.at[k])
        )
    for copy in copies:
        copy.start()
    half, heads, lanes = mine_ref.shape
    core = lax.axis_index("dec") & 1

    def widen(k, carry):
        for place_at, ref in ((core, mine_ref), (1 - core, other_ref)):
            item = place_at * half + half - 1 - k
            at = pl.ds(pl.multiple_of(item * heads, heads), heads)
            wide_ref[at, :] = ref[k].astype(jnp.float32)
        return carry

    lax.fori_loop(0, half, widen, 0, unroll=4)

    def body(h, carry):
        piece = wide_ref[pl.ds(h, 2 * half, stride=heads), :]
        at = pl.multiple_of(h * lanes, lanes)
        out_ref[:, pl.ds(at, lanes)] = piece.astype(out_ref.dtype)
        return carry

    lax.fori_loop(0, heads, body, 0, unroll=4)
    for copy in copies:
        copy.wait()


def finish(mine, other, pieces):
    half, heads, lanes = mine.shape
    width, rows = pieces[0].shape
    vmem = pl.BlockSpec(memory_space=pltpu.VMEM)
    return pl.pallas_call(
        finish_kernel,
        in_specs=[vmem] * 6,
        out_specs=[vmem, pl.BlockSpec(memory_space=pl.ANY)],
        out_shape=[
            jax.ShapeDtypeStruct((2 * half, heads * lanes), mine.dtype),
            jax.ShapeDtypeStruct((width, rows * len(pieces)), pieces[0].dtype),
        ],
        scratch_shapes=[
            pltpu.VMEM((2 * half * heads, lanes), jnp.float32),
            pltpu.SemaphoreType.DMA((len(pieces),)),
        ],
        compiler_params=params(6),
        name="finish",
    )(mine, other, *pieces)


def exchange(piece, groups, turn):
    return lax.ppermute(piece, "pre", [(i, i ^ turn) for i in range(groups)])


def around(piece, groups, owners):
    core = lax.axis_index("dec") % 2
    first = exchange(piece, groups, 3)
    second = exchange(piece, groups, 1)
    forward = [
        (g * owners + d, (g ^ (1 if d % 2 == 0 else 3)) * owners + d)
        for g in range(groups)
        for d in range(owners)
    ]
    chosen = jnp.where(core == 0, first, second)
    far = lax.ppermute(chosen, ("pre", "dec"), forward)
    return [piece, first, second, far], chosen


def per_device(
    hidden,
    w_down,
    kv_gain,
    query_latent,
    query_rope,
    w_up_value,
    request_rows,
    row_request,
    step_position,
    destination,
):
    groups = lax.axis_size("pre")
    owners = lax.axis_size("dec")
    steps, batch, heads, _ = query_latent.shape
    items = steps * batch
    plane = [[2 * k + core for k in reversed(range(SIDE * SIDE))] for core in range(2)]
    sibling = [(d, d ^ 1) for d in range(owners)]

    produced, packed = produce(
        groups, owners, request_rows, destination, hidden, w_down.T, kv_gain
    )
    chunks, chosen = around(produced, groups, owners)

    exchanged = functools.partial(
        lax.all_to_all, axis_name="dec", split_axis=0, concat_axis=0, tiled=True
    )
    lengths, _ = lax.optimization_barrier((request_rows, chosen))
    near_bias, far_bias, valid, chunks[0] = prepare(
        owners, groups, lengths, row_request, step_position, produced
    )
    keep, send = attend(
        near_bias,
        far_bias,
        valid,
        query_latent.reshape(items, heads, -1),
        query_rope.reshape(items, heads, -1),
        chunks,
        w_up_value,
    )
    arrived = exchanged(packed, axis_index_groups=[list(reversed(range(owners)))])
    quarter = place(arrived, *produced.shape)
    pieces = [quarter] + [exchange(quarter, groups, turn) for turn in TURNS[1:]]

    parts = merge_pair(keep, lax.ppermute(send, "dec", sibling))
    result = merge(exchanged(parts, axis_index_groups=plane))
    result = exchanged(result, axis_index_groups=plane)
    result, kv_cache = finish(result, lax.ppermute(result, "dec", sibling), pieces)
    attention_out = result.reshape(steps, batch, -1)
    kv_cache = kv_cache.T
    return (attention_out, kv_cache)


def solution(mesh):
    return jax.shard_map(
        per_device,
        mesh=mesh,
        in_specs=(
            P(("pre", "dec"), None),
            P(),
            P(),
            P(None, None, "pre", None),
            P(None, None, "pre", None),
            P("pre", None, None),
            P(),
            P(),
            P(),
            P(),
        ),
        out_specs=(P(None, None, "pre"), P("dec", None)),
        check_vma=False,
    )
```

```python
import functools
import math

import jax
import jax.numpy as jnp
import numpy as np
from jax import lax
from jax.experimental import pallas as pl
from jax.experimental.pallas import tpu as pltpu
from jax.sharding import PartitionSpec as P

LAT = 512
ROPE = 64
MOST = 2
PAD = 8
SIDE = 4
TURNS = (0, 3, 1, 2)
CUT_HEADS = 8
DEPTH = 1792

score_scale = 0.07216878364870323
mask_value = -1e30
norm_eps = 1e-06
log2_e = 1.4426950408889634


def frequencies():
    half = ROPE // 2
    pair_index = np.arange(half, dtype=np.float64)
    frequency = np.exp(pair_index * (-2.0 * math.log(10000.0) / ROPE)).astype(np.float32)
    return np.tile(frequency[:, None], (1, 128))


WIDE = 640


def shift_of(count):
    assert count & (count - 1) == 0
    return count.bit_length() - 1


def params(megabytes):
    return pltpu.CompilerParams(vmem_limit_bytes=megabytes * 1024 * 1024)


def produce_kernel(
    owners, lengths_hbm, hidden_hbm, w_hbm, gain_hbm, freq_hbm,
    out_ref, hidden_ref, w_ref, acc_ref, lengths_ref, gain_ref, freq_ref, turn_ref, column_ref,
    sems, small_sems,
):
    pieces, rows, depth = hidden_ref.shape
    half = ROPE // 2
    small = [
        pltpu.make_async_copy(source, target, small_sems.at[k])
        for k, (source, target) in enumerate(
            ((lengths_hbm, lengths_ref), (gain_hbm, gain_ref), (freq_hbm, freq_ref))
        )
    ]

    def copies(k):
        columns = pl.ds(pl.multiple_of(k * depth, depth), depth)
        return (
            pltpu.make_async_copy(hidden_hbm.at[:, columns], hidden_ref.at[k], sems.at[0, k]),
            pltpu.make_async_copy(w_hbm.at[:, columns], w_ref.at[k], sems.at[1, k]),
        )

    def begin(k, carry):
        for copy in copies(k):
            copy.start()
        return carry

    for copy in small:
        copy.start()
    lax.fori_loop(0, pieces, begin, 0)
    acc_ref[...] = jnp.zeros_like(acc_ref)
    for copy in small:
        copy.wait()
    device = lax.axis_index("pre") * owners + lax.axis_index("dec")
    row = device * rows + lax.broadcasted_iota(jnp.int32, (1, rows), 1)
    start = jnp.zeros((1, rows), jnp.int32)
    first_row = jnp.int32(0)
    for r in range(lengths_ref.shape[0] - 1):
        first_row = first_row + lengths_ref[r]
        start = jnp.where(row >= first_row, first_row, start)
    angles = freq_ref[:, 0:1] * (row - start).astype(jnp.float32)
    turn_ref[:half, :] = jnp.cos(angles)
    turn_ref[half:, :] = jnp.sin(angles)
    column_ref[...] = jnp.transpose(jnp.broadcast_to(gain_ref[...], (128, LAT)))

    def body(k, carry):
        for copy in copies(k):
            copy.wait()
        acc_ref[...] += lax.dot_general(
            w_ref[k],
            hidden_ref[k],
            (((1,), (1,)), ((), ())),
            preferred_element_type=jnp.float32,
        )
        return carry

    lax.fori_loop(0, pieces, body, 0)
    latent = acc_ref[:LAT, :]
    inverse_rms = lax.rsqrt(jnp.mean(latent * latent, axis=0, keepdims=True) + norm_eps)
    out_ref[:LAT, :] = (latent * inverse_rms * column_ref[:, 0:1]).astype(out_ref.dtype)
    cosine, sine = turn_ref[:half, :], turn_ref[half:, :]
    first = acc_ref[LAT : LAT + half, :]
    second = acc_ref[LAT + half :, :]
    turned = first * cosine - second * sine
    out_ref[LAT : LAT + half, :] = turned.astype(out_ref.dtype)
    turned = second * cosine + first * sine
    out_ref[LAT + half :, :] = turned.astype(out_ref.dtype)


def produce(owners, lengths, hidden, w_turned, gain):
    rows, width = hidden.shape
    row_width = w_turned.shape[0]
    pieces = width // DEPTH
    return pl.pallas_call(
        functools.partial(produce_kernel, owners),
        in_specs=[pl.BlockSpec(memory_space=pltpu.HBM)] * 5,
        out_specs=pl.BlockSpec(memory_space=pltpu.VMEM),
        out_shape=jax.ShapeDtypeStruct((row_width, rows), jnp.bfloat16),
        scratch_shapes=[
            pltpu.VMEM((pieces, rows, DEPTH), jnp.bfloat16),
            pltpu.VMEM((pieces, row_width, DEPTH), jnp.bfloat16),
            pltpu.VMEM((row_width, rows), jnp.float32),
            pltpu.SMEM(lengths.shape, jnp.int32),
            pltpu.VMEM((1, LAT), jnp.float32),
            pltpu.VMEM((ROPE // 2, 128), jnp.float32),
            pltpu.VMEM((ROPE, rows), jnp.float32),
            pltpu.VMEM((LAT, 128), jnp.float32),
            pltpu.SemaphoreType.DMA((2, pieces)),
            pltpu.SemaphoreType.DMA((3,)),
        ],
        name="produce",
    )(lengths, hidden, w_turned, gain.reshape(1, -1), jnp.asarray(frequencies()))


def pack_kernel(
    groups, owners, dest_hbm, rows_hbm, out_ref, turned_ref, dest_ref, rows_ref, count_ref, slot_ref,
    sems,
):
    dest_copy = pltpu.make_async_copy(dest_hbm, dest_ref, sems.at[0])
    rows_copy = pltpu.make_async_copy(rows_hbm, rows_ref, sems.at[1])
    dest_copy.start()
    rows_copy.start()
    width, rows = rows_ref.shape
    block_rows = out_ref.shape[1]
    blocks = rows // block_rows
    group = lax.axis_index("pre")
    first = (group * owners + lax.axis_index("dec")) * blocks
    out_ref[...] = jnp.full(out_ref.shape, -1.0, out_ref.dtype)

    def clear(owner, carry):
        count_ref[owner] = 0
        return carry

    def choose(b, carry):
        owner = lax.shift_right_logical(dest_ref[first + b], shift_of(groups * owners))
        rank = count_ref[owner]
        count_ref[owner] = rank + 1
        slot_ref[b] = (owners - 1 - owner) * MOST + rank
        return carry

    lax.fori_loop(0, owners, clear, 0)
    dest_copy.wait()
    lax.fori_loop(0, blocks, choose, 0)
    rows_copy.wait()
    for at in range(0, width, 128):
        count = min(128, width - at)
        wide = rows_ref[at : at + count, :].astype(jnp.float32)
        if count < 128:
            wide = jnp.concatenate([wide, jnp.zeros((128 - count, rows), jnp.float32)], axis=0)
        turned_ref[:, :, at : at + 128] = jnp.transpose(wide).reshape(blocks, block_rows, 128)
    lane = lax.broadcasted_iota(jnp.int32, (block_rows, WIDE), 1)

    def put(b, carry):
        place_at = (dest_ref[first + b] & (groups * owners - 1)) - group * owners
        block = jnp.where(lane < width, turned_ref[b], place_at.astype(jnp.float32))
        out_ref[slot_ref[b]] = block.astype(out_ref.dtype)
        return carry

    lax.fori_loop(0, blocks, put, 0, unroll=4)


def pack(groups, owners, destination, produced):
    width, rows = produced.shape
    block_rows = rows // owners
    return pl.pallas_call(
        functools.partial(pack_kernel, groups, owners),
        in_specs=[pl.BlockSpec(memory_space=pltpu.HBM)] * 2,
        out_specs=pl.BlockSpec(memory_space=pltpu.VMEM),
        out_shape=jax.ShapeDtypeStruct((owners * MOST, block_rows, WIDE), produced.dtype),
        scratch_shapes=[
            pltpu.VMEM((owners, block_rows, WIDE), jnp.float32),
            pltpu.SMEM(destination.shape, jnp.int32),
            pltpu.VMEM(produced.shape, produced.dtype),
            pltpu.SMEM((owners,), jnp.int32),
            pltpu.SMEM((owners,), jnp.int32),
            pltpu.SemaphoreType.DMA((2,)),
        ],
        name="pack",
    )(destination, produced)


def place_kernel(arrived_ref, out_ref, rows_ref):
    blocks, block_rows, _ = arrived_ref.shape
    width, rows = out_ref.shape
    depth = 256
    part = depth // block_rows
    row = lax.broadcasted_iota(jnp.int32, (rows, depth), 0).astype(jnp.float32)
    lane = lax.broadcasted_iota(jnp.int32, (1, depth), 1)
    within = lax.rem(lane, block_rows).astype(jnp.float32)
    for k in range(blocks // part):
        source = arrived_ref[k * part : (k + 1) * part].astype(jnp.float32).reshape(depth, WIDE)
        slot = jnp.transpose(source[:, WIDE - 128 :])[127:128, :]
        select = jnp.where(row == slot * block_rows + within, 1.0, 0.0).astype(jnp.bfloat16)
        placed = jnp.dot(select, source.astype(jnp.bfloat16), preferred_element_type=jnp.float32)
        if k == 0:
            rows_ref[...] = placed
        else:
            rows_ref[...] += placed
    for at in range(0, width, 128):
        count = min(128, width - at)
        turned = jnp.transpose(rows_ref[:, at : at + 128])
        out_ref[at : at + count, :] = turned[:count].astype(out_ref.dtype)


def place(arrived, width, rows):
    vmem = pl.BlockSpec(memory_space=pltpu.VMEM)
    return pl.pallas_call(
        place_kernel,
        in_specs=[vmem],
        out_specs=vmem,
        out_shape=jax.ShapeDtypeStruct((width, rows), arrived.dtype),
        scratch_shapes=[pltpu.VMEM((rows, WIDE), jnp.float32)],
        compiler_params=params(8),
        name="place",
    )(arrived)


def prepare_kernel(
    owners, lengths_ref, request_ref, position_ref, own_hbm,
    near_ref, far_ref, valid_ref, own_ref, sem,
):
    copy = pltpu.make_async_copy(own_hbm, own_ref, sem)
    copy.start()
    steps, batch = position_ref.shape
    heads = CUT_HEADS
    count = own_ref.shape[1]
    group, owner = lax.axis_index("pre"), lax.axis_index("dec")
    row = lax.broadcasted_iota(jnp.int32, (heads, count), 1)
    bases = [((group ^ turn) * owners + owner) * count for turn in TURNS]

    def fill(b, carry):
        request = request_ref[b]
        start = jnp.int32(0)
        for r in range(lengths_ref.shape[0] - 1):
            start = start + jnp.where(request > r, lengths_ref[r], 0)
        for s in range(steps):
            stop = start + position_ref[s, b]
            at = pl.ds(pl.multiple_of((s * batch + b) * heads, heads), heads)
            seen = jnp.int32(0)
            for c, base in enumerate(bases):
                bias = jnp.where((row >= start - base) & (row < stop - base), 0.0, mask_value)
                if c < len(bases) - 1:
                    near_ref[at, c * count : (c + 1) * count] = bias
                else:
                    far_ref[at, :] = bias
                seen = seen + jnp.where((start < base + count) & (stop > base), 1, 0)
            valid_ref[at, :] = jnp.full((heads, 128), seen, jnp.int32)
        return carry

    lax.fori_loop(0, batch, fill, 0)
    copy.wait()


def prepare(owners, groups, lengths, row_request, step_position, own):
    rows = step_position.size * CUT_HEADS
    smem = pl.BlockSpec(memory_space=pltpu.SMEM)
    vmem = pl.BlockSpec(memory_space=pltpu.VMEM)
    return pl.pallas_call(
        functools.partial(prepare_kernel, owners),
        in_specs=[smem] * 3 + [pl.BlockSpec(memory_space=pl.ANY)],
        out_specs=[vmem] * 4,
        out_shape=[
            jax.ShapeDtypeStruct((rows, (groups - 1) * own.shape[1]), jnp.float32),
            jax.ShapeDtypeStruct((rows, own.shape[1]), jnp.float32),
            jax.ShapeDtypeStruct((rows, 128), jnp.int32),
            jax.ShapeDtypeStruct(own.shape, own.dtype),
        ],
        scratch_shapes=[pltpu.SemaphoreType.DMA(())],
        compiler_params=params(8),
        name="prepare",
    )(lengths, row_request, step_position, own)


def scores_of(latent_ref, rope_ref, cut, chunk_refs, bias_ref):
    items, _, heads, _ = latent_ref.shape
    rows = items * heads
    latent = latent_ref[:, cut].reshape(rows, LAT)
    rope = rope_ref[:, cut].reshape(rows, ROPE)
    scores = []
    for c, chunk_ref in enumerate(chunk_refs):
        count = chunk_ref.shape[1]
        s = jnp.dot(latent, chunk_ref[:LAT, :], preferred_element_type=jnp.float32)
        s += jnp.dot(rope, chunk_ref[LAT:, :], preferred_element_type=jnp.float32)
        scores.append(s + bias_ref[:, c * count : (c + 1) * count])
    return scores


def weigh(scores, peak, chunk_refs):
    weights = [jnp.exp2((s - peak) * (score_scale * log2_e)) for s in scores]
    total = jnp.sum(functools.reduce(jnp.add, weights), axis=1, keepdims=True)
    mixed = sum(
        lax.dot_general(
            p.astype(jnp.bfloat16),
            chunk_ref[:LAT, :],
            (((1,), (1,)), ((), ())),
            preferred_element_type=jnp.float32,
        )
        for p, chunk_ref in zip(weights, chunk_refs)
    )
    return total, mixed


def near_kernel(
    bias_ref, latent_ref, rope_ref, k0, k1, k2, w_hbm, mixed_ref, stat_ref, w_ref, sem
):
    copy = pltpu.make_async_copy(w_hbm, w_ref, sem)
    copy.start()
    chunk_refs = (k0, k1, k2)
    cuts, rows, _ = mixed_ref.shape
    lane = lax.broadcasted_iota(jnp.int32, (rows, 128), 1)

    def body(cut, carry):
        scores = scores_of(latent_ref, rope_ref, cut, chunk_refs, bias_ref)
        peak = jnp.max(functools.reduce(jnp.maximum, scores), axis=1, keepdims=True)
        total, mixed = weigh(scores, peak, chunk_refs)
        mixed_ref[cut] = mixed
        stat_ref[cut] = jnp.where(lane == 0, peak, total)
        return carry

    lax.fori_loop(0, cuts, body, 0, unroll=2)
    copy.wait()


def apart(value):
    rows, width = value.shape
    tiles = value.reshape(rows // 16, 2, 8, width)
    first, second = tiles[:, 0], tiles[:, 1]
    upper_part = lax.broadcasted_iota(jnp.int32, first.shape, 1) < 4
    low = jnp.where(upper_part, first, pltpu.roll(second, 4, 1))
    high = jnp.where(upper_part, pltpu.roll(first, 4, 1), second)
    return low.reshape(rows // 2, width), high.reshape(rows // 2, width)


def together(low, high):
    rows, width = low.shape
    low = low.reshape(rows // 8, 8, width)
    high = high.reshape(rows // 8, 8, width)
    upper_part = lax.broadcasted_iota(jnp.int32, low.shape, 1) < 4
    first = jnp.where(upper_part, low, pltpu.roll(high, 4, 1))
    second = jnp.where(upper_part, pltpu.roll(low, 4, 1), high)
    return jnp.stack([first, second], axis=1).reshape(2 * rows, width)


def far_kernel(
    bias_ref, valid_ref, latent_ref, rope_ref, k3, mixed_ref, stat_ref, w_ref,
    keep_ref, send_ref, out_ref,
):
    items, cuts, heads, _ = latent_ref.shape
    rows = items * heads
    all_heads = cuts * heads

    out_ref[:, all_heads:, :] = jnp.zeros((items, PAD, 128), jnp.float32)
    head = lax.broadcasted_iota(jnp.int32, (rows, 128), 0) % heads
    lane = lax.broadcasted_iota(jnp.int32, (rows, 128), 1)
    half_heads = heads // 2
    head_of_half = lax.broadcasted_iota(jnp.int32, (rows // 2, 128), 0) % half_heads

    def body(cut, carry):
        scores = scores_of(latent_ref, rope_ref, cut, (k3,), bias_ref)
        old_peak, old_total = stat_ref[cut, :, 0:1], stat_ref[cut, :, 1:2]
        peak = jnp.maximum(old_peak, jnp.max(scores[0], axis=1, keepdims=True))
        factor = jnp.exp2((old_peak - peak) * (score_scale * log2_e))
        total, mixed = weigh(scores, peak, (k3,))
        total += old_total * factor
        valid = valid_ref[:, 0:1] > 0
        inverse = jnp.where(valid, 1.0 / total, 0.0)
        mixed = mixed * inverse + mixed_ref[cut] * (factor * inverse)
        level = jnp.where(valid, peak * score_scale + jnp.log(total), mask_value)
        low, high = apart(mixed)
        pieces = []
        for first, part in ((0, low), (half_heads, high)):
            upper = part.astype(jnp.bfloat16)
            lower = (part - upper.astype(jnp.float32)).astype(jnp.bfloat16)
            both = jnp.concatenate([upper, lower], axis=0)
            piece = jnp.zeros((rows // 2, 128), jnp.float32)
            for h in range(0, half_heads, 2):
                at = cut * heads + first + h
                pair = jnp.concatenate([w_ref[at], w_ref[at + 1]], axis=1)
                y = jnp.dot(both, pair, preferred_element_type=jnp.float32)
                y = y[: rows // 2] + y[rows // 2 :]
                piece = jnp.where(head_of_half == h, y[:, :128], piece)
                piece = jnp.where(head_of_half == h + 1, y[:, 128:], piece)
            pieces.append(piece)
        result = together(*pieces)
        at = pl.multiple_of(cut * heads, heads)
        out_ref[:, pl.ds(at, heads), :] = result.reshape(items, heads, 128)
        lines = jnp.where(lane == head + at, level, 0.0).reshape(items, heads, 128)
        lines = jnp.sum(lines, axis=1, keepdims=True)
        out_ref[:, all_heads:, :] += jnp.broadcast_to(lines, (items, PAD, 128))
        return carry

    lax.fori_loop(0, cuts, body, 0, unroll=2)
    half = items // 2
    core = lax.axis_index("dec") & 1

    def hand(i, carry):
        keep_ref[i] = out_ref[core * half + half - 1 - i]
        send_ref[i] = out_ref[(1 - core) * half + half - 1 - i]
        return carry

    lax.fori_loop(0, half, hand, 0)


def attend(near_bias, far_bias, valid, latent, rope, chunks, w_up):
    items, heads, _ = latent.shape
    cuts = heads // CUT_HEADS
    rows = items * CUT_HEADS
    latent = latent.reshape(items, cuts, CUT_HEADS, -1)
    rope = rope.reshape(items, cuts, CUT_HEADS, -1)
    vmem = pl.BlockSpec(memory_space=pltpu.VMEM)
    mixed, stat, w_near = pl.pallas_call(
        near_kernel,
        in_specs=[vmem] * 6 + [pl.BlockSpec(memory_space=pl.ANY)],
        out_specs=[vmem] * 3,
        out_shape=[
            jax.ShapeDtypeStruct((cuts, rows, LAT), jnp.float32),
            jax.ShapeDtypeStruct((cuts, rows, 128), jnp.float32),
            jax.ShapeDtypeStruct(w_up.shape, w_up.dtype),
        ],
        scratch_shapes=[pltpu.SemaphoreType.DMA(())],
        compiler_params=params(42),
        name="attend_near",
    )(near_bias, latent, rope, *chunks[:3], w_up)
    out_shape = jax.ShapeDtypeStruct((items // 2, heads + PAD, 128), jnp.float32)
    return pl.pallas_call(
        far_kernel,
        in_specs=[vmem] * 8,
        out_specs=[vmem] * 2,
        out_shape=[out_shape] * 2,
        scratch_shapes=[pltpu.VMEM((items, heads + PAD, 128), jnp.float32)],
        compiler_params=params(20),
        name="attend_far",
    )(far_bias, valid, latent, rope, chunks[3], mixed, stat, w_near)


def merge_step(levels):
    peak = functools.reduce(jnp.maximum, levels)
    scales = [jnp.exp(level - peak) for level in levels]
    total = functools.reduce(jnp.add, scales)
    return [scale / total for scale in scales], peak + jnp.log(total)


def spread_columns(line, heads):
    shape = line.shape[:-2] + (heads, line.shape[-1])
    axis = len(shape) - 1
    lane = lax.broadcasted_iota(jnp.int32, shape, axis)
    row = lax.broadcasted_iota(jnp.int32, shape, axis - 1)
    return jnp.sum(jnp.where(lane == row, line, 0.0), axis=axis, keepdims=True)


def pair_kernel(mine_ref, other_ref, out_ref):
    items, depth, _ = mine_ref.shape
    heads = depth - PAD
    step = 4

    def body(k, carry):
        at = pl.ds(k * step, step)
        parts = [mine_ref[at], other_ref[at]]
        scales, level = merge_step([part[:, heads:, :] for part in parts])
        result = sum(
            part[:, :heads, :] * spread_columns(scale[:, 0:1, :], heads)
            for part, scale in zip(parts, scales)
        )
        out_ref[at, :heads, :] = result
        out_ref[at, heads:, :] = level
        return carry

    lax.fori_loop(0, items // step, body, 0)


def merge_pair(mine, other):
    vmem = pl.BlockSpec(memory_space=pltpu.VMEM)
    return pl.pallas_call(
        pair_kernel,
        in_specs=[vmem] * 2,
        out_specs=vmem,
        out_shape=jax.ShapeDtypeStruct(mine.shape, mine.dtype),
        compiler_params=params(4),
        name="merge_pair",
    )(mine, other)


def merge_kernel(parts_ref, out_ref, scale_ref):
    sources, depth, lanes = parts_ref.shape
    heads = depth - PAD
    scales, _ = merge_step([parts_ref[k, heads:, :] for k in range(sources)])
    for k in range(sources):
        scale_ref[k] = scales[k]

    def body(k, so_far):
        return so_far + parts_ref[k, :heads, :] * spread_columns(scale_ref[k][0:1, :], heads)

    result = lax.fori_loop(
        0, sources, body, jnp.zeros((heads, lanes), jnp.float32), unroll=4
    ).astype(out_ref.dtype)
    for copy in range(out_ref.shape[0]):
        out_ref[copy] = result


def merge(parts):
    sources, depth, lanes = parts.shape
    vmem = pl.BlockSpec(memory_space=pltpu.VMEM)
    return pl.pallas_call(
        merge_kernel,
        in_specs=[vmem],
        out_specs=vmem,
        out_shape=jax.ShapeDtypeStruct((sources, depth - PAD, lanes), jnp.bfloat16),
        scratch_shapes=[pltpu.VMEM((sources, PAD, lanes), jnp.float32)],
        compiler_params=params(4),
        name="merge",
    )(parts)


def finish_kernel(mine_ref, other_ref, p0, p1, p2, p3, out_ref, cache_hbm, wide_ref, sems):
    group = lax.axis_index("pre")
    copies = []
    for k, (turn, piece) in enumerate(zip(TURNS, (p0, p1, p2, p3))):
        rows = piece.shape[1]
        at = pl.multiple_of((group ^ turn) * rows, rows)
        copies.append(
            pltpu.make_async_copy(piece, cache_hbm.at[:, pl.ds(at, rows)], sems.at[k])
        )
    for copy in copies:
        copy.start()
    half, heads, lanes = mine_ref.shape
    core = lax.axis_index("dec") & 1

    def widen(k, carry):
        for place_at, ref in ((core, mine_ref), (1 - core, other_ref)):
            item = place_at * half + half - 1 - k
            at = pl.ds(pl.multiple_of(item * heads, heads), heads)
            wide_ref[at, :] = ref[k].astype(jnp.float32)
        return carry

    lax.fori_loop(0, half, widen, 0, unroll=4)

    def body(h, carry):
        piece = wide_ref[pl.ds(h, 2 * half, stride=heads), :]
        at = pl.multiple_of(h * lanes, lanes)
        out_ref[:, pl.ds(at, lanes)] = piece.astype(out_ref.dtype)
        return carry

    lax.fori_loop(0, heads, body, 0, unroll=4)
    for copy in copies:
        copy.wait()


def finish(mine, other, pieces):
    half, heads, lanes = mine.shape
    width, rows = pieces[0].shape
    vmem = pl.BlockSpec(memory_space=pltpu.VMEM)
    return pl.pallas_call(
        finish_kernel,
        in_specs=[vmem] * 6,
        out_specs=[vmem, pl.BlockSpec(memory_space=pl.ANY)],
        out_shape=[
            jax.ShapeDtypeStruct((2 * half, heads * lanes), mine.dtype),
            jax.ShapeDtypeStruct((width, rows * len(pieces)), pieces[0].dtype),
        ],
        scratch_shapes=[
            pltpu.VMEM((2 * half * heads, lanes), jnp.float32),
            pltpu.SemaphoreType.DMA((len(pieces),)),
        ],
        compiler_params=params(6),
        name="finish",
    )(mine, other, *pieces)


def exchange(piece, groups, turn):
    return lax.ppermute(piece, "pre", [(i, i ^ turn) for i in range(groups)])


def around(piece, groups, owners):
    core = lax.axis_index("dec") % 2
    first = exchange(piece, groups, 3)
    second = exchange(piece, groups, 1)
    forward = [
        (g * owners + d, (g ^ (1 if d % 2 == 0 else 3)) * owners + d)
        for g in range(groups)
        for d in range(owners)
    ]
    chosen = jnp.where(core == 0, first, second)
    far = lax.ppermute(chosen, ("pre", "dec"), forward)
    return [piece, first, second, far]


def per_device(
    hidden,
    w_down,
    kv_gain,
    query_latent,
    query_rope,
    w_up_value,
    request_rows,
    row_request,
    step_position,
    destination,
):
    groups = lax.axis_size("pre")
    owners = lax.axis_size("dec")
    steps, batch, heads, _ = query_latent.shape
    items = steps * batch
    plane = [[2 * k + core for k in reversed(range(SIDE * SIDE))] for core in range(2)]
    sibling = [(d, d ^ 1) for d in range(owners)]

    produced = produce(owners, request_rows, hidden, w_down.T, kv_gain)
    chunks = around(produced, groups, owners)

    exchanged = functools.partial(
        lax.all_to_all, axis_name="dec", split_axis=0, concat_axis=0, tiled=True
    )
    near_bias, far_bias, valid, chunks[0] = prepare(
        owners, groups, request_rows, row_request, step_position, produced
    )
    keep, send = attend(
        near_bias,
        far_bias,
        valid,
        query_latent.reshape(items, heads, -1),
        query_rope.reshape(items, heads, -1),
        chunks,
        w_up_value,
    )
    packed = pack(groups, owners, destination, produced)
    arrived = exchanged(packed, axis_index_groups=[list(reversed(range(owners)))])
    quarter = place(arrived, *produced.shape)
    pieces = [quarter] + [exchange(quarter, groups, turn) for turn in TURNS[1:]]

    parts = merge_pair(keep, lax.ppermute(send, "dec", sibling))
    result = merge(exchanged(parts, axis_index_groups=plane))
    result = exchanged(result, axis_index_groups=plane)
    result, kv_cache = finish(result, lax.ppermute(result, "dec", sibling), pieces)
    attention_out = result.reshape(steps, batch, -1)
    kv_cache = kv_cache.T
    return (attention_out, kv_cache)


def solution(mesh):
    return jax.shard_map(
        per_device,
        mesh=mesh,
        in_specs=(
            P(("pre", "dec"), None),
            P(),
            P(),
            P(None, None, "pre", None),
            P(None, None, "pre", None),
            P("pre", None, None),
            P(),
            P(),
            P(),
            P(),
        ),
        out_specs=(P(None, None, "pre"), P("dec", None)),
        check_vma=False,
    )
```

```python
import functools
import math

import jax
import jax.numpy as jnp
import numpy as np
from jax import lax
from jax.experimental import pallas as pl
from jax.experimental.pallas import tpu as pltpu
from jax.sharding import PartitionSpec as P

LAT = 512
ROPE = 64
MOST = 2
PAD = 8
SIDE = 4
TURNS = (0, 3, 1, 2)
CUT_HEADS = 8
DEPTH = 1792

score_scale = 0.07216878364870323
mask_value = -1e30
norm_eps = 1e-06
log2_e = 1.4426950408889634


def frequencies():
    half = ROPE // 2
    pair_index = np.arange(half, dtype=np.float64)
    frequency = np.exp(pair_index * (-2.0 * math.log(10000.0) / ROPE)).astype(np.float32)
    return np.tile(frequency[:, None], (1, 128))


WIDE = 640


def shift_of(count):
    assert count & (count - 1) == 0
    return count.bit_length() - 1


def params(megabytes):
    return pltpu.CompilerParams(vmem_limit_bytes=megabytes * 1024 * 1024)


def produce_kernel(
    groups, owners, lengths_hbm, dest_hbm, hidden_hbm, w_hbm, gain_hbm, freq_hbm,
    out_ref, packed_ref, hidden_ref, w_ref, acc_ref, lengths_ref, dest_ref, gain_ref, freq_ref,
    turn_ref, column_ref, rows_ref, count_ref, slot_ref, sems, small_sems,
):
    pieces, rows, depth = hidden_ref.shape
    half = ROPE // 2
    small = [
        pltpu.make_async_copy(source, target, small_sems.at[k])
        for k, (source, target) in enumerate(
            (
                (lengths_hbm, lengths_ref),
                (dest_hbm, dest_ref),
                (gain_hbm, gain_ref),
                (freq_hbm, freq_ref),
            )
        )
    ]

    def copies(k):
        columns = pl.ds(pl.multiple_of(k * depth, depth), depth)
        return (
            pltpu.make_async_copy(hidden_hbm.at[:, columns], hidden_ref.at[k], sems.at[0, k]),
            pltpu.make_async_copy(w_hbm.at[:, columns], w_ref.at[k], sems.at[1, k]),
        )

    def begin(k, carry):
        for copy in copies(k):
            copy.start()
        return carry

    for copy in small:
        copy.start()
    lax.fori_loop(0, pieces, begin, 0)
    acc_ref[...] = jnp.zeros_like(acc_ref)
    packed_ref[...] = jnp.full(packed_ref.shape, -1.0, packed_ref.dtype)
    for copy in small:
        copy.wait()
    group = lax.axis_index("pre")
    device = group * owners + lax.axis_index("dec")
    block_rows = packed_ref.shape[1]
    blocks = rows // block_rows

    def clear(owner, carry):
        count_ref[owner] = 0
        return carry

    def choose(b, carry):
        owner = lax.shift_right_logical(dest_ref[device * blocks + b], shift_of(groups * owners))
        rank = count_ref[owner]
        count_ref[owner] = rank + 1
        slot_ref[b] = (owners - 1 - owner) * MOST + rank
        return carry

    lax.fori_loop(0, owners, clear, 0)
    lax.fori_loop(0, blocks, choose, 0)
    row = device * rows + lax.broadcasted_iota(jnp.int32, (1, rows), 1)
    start = jnp.zeros((1, rows), jnp.int32)
    first_row = jnp.int32(0)
    for r in range(lengths_ref.shape[0] - 1):
        first_row = first_row + lengths_ref[r]
        start = jnp.where(row >= first_row, first_row, start)
    angles = freq_ref[:, 0:1] * (row - start).astype(jnp.float32)
    turn_ref[:half, :] = jnp.cos(angles)
    turn_ref[half:, :] = jnp.sin(angles)
    column_ref[...] = jnp.transpose(jnp.broadcast_to(gain_ref[...], (128, LAT)))

    def body(k, carry):
        for copy in copies(k):
            copy.wait()
        acc_ref[...] += lax.dot_general(
            w_ref[k],
            hidden_ref[k],
            (((1,), (1,)), ((), ())),
            preferred_element_type=jnp.float32,
        )
        return carry

    lax.fori_loop(0, pieces, body, 0)
    latent = acc_ref[:LAT, :]
    inverse_rms = lax.rsqrt(jnp.mean(latent * latent, axis=0, keepdims=True) + norm_eps)
    out_ref[:LAT, :] = (latent * inverse_rms * column_ref[:, 0:1]).astype(out_ref.dtype)
    cosine, sine = turn_ref[:half, :], turn_ref[half:, :]
    first = acc_ref[LAT : LAT + half, :]
    second = acc_ref[LAT + half :, :]
    turned = first * cosine - second * sine
    out_ref[LAT : LAT + half, :] = turned.astype(out_ref.dtype)
    turned = second * cosine + first * sine
    out_ref[LAT + half :, :] = turned.astype(out_ref.dtype)
    width = out_ref.shape[0]
    for at in range(0, width, 128):
        count = min(128, width - at)
        wide = out_ref[at : at + count, :].astype(jnp.float32)
        if count < 128:
            wide = jnp.concatenate([wide, jnp.zeros((128 - count, rows), jnp.float32)], axis=0)
        rows_ref[:, :, at : at + 128] = jnp.transpose(wide).reshape(blocks, block_rows, 128)
    lane = lax.broadcasted_iota(jnp.int32, (block_rows, WIDE), 1)

    def put(b, carry):
        place_at = (dest_ref[device * blocks + b] & (groups * owners - 1)) - group * owners
        block = jnp.where(lane < width, rows_ref[b], place_at.astype(jnp.float32))
        packed_ref[slot_ref[b]] = block.astype(packed_ref.dtype)
        return carry

    lax.fori_loop(0, blocks, put, 0, unroll=4)


def produce(groups, owners, lengths, destination, hidden, w_turned, gain):
    rows, width = hidden.shape
    row_width = w_turned.shape[0]
    pieces = width // DEPTH
    block_rows = rows // owners
    vmem = pl.BlockSpec(memory_space=pltpu.VMEM)
    return pl.pallas_call(
        functools.partial(produce_kernel, groups, owners),
        in_specs=[pl.BlockSpec(memory_space=pltpu.HBM)] * 6,
        out_specs=[vmem, vmem],
        out_shape=[
            jax.ShapeDtypeStruct((row_width, rows), jnp.bfloat16),
            jax.ShapeDtypeStruct((owners * MOST, block_rows, WIDE), jnp.bfloat16),
        ],
        scratch_shapes=[
            pltpu.VMEM((pieces, rows, DEPTH), jnp.bfloat16),
            pltpu.VMEM((pieces, row_width, DEPTH), jnp.bfloat16),
            pltpu.VMEM((row_width, rows), jnp.float32),
            pltpu.SMEM(lengths.shape, jnp.int32),
            pltpu.SMEM(destination.shape, jnp.int32),
            pltpu.VMEM((1, LAT), jnp.float32),
            pltpu.VMEM((ROPE // 2, 128), jnp.float32),
            pltpu.VMEM((ROPE, rows), jnp.float32),
            pltpu.VMEM((LAT, 128), jnp.float32),
            pltpu.VMEM((owners, block_rows, WIDE), jnp.float32),
            pltpu.SMEM((owners,), jnp.int32),
            pltpu.SMEM((owners,), jnp.int32),
            pltpu.SemaphoreType.DMA((2, pieces)),
            pltpu.SemaphoreType.DMA((4,)),
        ],
        name="produce",
    )(
        lengths,
        destination,
        hidden,
        w_turned,
        gain.reshape(1, -1),
        jnp.asarray(frequencies()),
    )


def place_kernel(arrived_ref, out_ref, rows_ref):
    blocks, block_rows, _ = arrived_ref.shape
    width, rows = out_ref.shape
    depth = 256
    part = depth // block_rows
    row = lax.broadcasted_iota(jnp.int32, (rows, depth), 0).astype(jnp.float32)
    lane = lax.broadcasted_iota(jnp.int32, (1, depth), 1)
    within = lax.rem(lane, block_rows).astype(jnp.float32)
    for k in range(blocks // part):
        source = arrived_ref[k * part : (k + 1) * part].astype(jnp.float32).reshape(depth, WIDE)
        slot = jnp.transpose(source[:, WIDE - 128 :])[127:128, :]
        select = jnp.where(row == slot * block_rows + within, 1.0, 0.0).astype(jnp.bfloat16)
        placed = jnp.dot(select, source.astype(jnp.bfloat16), preferred_element_type=jnp.float32)
        if k == 0:
            rows_ref[...] = placed
        else:
            rows_ref[...] += placed
    for at in range(0, width, 128):
        count = min(128, width - at)
        turned = jnp.transpose(rows_ref[:, at : at + 128])
        out_ref[at : at + count, :] = turned[:count].astype(out_ref.dtype)


def place(arrived, width, rows):
    vmem = pl.BlockSpec(memory_space=pltpu.VMEM)
    return pl.pallas_call(
        place_kernel,
        in_specs=[vmem],
        out_specs=vmem,
        out_shape=jax.ShapeDtypeStruct((width, rows), arrived.dtype),
        scratch_shapes=[pltpu.VMEM((rows, WIDE), jnp.float32)],
        compiler_params=params(8),
        name="place",
    )(arrived)


def prepare_kernel(
    owners, lengths_ref, request_ref, position_ref, own_hbm,
    near_ref, far_ref, valid_ref, own_ref, sem,
):
    copy = pltpu.make_async_copy(own_hbm, own_ref, sem)
    copy.start()
    steps, batch = position_ref.shape
    heads = CUT_HEADS
    count = own_ref.shape[1]
    group, owner = lax.axis_index("pre"), lax.axis_index("dec")
    row = lax.broadcasted_iota(jnp.int32, (heads, count), 1)
    bases = [((group ^ turn) * owners + owner) * count for turn in TURNS]

    def fill(b, carry):
        request = request_ref[b]
        start = jnp.int32(0)
        for r in range(lengths_ref.shape[0] - 1):
            start = start + jnp.where(request > r, lengths_ref[r], 0)
        for s in range(steps):
            stop = start + position_ref[s, b]
            at = pl.ds(pl.multiple_of((s * batch + b) * heads, heads), heads)
            seen = jnp.int32(0)
            for c, base in enumerate(bases):
                bias = jnp.where((row >= start - base) & (row < stop - base), 0.0, mask_value)
                if c < len(bases) - 1:
                    near_ref[at, c * count : (c + 1) * count] = bias
                else:
                    far_ref[at, :] = bias
                seen = seen + jnp.where((start < base + count) & (stop > base), 1, 0)
            valid_ref[at, :] = jnp.full((heads, 128), seen, jnp.int32)
        return carry

    lax.fori_loop(0, batch, fill, 0)
    copy.wait()


def prepare(owners, groups, lengths, row_request, step_position, own):
    rows = step_position.size * CUT_HEADS
    smem = pl.BlockSpec(memory_space=pltpu.SMEM)
    vmem = pl.BlockSpec(memory_space=pltpu.VMEM)
    return pl.pallas_call(
        functools.partial(prepare_kernel, owners),
        in_specs=[smem] * 3 + [pl.BlockSpec(memory_space=pl.ANY)],
        out_specs=[vmem] * 4,
        out_shape=[
            jax.ShapeDtypeStruct((rows, (groups - 1) * own.shape[1]), jnp.float32),
            jax.ShapeDtypeStruct((rows, own.shape[1]), jnp.float32),
            jax.ShapeDtypeStruct((rows, 128), jnp.int32),
            jax.ShapeDtypeStruct(own.shape, own.dtype),
        ],
        scratch_shapes=[pltpu.SemaphoreType.DMA(())],
        compiler_params=params(8),
        name="prepare",
    )(lengths, row_request, step_position, own)


def scores_of(latent_ref, rope_ref, cut, chunk_refs, bias_ref):
    items, _, heads, _ = latent_ref.shape
    rows = items * heads
    latent = latent_ref[:, cut].reshape(rows, LAT)
    rope = rope_ref[:, cut].reshape(rows, ROPE)
    scores = []
    for c, chunk_ref in enumerate(chunk_refs):
        count = chunk_ref.shape[1]
        s = jnp.dot(latent, chunk_ref[:LAT, :], preferred_element_type=jnp.float32)
        s += jnp.dot(rope, chunk_ref[LAT:, :], preferred_element_type=jnp.float32)
        scores.append(s + bias_ref[:, c * count : (c + 1) * count])
    return scores


def weigh(scores, peak, chunk_refs):
    weights = [jnp.exp2((s - peak) * (score_scale * log2_e)) for s in scores]
    total = jnp.sum(functools.reduce(jnp.add, weights), axis=1, keepdims=True)
    mixed = sum(
        lax.dot_general(
            p.astype(jnp.bfloat16),
            chunk_ref[:LAT, :],
            (((1,), (1,)), ((), ())),
            preferred_element_type=jnp.float32,
        )
        for p, chunk_ref in zip(weights, chunk_refs)
    )
    return total, mixed


def near_kernel(
    bias_ref, latent_ref, rope_ref, k0, k1, k2, w_hbm, mixed_ref, stat_ref, w_ref, sem
):
    copy = pltpu.make_async_copy(w_hbm, w_ref, sem)
    copy.start()
    chunk_refs = (k0, k1, k2)
    cuts, rows, _ = mixed_ref.shape
    lane = lax.broadcasted_iota(jnp.int32, (rows, 128), 1)

    def body(cut, carry):
        scores = scores_of(latent_ref, rope_ref, cut, chunk_refs, bias_ref)
        peak = jnp.max(functools.reduce(jnp.maximum, scores), axis=1, keepdims=True)
        total, mixed = weigh(scores, peak, chunk_refs)
        mixed_ref[cut] = mixed
        stat_ref[cut] = jnp.where(lane == 0, peak, total)
        return carry

    lax.fori_loop(0, cuts, body, 0, unroll=2)
    copy.wait()


def apart(value):
    rows, width = value.shape
    tiles = value.reshape(rows // 16, 2, 8, width)
    first, second = tiles[:, 0], tiles[:, 1]
    upper_part = lax.broadcasted_iota(jnp.int32, first.shape, 1) < 4
    low = jnp.where(upper_part, first, pltpu.roll(second, 4, 1))
    high = jnp.where(upper_part, pltpu.roll(first, 4, 1), second)
    return low.reshape(rows // 2, width), high.reshape(rows // 2, width)


def together(low, high):
    rows, width = low.shape
    low = low.reshape(rows // 8, 8, width)
    high = high.reshape(rows // 8, 8, width)
    upper_part = lax.broadcasted_iota(jnp.int32, low.shape, 1) < 4
    first = jnp.where(upper_part, low, pltpu.roll(high, 4, 1))
    second = jnp.where(upper_part, pltpu.roll(low, 4, 1), high)
    return jnp.stack([first, second], axis=1).reshape(2 * rows, width)


def far_kernel(
    bias_ref, valid_ref, latent_ref, rope_ref, k3, mixed_ref, stat_ref, w_ref,
    keep_ref, send_ref, out_ref,
):
    items, cuts, heads, _ = latent_ref.shape
    rows = items * heads
    all_heads = cuts * heads

    out_ref[:, all_heads:, :] = jnp.zeros((items, PAD, 128), jnp.float32)
    head = lax.broadcasted_iota(jnp.int32, (rows, 128), 0) % heads
    lane = lax.broadcasted_iota(jnp.int32, (rows, 128), 1)
    half_heads = heads // 2
    head_of_half = lax.broadcasted_iota(jnp.int32, (rows // 2, 128), 0) % half_heads

    def body(cut, carry):
        scores = scores_of(latent_ref, rope_ref, cut, (k3,), bias_ref)
        old_peak, old_total = stat_ref[cut, :, 0:1], stat_ref[cut, :, 1:2]
        peak = jnp.maximum(old_peak, jnp.max(scores[0], axis=1, keepdims=True))
        factor = jnp.exp2((old_peak - peak) * (score_scale * log2_e))
        total, mixed = weigh(scores, peak, (k3,))
        total += old_total * factor
        valid = valid_ref[:, 0:1] > 0
        inverse = jnp.where(valid, 1.0 / total, 0.0)
        mixed = mixed * inverse + mixed_ref[cut] * (factor * inverse)
        level = jnp.where(valid, peak * score_scale + jnp.log(total), mask_value)
        low, high = apart(mixed)
        pieces = []
        for first, part in ((0, low), (half_heads, high)):
            upper = part.astype(jnp.bfloat16)
            lower = (part - upper.astype(jnp.float32)).astype(jnp.bfloat16)
            both = jnp.concatenate([upper, lower], axis=0)
            piece = jnp.zeros((rows // 2, 128), jnp.float32)
            for h in range(0, half_heads, 2):
                at = cut * heads + first + h
                pair = jnp.concatenate([w_ref[at], w_ref[at + 1]], axis=1)
                y = jnp.dot(both, pair, preferred_element_type=jnp.float32)
                y = y[: rows // 2] + y[rows // 2 :]
                piece = jnp.where(head_of_half == h, y[:, :128], piece)
                piece = jnp.where(head_of_half == h + 1, y[:, 128:], piece)
            pieces.append(piece)
        result = together(*pieces)
        at = pl.multiple_of(cut * heads, heads)
        out_ref[:, pl.ds(at, heads), :] = result.reshape(items, heads, 128)
        lines = jnp.where(lane == head + at, level, 0.0).reshape(items, heads, 128)
        lines = jnp.sum(lines, axis=1, keepdims=True)
        out_ref[:, all_heads:, :] += jnp.broadcast_to(lines, (items, PAD, 128))
        return carry

    lax.fori_loop(0, cuts, body, 0, unroll=2)
    half = items // 2
    core = lax.axis_index("dec") & 1

    def hand(i, carry):
        keep_ref[i] = out_ref[core * half + half - 1 - i]
        send_ref[i] = out_ref[(1 - core) * half + half - 1 - i]
        return carry

    lax.fori_loop(0, half, hand, 0)


def attend(near_bias, far_bias, valid, latent, rope, chunks, w_up):
    items, heads, _ = latent.shape
    cuts = heads // CUT_HEADS
    rows = items * CUT_HEADS
    latent = latent.reshape(items, cuts, CUT_HEADS, -1)
    rope = rope.reshape(items, cuts, CUT_HEADS, -1)
    vmem = pl.BlockSpec(memory_space=pltpu.VMEM)
    mixed, stat, w_near = pl.pallas_call(
        near_kernel,
        in_specs=[vmem] * 6 + [pl.BlockSpec(memory_space=pl.ANY)],
        out_specs=[vmem] * 3,
        out_shape=[
            jax.ShapeDtypeStruct((cuts, rows, LAT), jnp.float32),
            jax.ShapeDtypeStruct((cuts, rows, 128), jnp.float32),
            jax.ShapeDtypeStruct(w_up.shape, w_up.dtype),
        ],
        scratch_shapes=[pltpu.SemaphoreType.DMA(())],
        compiler_params=params(42),
        name="attend_near",
    )(near_bias, latent, rope, *chunks[:3], w_up)
    out_shape = jax.ShapeDtypeStruct((items // 2, heads + PAD, 128), jnp.float32)
    return pl.pallas_call(
        far_kernel,
        in_specs=[vmem] * 8,
        out_specs=[vmem] * 2,
        out_shape=[out_shape] * 2,
        scratch_shapes=[pltpu.VMEM((items, heads + PAD, 128), jnp.float32)],
        compiler_params=params(20),
        name="attend_far",
    )(far_bias, valid, latent, rope, chunks[3], mixed, stat, w_near)


def merge_step(levels):
    peak = functools.reduce(jnp.maximum, levels)
    scales = [jnp.exp(level - peak) for level in levels]
    total = functools.reduce(jnp.add, scales)
    return [scale / total for scale in scales], peak + jnp.log(total)


def spread_columns(line, heads):
    shape = line.shape[:-2] + (heads, line.shape[-1])
    axis = len(shape) - 1
    lane = lax.broadcasted_iota(jnp.int32, shape, axis)
    row = lax.broadcasted_iota(jnp.int32, shape, axis - 1)
    return jnp.sum(jnp.where(lane == row, line, 0.0), axis=axis, keepdims=True)


def pair_kernel(mine_ref, other_ref, out_ref):
    items, depth, _ = mine_ref.shape
    heads = depth - PAD
    step = 4

    def body(k, carry):
        at = pl.ds(k * step, step)
        parts = [mine_ref[at], other_ref[at]]
        scales, level = merge_step([part[:, heads:, :] for part in parts])
        result = sum(
            part[:, :heads, :] * spread_columns(scale[:, 0:1, :], heads)
            for part, scale in zip(parts, scales)
        )
        out_ref[at, :heads, :] = result
        out_ref[at, heads:, :] = level
        return carry

    lax.fori_loop(0, items // step, body, 0)


def merge_pair(mine, other):
    vmem = pl.BlockSpec(memory_space=pltpu.VMEM)
    return pl.pallas_call(
        pair_kernel,
        in_specs=[vmem] * 2,
        out_specs=vmem,
        out_shape=jax.ShapeDtypeStruct(mine.shape, mine.dtype),
        compiler_params=params(4),
        name="merge_pair",
    )(mine, other)


def merge_kernel(parts_ref, out_ref, scale_ref):
    sources, depth, lanes = parts_ref.shape
    heads = depth - PAD
    scales, _ = merge_step([parts_ref[k, heads:, :] for k in range(sources)])
    for k in range(sources):
        scale_ref[k] = scales[k]

    def body(k, so_far):
        return so_far + parts_ref[k, :heads, :] * spread_columns(scale_ref[k][0:1, :], heads)

    result = lax.fori_loop(
        0, sources, body, jnp.zeros((heads, lanes), jnp.float32), unroll=4
    ).astype(out_ref.dtype)
    for copy in range(out_ref.shape[0]):
        out_ref[copy] = result


def merge(parts):
    sources, depth, lanes = parts.shape
    vmem = pl.BlockSpec(memory_space=pltpu.VMEM)
    return pl.pallas_call(
        merge_kernel,
        in_specs=[vmem],
        out_specs=vmem,
        out_shape=jax.ShapeDtypeStruct((sources, depth - PAD, lanes), jnp.bfloat16),
        scratch_shapes=[pltpu.VMEM((sources, PAD, lanes), jnp.float32)],
        compiler_params=params(4),
        name="merge",
    )(parts)


def finish_kernel(mine_ref, other_ref, p0, p1, p2, p3, out_ref, cache_hbm, wide_ref, sems):
    group = lax.axis_index("pre")
    copies = []
    for k, (turn, piece) in enumerate(zip(TURNS, (p0, p1, p2, p3))):
        rows = piece.shape[1]
        at = pl.multiple_of((group ^ turn) * rows, rows)
        copies.append(
            pltpu.make_async_copy(piece, cache_hbm.at[:, pl.ds(at, rows)], sems.at[k])
        )
    for copy in copies:
        copy.start()
    half, heads, lanes = mine_ref.shape
    core = lax.axis_index("dec") & 1

    def widen(k, carry):
        for place_at, ref in ((core, mine_ref), (1 - core, other_ref)):
            item = place_at * half + half - 1 - k
            at = pl.ds(pl.multiple_of(item * heads, heads), heads)
            wide_ref[at, :] = ref[k].astype(jnp.float32)
        return carry

    lax.fori_loop(0, half, widen, 0, unroll=4)

    def body(h, carry):
        piece = wide_ref[pl.ds(h, 2 * half, stride=heads), :]
        at = pl.multiple_of(h * lanes, lanes)
        out_ref[:, pl.ds(at, lanes)] = piece.astype(out_ref.dtype)
        return carry

    lax.fori_loop(0, heads, body, 0, unroll=4)
    for copy in copies:
        copy.wait()


def finish(mine, other, pieces):
    half, heads, lanes = mine.shape
    width, rows = pieces[0].shape
    vmem = pl.BlockSpec(memory_space=pltpu.VMEM)
    return pl.pallas_call(
        finish_kernel,
        in_specs=[vmem] * 6,
        out_specs=[vmem, pl.BlockSpec(memory_space=pl.ANY)],
        out_shape=[
            jax.ShapeDtypeStruct((2 * half, heads * lanes), mine.dtype),
            jax.ShapeDtypeStruct((width, rows * len(pieces)), pieces[0].dtype),
        ],
        scratch_shapes=[
            pltpu.VMEM((2 * half * heads, lanes), jnp.float32),
            pltpu.SemaphoreType.DMA((len(pieces),)),
        ],
        compiler_params=params(6),
        name="finish",
    )(mine, other, *pieces)


def exchange(piece, groups, turn):
    return lax.ppermute(piece, "pre", [(i, i ^ turn) for i in range(groups)])


def around(piece, groups, owners, gate):
    core = lax.axis_index("dec") % 2
    first = exchange(piece, groups, 3)
    second = exchange(piece, groups, 1)
    early_first, early_second, _ = lax.optimization_barrier((first, second, gate))
    forward = [
        (g * owners + d, (g ^ (1 if d % 2 == 0 else 3)) * owners + d)
        for g in range(groups)
        for d in range(owners)
    ]
    chosen = jnp.where(core == 0, early_first, early_second)
    far = lax.ppermute(chosen, ("pre", "dec"), forward)
    return [piece, first, second, far]


def per_device(
    hidden,
    w_down,
    kv_gain,
    query_latent,
    query_rope,
    w_up_value,
    request_rows,
    row_request,
    step_position,
    destination,
):
    groups = lax.axis_size("pre")
    owners = lax.axis_size("dec")
    steps, batch, heads, _ = query_latent.shape
    items = steps * batch
    plane = [[2 * k + core for k in reversed(range(SIDE * SIDE))] for core in range(2)]
    sibling = [(d, d ^ 1) for d in range(owners)]

    produced, packed = produce(
        groups, owners, request_rows, destination, hidden, w_down.T, kv_gain
    )
    near_bias, far_bias, valid, own = prepare(
        owners, groups, request_rows, row_request, step_position, produced
    )
    chunks = around(produced, groups, owners, valid)
    chunks[0] = own

    exchanged = functools.partial(
        lax.all_to_all, axis_name="dec", split_axis=0, concat_axis=0, tiled=True
    )
    keep, send = attend(
        near_bias,
        far_bias,
        valid,
        query_latent.reshape(items, heads, -1),
        query_rope.reshape(items, heads, -1),
        chunks,
        w_up_value,
    )
    arrived = exchanged(packed, axis_index_groups=[list(reversed(range(owners)))])
    quarter = place(arrived, *produced.shape)
    pieces = [quarter] + [exchange(quarter, groups, turn) for turn in TURNS[1:]]

    parts = merge_pair(keep, lax.ppermute(send, "dec", sibling))
    result = merge(exchanged(parts, axis_index_groups=plane))
    result = exchanged(result, axis_index_groups=plane)
    result, kv_cache = finish(result, lax.ppermute(result, "dec", sibling), pieces)
    attention_out = result.reshape(steps, batch, -1)
    kv_cache = kv_cache.T
    return (attention_out, kv_cache)


def solution(mesh):
    return jax.shard_map(
        per_device,
        mesh=mesh,
        in_specs=(
            P(("pre", "dec"), None),
            P(),
            P(),
            P(None, None, "pre", None),
            P(None, None, "pre", None),
            P("pre", None, None),
            P(),
            P(),
            P(),
            P(),
        ),
        out_specs=(P(None, None, "pre"), P("dec", None)),
        check_vma=False,
    )
```

```python
import functools
import math

import jax
import jax.numpy as jnp
import numpy as np
from jax import lax
from jax.experimental import pallas as pl
from jax.experimental.pallas import tpu as pltpu
from jax.sharding import PartitionSpec as P

LAT = 512
ROPE = 64
MOST = 2
PAD = 8
SIDE = 4
TURNS = (0, 3, 1, 2)
CUT_HEADS = 8
DEPTH = 1792

score_scale = 0.07216878364870323
mask_value = -1e30
norm_eps = 1e-06
log2_e = 1.4426950408889634


def frequencies():
    half = ROPE // 2
    pair_index = np.arange(half, dtype=np.float64)
    frequency = np.exp(pair_index * (-2.0 * math.log(10000.0) / ROPE)).astype(np.float32)
    return np.tile(frequency[:, None], (1, 128))


WIDE = 640


def shift_of(count):
    assert count & (count - 1) == 0
    return count.bit_length() - 1


def params(megabytes):
    return pltpu.CompilerParams(vmem_limit_bytes=megabytes * 1024 * 1024)


def produce_kernel(
    groups, owners, lengths_hbm, dest_hbm, hidden_hbm, w_hbm, gain_hbm, freq_hbm,
    out_ref, packed_ref, hidden_ref, w_ref, acc_ref, lengths_ref, dest_ref, gain_ref, freq_ref,
    turn_ref, column_ref, rows_ref, count_ref, slot_ref, sems, small_sems,
):
    pieces, rows, depth = hidden_ref.shape
    half = ROPE // 2
    small = [
        pltpu.make_async_copy(source, target, small_sems.at[k])
        for k, (source, target) in enumerate(
            (
                (lengths_hbm, lengths_ref),
                (dest_hbm, dest_ref),
                (gain_hbm, gain_ref),
                (freq_hbm, freq_ref),
            )
        )
    ]

    def copies(k):
        columns = pl.ds(pl.multiple_of(k * depth, depth), depth)
        return (
            pltpu.make_async_copy(hidden_hbm.at[:, columns], hidden_ref.at[k], sems.at[0, k]),
            pltpu.make_async_copy(w_hbm.at[:, columns], w_ref.at[k], sems.at[1, k]),
        )

    def begin(k, carry):
        for copy in copies(k):
            copy.start()
        return carry

    for copy in small:
        copy.start()
    lax.fori_loop(0, pieces, begin, 0)
    acc_ref[...] = jnp.zeros_like(acc_ref)
    packed_ref[...] = jnp.full(packed_ref.shape, -1.0, packed_ref.dtype)
    for copy in small:
        copy.wait()
    group = lax.axis_index("pre")
    device = group * owners + lax.axis_index("dec")
    block_rows = packed_ref.shape[1]
    blocks = rows // block_rows

    def clear(owner, carry):
        count_ref[owner] = 0
        return carry

    def choose(b, carry):
        owner = lax.shift_right_logical(dest_ref[device * blocks + b], shift_of(groups * owners))
        rank = count_ref[owner]
        count_ref[owner] = rank + 1
        slot_ref[b] = (owners - 1 - owner) * MOST + rank
        return carry

    lax.fori_loop(0, owners, clear, 0)
    lax.fori_loop(0, blocks, choose, 0)
    row = device * rows + lax.broadcasted_iota(jnp.int32, (1, rows), 1)
    start = jnp.zeros((1, rows), jnp.int32)
    first_row = jnp.int32(0)
    for r in range(lengths_ref.shape[0] - 1):
        first_row = first_row + lengths_ref[r]
        start = jnp.where(row >= first_row, first_row, start)
    angles = freq_ref[:, 0:1] * (row - start).astype(jnp.float32)
    turn_ref[:half, :] = jnp.cos(angles)
    turn_ref[half:, :] = jnp.sin(angles)
    column_ref[...] = jnp.transpose(jnp.broadcast_to(gain_ref[...], (128, LAT)))

    def body(k, carry):
        for copy in copies(k):
            copy.wait()
        acc_ref[...] += lax.dot_general(
            w_ref[k],
            hidden_ref[k],
            (((1,), (1,)), ((), ())),
            preferred_element_type=jnp.float32,
        )
        return carry

    lax.fori_loop(0, pieces, body, 0)
    latent = acc_ref[:LAT, :]
    inverse_rms = lax.rsqrt(jnp.mean(latent * latent, axis=0, keepdims=True) + norm_eps)
    out_ref[:LAT, :] = (latent * inverse_rms * column_ref[:, 0:1]).astype(out_ref.dtype)
    cosine, sine = turn_ref[:half, :], turn_ref[half:, :]
    first = acc_ref[LAT : LAT + half, :]
    second = acc_ref[LAT + half :, :]
    turned = first * cosine - second * sine
    out_ref[LAT : LAT + half, :] = turned.astype(out_ref.dtype)
    turned = second * cosine + first * sine
    out_ref[LAT + half :, :] = turned.astype(out_ref.dtype)
    width = out_ref.shape[0]
    for at in range(0, width, 128):
        count = min(128, width - at)
        wide = out_ref[at : at + count, :].astype(jnp.float32)
        if count < 128:
            wide = jnp.concatenate([wide, jnp.zeros((128 - count, rows), jnp.float32)], axis=0)
        rows_ref[:, :, at : at + 128] = jnp.transpose(wide).reshape(blocks, block_rows, 128)
    lane = lax.broadcasted_iota(jnp.int32, (block_rows, WIDE), 1)

    def put(b, carry):
        place_at = (dest_ref[device * blocks + b] & (groups * owners - 1)) - group * owners
        block = jnp.where(lane < width, rows_ref[b], place_at.astype(jnp.float32))
        packed_ref[slot_ref[b]] = block.astype(packed_ref.dtype)
        return carry

    lax.fori_loop(0, blocks, put, 0, unroll=4)


def produce(groups, owners, lengths, destination, hidden, w_turned, gain):
    rows, width = hidden.shape
    row_width = w_turned.shape[0]
    pieces = width // DEPTH
    block_rows = rows // owners
    vmem = pl.BlockSpec(memory_space=pltpu.VMEM)
    return pl.pallas_call(
        functools.partial(produce_kernel, groups, owners),
        in_specs=[pl.BlockSpec(memory_space=pltpu.HBM)] * 6,
        out_specs=[vmem, vmem],
        out_shape=[
            jax.ShapeDtypeStruct((row_width, rows), jnp.bfloat16),
            jax.ShapeDtypeStruct((owners * MOST, block_rows, WIDE), jnp.bfloat16),
        ],
        scratch_shapes=[
            pltpu.VMEM((pieces, rows, DEPTH), jnp.bfloat16),
            pltpu.VMEM((pieces, row_width, DEPTH), jnp.bfloat16),
            pltpu.VMEM((row_width, rows), jnp.float32),
            pltpu.SMEM(lengths.shape, jnp.int32),
            pltpu.SMEM(destination.shape, jnp.int32),
            pltpu.VMEM((1, LAT), jnp.float32),
            pltpu.VMEM((ROPE // 2, 128), jnp.float32),
            pltpu.VMEM((ROPE, rows), jnp.float32),
            pltpu.VMEM((LAT, 128), jnp.float32),
            pltpu.VMEM((owners, block_rows, WIDE), jnp.float32),
            pltpu.SMEM((owners,), jnp.int32),
            pltpu.SMEM((owners,), jnp.int32),
            pltpu.SemaphoreType.DMA((2, pieces)),
            pltpu.SemaphoreType.DMA((4,)),
        ],
        name="produce",
    )(
        lengths,
        destination,
        hidden,
        w_turned,
        gain.reshape(1, -1),
        jnp.asarray(frequencies()),
    )


def place_kernel(arrived_ref, out_ref, rows_ref):
    blocks, block_rows, _ = arrived_ref.shape
    width, rows = out_ref.shape
    depth = 256
    part = depth // block_rows
    row = lax.broadcasted_iota(jnp.int32, (rows, depth), 0).astype(jnp.float32)
    lane = lax.broadcasted_iota(jnp.int32, (1, depth), 1)
    within = lax.rem(lane, block_rows).astype(jnp.float32)
    for k in range(blocks // part):
        source = arrived_ref[k * part : (k + 1) * part].astype(jnp.float32).reshape(depth, WIDE)
        slot = jnp.transpose(source[:, WIDE - 128 :])[127:128, :]
        select = jnp.where(row == slot * block_rows + within, 1.0, 0.0).astype(jnp.bfloat16)
        placed = jnp.dot(select, source.astype(jnp.bfloat16), preferred_element_type=jnp.float32)
        if k == 0:
            rows_ref[...] = placed
        else:
            rows_ref[...] += placed
    for at in range(0, width, 128):
        count = min(128, width - at)
        turned = jnp.transpose(rows_ref[:, at : at + 128])
        out_ref[at : at + count, :] = turned[:count].astype(out_ref.dtype)


def place(arrived, width, rows):
    vmem = pl.BlockSpec(memory_space=pltpu.VMEM)
    return pl.pallas_call(
        place_kernel,
        in_specs=[vmem],
        out_specs=vmem,
        out_shape=jax.ShapeDtypeStruct((width, rows), arrived.dtype),
        scratch_shapes=[pltpu.VMEM((rows, WIDE), jnp.float32)],
        compiler_params=params(8),
        name="place",
    )(arrived)


def prepare_kernel(
    owners, lengths_ref, request_ref, position_ref, own_hbm,
    near_ref, far_ref, valid_ref, own_ref, sem,
):
    copy = pltpu.make_async_copy(own_hbm, own_ref, sem)
    copy.start()
    steps, batch = position_ref.shape
    heads = CUT_HEADS
    count = own_ref.shape[1]
    group, owner = lax.axis_index("pre"), lax.axis_index("dec")
    row = lax.broadcasted_iota(jnp.int32, (heads, count), 1)
    bases = [((group ^ turn) * owners + owner) * count for turn in TURNS]

    def fill(b, carry):
        request = request_ref[b]
        start = jnp.int32(0)
        for r in range(lengths_ref.shape[0] - 1):
            start = start + jnp.where(request > r, lengths_ref[r], 0)
        for s in range(steps):
            stop = start + position_ref[s, b]
            at = pl.ds(pl.multiple_of((s * batch + b) * heads, heads), heads)
            seen = jnp.int32(0)
            for c, base in enumerate(bases):
                bias = jnp.where((row >= start - base) & (row < stop - base), 0.0, mask_value)
                if c < len(bases) - 1:
                    near_ref[at, c * count : (c + 1) * count] = bias
                else:
                    far_ref[at, :] = bias
                seen = seen + jnp.where((start < base + count) & (stop > base), 1, 0)
            valid_ref[at, :] = jnp.full((heads, 128), seen, jnp.int32)
        return carry

    lax.fori_loop(0, batch, fill, 0)
    copy.wait()


def prepare(owners, groups, lengths, row_request, step_position, own):
    rows = step_position.size * CUT_HEADS
    smem = pl.BlockSpec(memory_space=pltpu.SMEM)
    vmem = pl.BlockSpec(memory_space=pltpu.VMEM)
    return pl.pallas_call(
        functools.partial(prepare_kernel, owners),
        in_specs=[smem] * 3 + [pl.BlockSpec(memory_space=pl.ANY)],
        out_specs=[vmem] * 4,
        out_shape=[
            jax.ShapeDtypeStruct((rows, (groups - 1) * own.shape[1]), jnp.float32),
            jax.ShapeDtypeStruct((rows, own.shape[1]), jnp.float32),
            jax.ShapeDtypeStruct((rows, 128), jnp.int32),
            jax.ShapeDtypeStruct(own.shape, own.dtype),
        ],
        scratch_shapes=[pltpu.SemaphoreType.DMA(())],
        compiler_params=params(8),
        name="prepare",
    )(lengths, row_request, step_position, own)


def scores_of(latent_ref, rope_ref, cut, chunk_refs, bias_ref):
    items, _, heads, _ = latent_ref.shape
    rows = items * heads
    latent = latent_ref[:, cut].reshape(rows, LAT)
    rope = rope_ref[:, cut].reshape(rows, ROPE)
    scores = []
    for c, chunk_ref in enumerate(chunk_refs):
        count = chunk_ref.shape[1]
        s = jnp.dot(latent, chunk_ref[:LAT, :], preferred_element_type=jnp.float32)
        s += jnp.dot(rope, chunk_ref[LAT:, :], preferred_element_type=jnp.float32)
        scores.append(s + bias_ref[:, c * count : (c + 1) * count])
    return scores


def weigh(scores, peak, chunk_refs):
    weights = [jnp.exp2((s - peak) * (score_scale * log2_e)) for s in scores]
    total = jnp.sum(functools.reduce(jnp.add, weights), axis=1, keepdims=True)
    mixed = sum(
        lax.dot_general(
            p.astype(jnp.bfloat16),
            chunk_ref[:LAT, :],
            (((1,), (1,)), ((), ())),
            preferred_element_type=jnp.float32,
        )
        for p, chunk_ref in zip(weights, chunk_refs)
    )
    return total, mixed


def near_kernel(
    bias_ref, latent_ref, rope_ref, k0, k1, k2, w_hbm, mixed_ref, stat_ref, w_ref, sem
):
    copy = pltpu.make_async_copy(w_hbm, w_ref, sem)
    copy.start()
    chunk_refs = (k0, k1, k2)
    cuts, rows, _ = mixed_ref.shape
    lane = lax.broadcasted_iota(jnp.int32, (rows, 128), 1)

    def body(cut, carry):
        scores = scores_of(latent_ref, rope_ref, cut, chunk_refs, bias_ref)
        peak = jnp.max(functools.reduce(jnp.maximum, scores), axis=1, keepdims=True)
        total, mixed = weigh(scores, peak, chunk_refs)
        mixed_ref[cut] = mixed
        stat_ref[cut] = jnp.where(lane == 0, peak, total)
        return carry

    lax.fori_loop(0, cuts, body, 0, unroll=2)
    copy.wait()


def apart(value):
    rows, width = value.shape
    tiles = value.reshape(rows // 16, 2, 8, width)
    first, second = tiles[:, 0], tiles[:, 1]
    upper_part = lax.broadcasted_iota(jnp.int32, first.shape, 1) < 4
    low = jnp.where(upper_part, first, pltpu.roll(second, 4, 1))
    high = jnp.where(upper_part, pltpu.roll(first, 4, 1), second)
    return low.reshape(rows // 2, width), high.reshape(rows // 2, width)


def together(low, high):
    rows, width = low.shape
    low = low.reshape(rows // 8, 8, width)
    high = high.reshape(rows // 8, 8, width)
    upper_part = lax.broadcasted_iota(jnp.int32, low.shape, 1) < 4
    first = jnp.where(upper_part, low, pltpu.roll(high, 4, 1))
    second = jnp.where(upper_part, pltpu.roll(low, 4, 1), high)
    return jnp.stack([first, second], axis=1).reshape(2 * rows, width)


def far_kernel(
    bias_ref, valid_ref, latent_ref, rope_ref, k3, mixed_ref, stat_ref, w_ref,
    keep_ref, send_ref, out_ref,
):
    items, cuts, heads, _ = latent_ref.shape
    rows = items * heads
    all_heads = cuts * heads

    out_ref[:, all_heads:, :] = jnp.zeros((items, PAD, 128), jnp.float32)
    head = lax.broadcasted_iota(jnp.int32, (rows, 128), 0) % heads
    lane = lax.broadcasted_iota(jnp.int32, (rows, 128), 1)
    half_heads = heads // 2
    head_of_half = lax.broadcasted_iota(jnp.int32, (rows // 2, 128), 0) % half_heads

    def body(cut, carry):
        scores = scores_of(latent_ref, rope_ref, cut, (k3,), bias_ref)
        old_peak, old_total = stat_ref[cut, :, 0:1], stat_ref[cut, :, 1:2]
        peak = jnp.maximum(old_peak, jnp.max(scores[0], axis=1, keepdims=True))
        factor = jnp.exp2((old_peak - peak) * (score_scale * log2_e))
        total, mixed = weigh(scores, peak, (k3,))
        total += old_total * factor
        valid = valid_ref[:, 0:1] > 0
        inverse = jnp.where(valid, 1.0 / total, 0.0)
        mixed = mixed * inverse + mixed_ref[cut] * (factor * inverse)
        level = jnp.where(valid, peak * score_scale + jnp.log(total), mask_value)
        low, high = apart(mixed)
        pieces = []
        for first, part in ((0, low), (half_heads, high)):
            upper = part.astype(jnp.bfloat16)
            lower = (part - upper.astype(jnp.float32)).astype(jnp.bfloat16)
            both = jnp.concatenate([upper, lower], axis=0)
            piece = jnp.zeros((rows // 2, 128), jnp.float32)
            for h in range(0, half_heads, 2):
                at = cut * heads + first + h
                pair = jnp.concatenate([w_ref[at], w_ref[at + 1]], axis=1)
                y = jnp.dot(both, pair, preferred_element_type=jnp.float32)
                y = y[: rows // 2] + y[rows // 2 :]
                piece = jnp.where(head_of_half == h, y[:, :128], piece)
                piece = jnp.where(head_of_half == h + 1, y[:, 128:], piece)
            pieces.append(piece)
        result = together(*pieces)
        at = pl.multiple_of(cut * heads, heads)
        out_ref[:, pl.ds(at, heads), :] = result.reshape(items, heads, 128)
        lines = jnp.where(lane == head + at, level, 0.0).reshape(items, heads, 128)
        lines = jnp.sum(lines, axis=1, keepdims=True)
        out_ref[:, all_heads:, :] += jnp.broadcast_to(lines, (items, PAD, 128))
        return carry

    lax.fori_loop(0, cuts, body, 0, unroll=2)
    half = items // 2
    core = lax.axis_index("dec") & 1

    def hand(i, carry):
        keep_ref[i] = out_ref[core * half + half - 1 - i]
        send_ref[i] = out_ref[(1 - core) * half + half - 1 - i]
        return carry

    lax.fori_loop(0, half, hand, 0)


def attend(near_bias, far_bias, valid, latent, rope, chunks, w_up):
    items, heads, _ = latent.shape
    cuts = heads // CUT_HEADS
    rows = items * CUT_HEADS
    latent = latent.reshape(items, cuts, CUT_HEADS, -1)
    rope = rope.reshape(items, cuts, CUT_HEADS, -1)
    vmem = pl.BlockSpec(memory_space=pltpu.VMEM)
    mixed, stat, w_near = pl.pallas_call(
        near_kernel,
        in_specs=[vmem] * 6 + [pl.BlockSpec(memory_space=pl.ANY)],
        out_specs=[vmem] * 3,
        out_shape=[
            jax.ShapeDtypeStruct((cuts, rows, LAT), jnp.float32),
            jax.ShapeDtypeStruct((cuts, rows, 128), jnp.float32),
            jax.ShapeDtypeStruct(w_up.shape, w_up.dtype),
        ],
        scratch_shapes=[pltpu.SemaphoreType.DMA(())],
        compiler_params=params(42),
        name="attend_near",
    )(near_bias, latent, rope, *chunks[:3], w_up)
    out_shape = jax.ShapeDtypeStruct((items // 2, heads + PAD, 128), jnp.float32)
    return pl.pallas_call(
        far_kernel,
        in_specs=[vmem] * 8,
        out_specs=[vmem] * 2,
        out_shape=[out_shape] * 2,
        scratch_shapes=[pltpu.VMEM((items, heads + PAD, 128), jnp.float32)],
        compiler_params=params(20),
        name="attend_far",
    )(far_bias, valid, latent, rope, chunks[3], mixed, stat, w_near)


def merge_step(levels):
    peak = functools.reduce(jnp.maximum, levels)
    scales = [jnp.exp(level - peak) for level in levels]
    total = functools.reduce(jnp.add, scales)
    return [scale / total for scale in scales], peak + jnp.log(total)


def spread_columns(line, heads):
    shape = line.shape[:-2] + (heads, line.shape[-1])
    axis = len(shape) - 1
    lane = lax.broadcasted_iota(jnp.int32, shape, axis)
    row = lax.broadcasted_iota(jnp.int32, shape, axis - 1)
    return jnp.sum(jnp.where(lane == row, line, 0.0), axis=axis, keepdims=True)


def pair_kernel(mine_ref, other_ref, out_ref):
    items, depth, _ = mine_ref.shape
    heads = depth - PAD
    step = 4

    def body(k, carry):
        at = pl.ds(k * step, step)
        parts = [mine_ref[at], other_ref[at]]
        scales, level = merge_step([part[:, heads:, :] for part in parts])
        result = sum(
            part[:, :heads, :] * spread_columns(scale[:, 0:1, :], heads)
            for part, scale in zip(parts, scales)
        )
        out_ref[at, :heads, :] = result
        out_ref[at, heads:, :] = level
        return carry

    lax.fori_loop(0, items // step, body, 0)


def merge_pair(mine, other):
    vmem = pl.BlockSpec(memory_space=pltpu.VMEM)
    return pl.pallas_call(
        pair_kernel,
        in_specs=[vmem] * 2,
        out_specs=vmem,
        out_shape=jax.ShapeDtypeStruct(mine.shape, mine.dtype),
        compiler_params=params(4),
        name="merge_pair",
    )(mine, other)


def merge_kernel(parts_ref, out_ref, scale_ref):
    sources, depth, lanes = parts_ref.shape
    heads = depth - PAD
    scales, _ = merge_step([parts_ref[k, heads:, :] for k in range(sources)])
    for k in range(sources):
        scale_ref[k] = scales[k]

    def body(k, so_far):
        return so_far + parts_ref[k, :heads, :] * spread_columns(scale_ref[k][0:1, :], heads)

    result = lax.fori_loop(
        0, sources, body, jnp.zeros((heads, lanes), jnp.float32), unroll=4
    ).astype(out_ref.dtype)
    for copy in range(out_ref.shape[0]):
        out_ref[copy] = result


def merge(parts):
    sources, depth, lanes = parts.shape
    vmem = pl.BlockSpec(memory_space=pltpu.VMEM)
    return pl.pallas_call(
        merge_kernel,
        in_specs=[vmem],
        out_specs=vmem,
        out_shape=jax.ShapeDtypeStruct((2 * sources, depth - PAD, lanes), jnp.bfloat16),
        scratch_shapes=[pltpu.VMEM((sources, PAD, lanes), jnp.float32)],
        compiler_params=params(4),
        name="merge",
    )(parts)


def finish_kernel(result_ref, p0, p1, p2, p3, out_ref, cache_hbm, wide_ref, sems):
    group = lax.axis_index("pre")
    copies = []
    for k, (turn, piece) in enumerate(zip(TURNS, (p0, p1, p2, p3))):
        rows = piece.shape[1]
        at = pl.multiple_of((group ^ turn) * rows, rows)
        copies.append(
            pltpu.make_async_copy(piece, cache_hbm.at[:, pl.ds(at, rows)], sems.at[k])
        )
    for copy in copies:
        copy.start()
    items, heads, lanes = result_ref.shape

    def widen(k, carry):
        device = items - 1 - k
        item = (device & 1) * (items // 2) + lax.shift_right_logical(device, 1)
        at = pl.ds(pl.multiple_of(item * heads, heads), heads)
        wide_ref[at, :] = result_ref[k].astype(jnp.float32)
        return carry

    lax.fori_loop(0, items, widen, 0, unroll=8)

    def body(h, carry):
        piece = wide_ref[pl.ds(h, items, stride=heads), :]
        at = pl.multiple_of(h * lanes, lanes)
        out_ref[:, pl.ds(at, lanes)] = piece.astype(out_ref.dtype)
        return carry

    lax.fori_loop(0, heads, body, 0, unroll=4)
    for copy in copies:
        copy.wait()


def finish(result, pieces):
    items, heads, lanes = result.shape
    width, rows = pieces[0].shape
    vmem = pl.BlockSpec(memory_space=pltpu.VMEM)
    return pl.pallas_call(
        finish_kernel,
        in_specs=[vmem] * 5,
        out_specs=[vmem, pl.BlockSpec(memory_space=pl.ANY)],
        out_shape=[
            jax.ShapeDtypeStruct((items, heads * lanes), result.dtype),
            jax.ShapeDtypeStruct((width, rows * len(pieces)), pieces[0].dtype),
        ],
        scratch_shapes=[
            pltpu.VMEM((items * heads, lanes), jnp.float32),
            pltpu.SemaphoreType.DMA((len(pieces),)),
        ],
        compiler_params=params(6),
        name="finish",
    )(result, *pieces)


def exchange(piece, groups, turn):
    return lax.ppermute(piece, "pre", [(i, i ^ turn) for i in range(groups)])


def around(piece, groups, owners):
    core = lax.axis_index("dec") % 2
    first = exchange(piece, groups, 3)
    second = exchange(piece, groups, 1)
    forward = [
        (g * owners + d, (g ^ (1 if d % 2 == 0 else 3)) * owners + d)
        for g in range(groups)
        for d in range(owners)
    ]
    chosen = jnp.where(core == 0, first, second)
    far = lax.ppermute(chosen, ("pre", "dec"), forward)
    return [piece, first, second, far], chosen


def per_device(
    hidden,
    w_down,
    kv_gain,
    query_latent,
    query_rope,
    w_up_value,
    request_rows,
    row_request,
    step_position,
    destination,
):
    groups = lax.axis_size("pre")
    owners = lax.axis_size("dec")
    steps, batch, heads, _ = query_latent.shape
    items = steps * batch
    plane = [[2 * k + core for k in reversed(range(SIDE * SIDE))] for core in range(2)]
    everyone = [list(reversed(range(owners)))]
    sibling = [(d, d ^ 1) for d in range(owners)]

    produced, packed = produce(
        groups, owners, request_rows, destination, hidden, w_down.T, kv_gain
    )
    chunks, chosen = around(produced, groups, owners)

    exchanged = functools.partial(
        lax.all_to_all, axis_name="dec", split_axis=0, concat_axis=0, tiled=True
    )
    lengths, _ = lax.optimization_barrier((request_rows, chosen))
    near_bias, far_bias, valid, chunks[0] = prepare(
        owners, groups, lengths, row_request, step_position, produced
    )
    keep, send = attend(
        near_bias,
        far_bias,
        valid,
        query_latent.reshape(items, heads, -1),
        query_rope.reshape(items, heads, -1),
        chunks,
        w_up_value,
    )
    arrived = exchanged(packed, axis_index_groups=everyone)
    quarter = place(arrived, *produced.shape)
    pieces = [quarter] + [exchange(quarter, groups, turn) for turn in TURNS[1:]]

    parts = merge_pair(keep, lax.ppermute(send, "dec", sibling))
    result = merge(exchanged(parts, axis_index_groups=plane))
    result, kv_cache = finish(exchanged(result, axis_index_groups=everyone), pieces)
    attention_out = result.reshape(steps, batch, -1)
    kv_cache = kv_cache.T
    return (attention_out, kv_cache)


def solution(mesh):
    return jax.shard_map(
        per_device,
        mesh=mesh,
        in_specs=(
            P(("pre", "dec"), None),
            P(),
            P(),
            P(None, None, "pre", None),
            P(None, None, "pre", None),
            P("pre", None, None),
            P(),
            P(),
            P(),
            P(),
        ),
        out_specs=(P(None, None, "pre"), P("dec", None)),
        check_vma=False,
    )
```

```python
import functools
import math

import jax
import jax.numpy as jnp
import numpy as np
from jax import lax
from jax.experimental import pallas as pl
from jax.experimental.pallas import tpu as pltpu
from jax.sharding import PartitionSpec as P

LAT = 512
ROPE = 64
MOST = 2
PAD = 8
SIDE = 4
TURNS = (0, 3, 1, 2)
CUT_HEADS = 8
DEPTH = 1792

score_scale = 0.07216878364870323
mask_value = -1e30
norm_eps = 1e-06
log2_e = 1.4426950408889634


def frequencies():
    half = ROPE // 2
    pair_index = np.arange(half, dtype=np.float64)
    frequency = np.exp(pair_index * (-2.0 * math.log(10000.0) / ROPE)).astype(np.float32)
    return np.tile(frequency[:, None], (1, 128))


WIDE = 640


def shift_of(count):
    assert count & (count - 1) == 0
    return count.bit_length() - 1


def params(megabytes):
    return pltpu.CompilerParams(vmem_limit_bytes=megabytes * 1024 * 1024)


def produce_kernel(
    groups, owners, lengths_hbm, dest_hbm, hidden_hbm, w_hbm, gain_hbm, freq_hbm,
    out_ref, packed_ref, hidden_ref, w_ref, acc_ref, lengths_ref, dest_ref, gain_ref, freq_ref,
    turn_ref, column_ref, rows_ref, count_ref, slot_ref, sems, small_sems,
):
    pieces, rows, depth = hidden_ref.shape
    half = ROPE // 2
    small = [
        pltpu.make_async_copy(source, target, small_sems.at[k])
        for k, (source, target) in enumerate(
            (
                (lengths_hbm, lengths_ref),
                (dest_hbm, dest_ref),
                (gain_hbm, gain_ref),
                (freq_hbm, freq_ref),
            )
        )
    ]

    def copies(k):
        columns = pl.ds(pl.multiple_of(k * depth, depth), depth)
        return (
            pltpu.make_async_copy(hidden_hbm.at[:, columns], hidden_ref.at[k], sems.at[0, k]),
            pltpu.make_async_copy(w_hbm.at[:, columns], w_ref.at[k], sems.at[1, k]),
        )

    def begin(k, carry):
        for copy in copies(k):
            copy.start()
        return carry

    for copy in small:
        copy.start()
    lax.fori_loop(0, pieces, begin, 0)
    acc_ref[...] = jnp.zeros_like(acc_ref)
    packed_ref[...] = jnp.full(packed_ref.shape, -1.0, packed_ref.dtype)
    for copy in small:
        copy.wait()
    group = lax.axis_index("pre")
    device = group * owners + lax.axis_index("dec")
    block_rows = packed_ref.shape[1]
    blocks = rows // block_rows

    def clear(owner, carry):
        count_ref[owner] = 0
        return carry

    def choose(b, carry):
        owner = lax.shift_right_logical(dest_ref[device * blocks + b], shift_of(groups * owners))
        rank = count_ref[owner]
        count_ref[owner] = rank + 1
        slot_ref[b] = (owners - 1 - owner) * MOST + rank
        return carry

    lax.fori_loop(0, owners, clear, 0)
    lax.fori_loop(0, blocks, choose, 0)
    row = device * rows + lax.broadcasted_iota(jnp.int32, (1, rows), 1)
    start = jnp.zeros((1, rows), jnp.int32)
    first_row = jnp.int32(0)
    for r in range(lengths_ref.shape[0] - 1):
        first_row = first_row + lengths_ref[r]
        start = jnp.where(row >= first_row, first_row, start)
    angles = freq_ref[:, 0:1] * (row - start).astype(jnp.float32)
    turn_ref[:half, :] = jnp.cos(angles)
    turn_ref[half:, :] = jnp.sin(angles)
    column_ref[...] = jnp.transpose(jnp.broadcast_to(gain_ref[...], (128, LAT)))

    def body(k, carry):
        for copy in copies(k):
            copy.wait()
        acc_ref[...] += lax.dot_general(
            w_ref[k],
            hidden_ref[k],
            (((1,), (1,)), ((), ())),
            preferred_element_type=jnp.float32,
        )
        return carry

    lax.fori_loop(0, pieces, body, 0)
    latent = acc_ref[:LAT, :]
    inverse_rms = lax.rsqrt(jnp.mean(latent * latent, axis=0, keepdims=True) + norm_eps)
    out_ref[:LAT, :] = (latent * inverse_rms * column_ref[:, 0:1]).astype(out_ref.dtype)
    cosine, sine = turn_ref[:half, :], turn_ref[half:, :]
    first = acc_ref[LAT : LAT + half, :]
    second = acc_ref[LAT + half :, :]
    turned = first * cosine - second * sine
    out_ref[LAT : LAT + half, :] = turned.astype(out_ref.dtype)
    turned = second * cosine + first * sine
    out_ref[LAT + half :, :] = turned.astype(out_ref.dtype)
    width = out_ref.shape[0]
    for at in range(0, width, 128):
        count = min(128, width - at)
        wide = out_ref[at : at + count, :].astype(jnp.float32)
        if count < 128:
            wide = jnp.concatenate([wide, jnp.zeros((128 - count, rows), jnp.float32)], axis=0)
        rows_ref[:, :, at : at + 128] = jnp.transpose(wide).reshape(blocks, block_rows, 128)
    lane = lax.broadcasted_iota(jnp.int32, (block_rows, WIDE), 1)

    def put(b, carry):
        place_at = (dest_ref[device * blocks + b] & (groups * owners - 1)) - group * owners
        block = jnp.where(lane < width, rows_ref[b], place_at.astype(jnp.float32))
        packed_ref[slot_ref[b]] = block.astype(packed_ref.dtype)
        return carry

    lax.fori_loop(0, blocks, put, 0, unroll=4)


def produce(groups, owners, lengths, destination, hidden, w_turned, gain):
    rows, width = hidden.shape
    row_width = w_turned.shape[0]
    pieces = width // DEPTH
    block_rows = rows // owners
    vmem = pl.BlockSpec(memory_space=pltpu.VMEM)
    return pl.pallas_call(
        functools.partial(produce_kernel, groups, owners),
        in_specs=[pl.BlockSpec(memory_space=pltpu.HBM)] * 6,
        out_specs=[vmem, vmem],
        out_shape=[
            jax.ShapeDtypeStruct((row_width, rows), jnp.bfloat16),
            jax.ShapeDtypeStruct((owners * MOST, block_rows, WIDE), jnp.bfloat16),
        ],
        scratch_shapes=[
            pltpu.VMEM((pieces, rows, DEPTH), jnp.bfloat16),
            pltpu.VMEM((pieces, row_width, DEPTH), jnp.bfloat16),
            pltpu.VMEM((row_width, rows), jnp.float32),
            pltpu.SMEM(lengths.shape, jnp.int32),
            pltpu.SMEM(destination.shape, jnp.int32),
            pltpu.VMEM((1, LAT), jnp.float32),
            pltpu.VMEM((ROPE // 2, 128), jnp.float32),
            pltpu.VMEM((ROPE, rows), jnp.float32),
            pltpu.VMEM((LAT, 128), jnp.float32),
            pltpu.VMEM((owners, block_rows, WIDE), jnp.float32),
            pltpu.SMEM((owners,), jnp.int32),
            pltpu.SMEM((owners,), jnp.int32),
            pltpu.SemaphoreType.DMA((2, pieces)),
            pltpu.SemaphoreType.DMA((4,)),
        ],
        name="produce",
    )(
        lengths,
        destination,
        hidden,
        w_turned,
        gain.reshape(1, -1),
        jnp.asarray(frequencies()),
    )


def place_kernel(arrived_ref, out_ref, rows_ref):
    blocks, block_rows, _ = arrived_ref.shape
    width, rows = out_ref.shape
    depth = 256
    part = depth // block_rows
    row = lax.broadcasted_iota(jnp.int32, (rows, depth), 0).astype(jnp.float32)
    lane = lax.broadcasted_iota(jnp.int32, (1, depth), 1)
    within = lax.rem(lane, block_rows).astype(jnp.float32)
    for k in range(blocks // part):
        source = arrived_ref[k * part : (k + 1) * part].astype(jnp.float32).reshape(depth, WIDE)
        slot = jnp.transpose(source[:, WIDE - 128 :])[127:128, :]
        select = jnp.where(row == slot * block_rows + within, 1.0, 0.0).astype(jnp.bfloat16)
        placed = jnp.dot(select, source.astype(jnp.bfloat16), preferred_element_type=jnp.float32)
        if k == 0:
            rows_ref[...] = placed
        else:
            rows_ref[...] += placed
    for at in range(0, width, 128):
        count = min(128, width - at)
        turned = jnp.transpose(rows_ref[:, at : at + 128])
        out_ref[at : at + count, :] = turned[:count].astype(out_ref.dtype)


def place(arrived, width, rows):
    vmem = pl.BlockSpec(memory_space=pltpu.VMEM)
    return pl.pallas_call(
        place_kernel,
        in_specs=[vmem],
        out_specs=vmem,
        out_shape=jax.ShapeDtypeStruct((width, rows), arrived.dtype),
        scratch_shapes=[pltpu.VMEM((rows, WIDE), jnp.float32)],
        compiler_params=params(8),
        name="place",
    )(arrived)


def prepare_kernel(
    owners, lengths_ref, request_ref, position_ref, own_hbm,
    near_ref, far_ref, valid_ref, own_ref, sem,
):
    copy = pltpu.make_async_copy(own_hbm, own_ref, sem)
    copy.start()
    steps, batch = position_ref.shape
    heads = CUT_HEADS
    count = own_ref.shape[1]
    group, owner = lax.axis_index("pre"), lax.axis_index("dec")
    row = lax.broadcasted_iota(jnp.int32, (heads, count), 1)
    bases = [((group ^ turn) * owners + owner) * count for turn in TURNS]

    def fill(b, carry):
        request = request_ref[b]
        start = jnp.int32(0)
        for r in range(lengths_ref.shape[0] - 1):
            start = start + jnp.where(request > r, lengths_ref[r], 0)
        for s in range(steps):
            stop = start + position_ref[s, b]
            at = pl.ds(pl.multiple_of((s * batch + b) * heads, heads), heads)
            seen = jnp.int32(0)
            for c, base in enumerate(bases):
                bias = jnp.where((row >= start - base) & (row < stop - base), 0.0, mask_value)
                if c < len(bases) - 1:
                    near_ref[at, c * count : (c + 1) * count] = bias
                else:
                    far_ref[at, :] = bias
                seen = seen + jnp.where((start < base + count) & (stop > base), 1, 0)
            valid_ref[at, :] = jnp.full((heads, 128), seen, jnp.int32)
        return carry

    lax.fori_loop(0, batch, fill, 0)
    copy.wait()


def prepare(owners, groups, lengths, row_request, step_position, own):
    rows = step_position.size * CUT_HEADS
    smem = pl.BlockSpec(memory_space=pltpu.SMEM)
    vmem = pl.BlockSpec(memory_space=pltpu.VMEM)
    return pl.pallas_call(
        functools.partial(prepare_kernel, owners),
        in_specs=[smem] * 3 + [pl.BlockSpec(memory_space=pl.ANY)],
        out_specs=[vmem] * 4,
        out_shape=[
            jax.ShapeDtypeStruct((rows, (groups - 1) * own.shape[1]), jnp.float32),
            jax.ShapeDtypeStruct((rows, own.shape[1]), jnp.float32),
            jax.ShapeDtypeStruct((rows, 128), jnp.int32),
            jax.ShapeDtypeStruct(own.shape, own.dtype),
        ],
        scratch_shapes=[pltpu.SemaphoreType.DMA(())],
        compiler_params=params(8),
        name="prepare",
    )(lengths, row_request, step_position, own)


def scores_of(latent_ref, rope_ref, cut, chunk_refs, bias_ref):
    items, _, heads, _ = latent_ref.shape
    rows = items * heads
    latent = latent_ref[:, cut].reshape(rows, LAT)
    rope = rope_ref[:, cut].reshape(rows, ROPE)
    scores = []
    for c, chunk_ref in enumerate(chunk_refs):
        count = chunk_ref.shape[1]
        s = jnp.dot(latent, chunk_ref[:LAT, :], preferred_element_type=jnp.float32)
        s += jnp.dot(rope, chunk_ref[LAT:, :], preferred_element_type=jnp.float32)
        scores.append(s + bias_ref[:, c * count : (c + 1) * count])
    return scores


def weigh(scores, peak, chunk_refs):
    weights = [jnp.exp2((s - peak) * (score_scale * log2_e)) for s in scores]
    total = jnp.sum(functools.reduce(jnp.add, weights), axis=1, keepdims=True)
    mixed = sum(
        lax.dot_general(
            p.astype(jnp.bfloat16),
            chunk_ref[:LAT, :],
            (((1,), (1,)), ((), ())),
            preferred_element_type=jnp.float32,
        )
        for p, chunk_ref in zip(weights, chunk_refs)
    )
    return total, mixed


def near_kernel(
    bias_ref, latent_ref, rope_ref, k0, k1, k2, w_hbm, mixed_ref, stat_ref, w_ref, sem
):
    copy = pltpu.make_async_copy(w_hbm, w_ref, sem)
    copy.start()
    chunk_refs = (k0, k1, k2)
    cuts, rows, _ = mixed_ref.shape
    lane = lax.broadcasted_iota(jnp.int32, (rows, 128), 1)

    def body(cut, carry):
        scores = scores_of(latent_ref, rope_ref, cut, chunk_refs, bias_ref)
        peak = jnp.max(functools.reduce(jnp.maximum, scores), axis=1, keepdims=True)
        total, mixed = weigh(scores, peak, chunk_refs)
        mixed_ref[cut] = mixed
        stat_ref[cut] = jnp.where(lane == 0, peak, total)
        return carry

    lax.fori_loop(0, cuts, body, 0, unroll=2)
    copy.wait()


def apart(value):
    rows, width = value.shape
    tiles = value.reshape(rows // 16, 2, 8, width)
    first, second = tiles[:, 0], tiles[:, 1]
    upper_part = lax.broadcasted_iota(jnp.int32, first.shape, 1) < 4
    low = jnp.where(upper_part, first, pltpu.roll(second, 4, 1))
    high = jnp.where(upper_part, pltpu.roll(first, 4, 1), second)
    return low.reshape(rows // 2, width), high.reshape(rows // 2, width)


def together(low, high):
    rows, width = low.shape
    low = low.reshape(rows // 8, 8, width)
    high = high.reshape(rows // 8, 8, width)
    upper_part = lax.broadcasted_iota(jnp.int32, low.shape, 1) < 4
    first = jnp.where(upper_part, low, pltpu.roll(high, 4, 1))
    second = jnp.where(upper_part, pltpu.roll(low, 4, 1), high)
    return jnp.stack([first, second], axis=1).reshape(2 * rows, width)


def far_kernel(
    bias_ref, valid_ref, latent_ref, rope_ref, k3, mixed_ref, stat_ref, w_ref,
    keep_ref, send_ref, out_ref,
):
    items, cuts, heads, _ = latent_ref.shape
    rows = items * heads
    all_heads = cuts * heads

    out_ref[:, all_heads:, :] = jnp.zeros((items, PAD, 128), jnp.float32)
    head = lax.broadcasted_iota(jnp.int32, (rows, 128), 0) % heads
    lane = lax.broadcasted_iota(jnp.int32, (rows, 128), 1)
    half_heads = heads // 2
    head_of_half = lax.broadcasted_iota(jnp.int32, (rows // 2, 128), 0) % half_heads

    def body(cut, carry):
        scores = scores_of(latent_ref, rope_ref, cut, (k3,), bias_ref)
        old_peak, old_total = stat_ref[cut, :, 0:1], stat_ref[cut, :, 1:2]
        peak = jnp.maximum(old_peak, jnp.max(scores[0], axis=1, keepdims=True))
        factor = jnp.exp2((old_peak - peak) * (score_scale * log2_e))
        total, mixed = weigh(scores, peak, (k3,))
        total += old_total * factor
        valid = valid_ref[:, 0:1] > 0
        inverse = jnp.where(valid, 1.0 / total, 0.0)
        mixed = mixed * inverse + mixed_ref[cut] * (factor * inverse)
        level = jnp.where(valid, peak * score_scale + jnp.log(total), mask_value)
        low, high = apart(mixed)
        pieces = []
        for first, part in ((0, low), (half_heads, high)):
            upper = part.astype(jnp.bfloat16)
            lower = (part - upper.astype(jnp.float32)).astype(jnp.bfloat16)
            both = jnp.concatenate([upper, lower], axis=0)
            piece = jnp.zeros((rows // 2, 128), jnp.float32)
            for h in range(0, half_heads, 2):
                at = cut * heads + first + h
                pair = jnp.concatenate([w_ref[at], w_ref[at + 1]], axis=1)
                y = jnp.dot(both, pair, preferred_element_type=jnp.float32)
                y = y[: rows // 2] + y[rows // 2 :]
                piece = jnp.where(head_of_half == h, y[:, :128], piece)
                piece = jnp.where(head_of_half == h + 1, y[:, 128:], piece)
            pieces.append(piece)
        result = together(*pieces)
        at = pl.multiple_of(cut * heads, heads)
        out_ref[:, pl.ds(at, heads), :] = result.reshape(items, heads, 128)
        lines = jnp.where(lane == head + at, level, 0.0).reshape(items, heads, 128)
        lines = jnp.sum(lines, axis=1, keepdims=True)
        out_ref[:, all_heads:, :] += jnp.broadcast_to(lines, (items, PAD, 128))
        return carry

    lax.fori_loop(0, cuts, body, 0, unroll=2)
    half = items // 2
    core = lax.axis_index("dec") & 1

    def hand(i, carry):
        keep_ref[i] = out_ref[core * half + half - 1 - i]
        send_ref[i] = out_ref[(1 - core) * half + half - 1 - i]
        return carry

    lax.fori_loop(0, half, hand, 0)


def attend(near_bias, far_bias, valid, latent, rope, chunks, w_up):
    items, heads, _ = latent.shape
    cuts = heads // CUT_HEADS
    rows = items * CUT_HEADS
    latent = latent.reshape(items, cuts, CUT_HEADS, -1)
    rope = rope.reshape(items, cuts, CUT_HEADS, -1)
    vmem = pl.BlockSpec(memory_space=pltpu.VMEM)
    mixed, stat, w_near = pl.pallas_call(
        near_kernel,
        in_specs=[vmem] * 6 + [pl.BlockSpec(memory_space=pl.ANY)],
        out_specs=[vmem] * 3,
        out_shape=[
            jax.ShapeDtypeStruct((cuts, rows, LAT), jnp.float32),
            jax.ShapeDtypeStruct((cuts, rows, 128), jnp.float32),
            jax.ShapeDtypeStruct(w_up.shape, w_up.dtype),
        ],
        scratch_shapes=[pltpu.SemaphoreType.DMA(())],
        compiler_params=params(42),
        name="attend_near",
    )(near_bias, latent, rope, *chunks[:3], w_up)
    out_shape = jax.ShapeDtypeStruct((items // 2, heads + PAD, 128), jnp.float32)
    return pl.pallas_call(
        far_kernel,
        in_specs=[vmem] * 8,
        out_specs=[vmem] * 2,
        out_shape=[out_shape] * 2,
        scratch_shapes=[pltpu.VMEM((items, heads + PAD, 128), jnp.float32)],
        compiler_params=params(20),
        name="attend_far",
    )(far_bias, valid, latent, rope, chunks[3], mixed, stat, w_near)


def merge_step(levels):
    peak = functools.reduce(jnp.maximum, levels)
    scales = [jnp.exp(level - peak) for level in levels]
    total = functools.reduce(jnp.add, scales)
    return [scale / total for scale in scales], peak + jnp.log(total)


def spread_columns(line, heads):
    shape = line.shape[:-2] + (heads, line.shape[-1])
    axis = len(shape) - 1
    lane = lax.broadcasted_iota(jnp.int32, shape, axis)
    row = lax.broadcasted_iota(jnp.int32, shape, axis - 1)
    return jnp.sum(jnp.where(lane == row, line, 0.0), axis=axis, keepdims=True)


def pair_kernel(mine_ref, other_ref, out_ref):
    items, depth, _ = mine_ref.shape
    heads = depth - PAD
    step = 4

    def body(k, carry):
        at = pl.ds(k * step, step)
        parts = [mine_ref[at], other_ref[at]]
        scales, level = merge_step([part[:, heads:, :] for part in parts])
        result = sum(
            part[:, :heads, :] * spread_columns(scale[:, 0:1, :], heads)
            for part, scale in zip(parts, scales)
        )
        out_ref[at, :heads, :] = result
        out_ref[at, heads:, :] = level
        return carry

    lax.fori_loop(0, items // step, body, 0)


def merge_pair(mine, other):
    vmem = pl.BlockSpec(memory_space=pltpu.VMEM)
    return pl.pallas_call(
        pair_kernel,
        in_specs=[vmem] * 2,
        out_specs=vmem,
        out_shape=jax.ShapeDtypeStruct(mine.shape, mine.dtype),
        compiler_params=params(4),
        name="merge_pair",
    )(mine, other)


def merge_kernel(parts_ref, out_ref, scale_ref):
    sources, depth, lanes = parts_ref.shape
    heads = depth - PAD
    scales, _ = merge_step([parts_ref[k, heads:, :] for k in range(sources)])
    for k in range(sources):
        scale_ref[k] = scales[k]

    def body(k, so_far):
        return so_far + parts_ref[k, :heads, :] * spread_columns(scale_ref[k][0:1, :], heads)

    result = lax.fori_loop(
        0, sources, body, jnp.zeros((heads, lanes), jnp.float32), unroll=4
    ).astype(out_ref.dtype)
    for copy in range(out_ref.shape[0]):
        out_ref[copy] = result


def merge(parts):
    sources, depth, lanes = parts.shape
    vmem = pl.BlockSpec(memory_space=pltpu.VMEM)
    return pl.pallas_call(
        merge_kernel,
        in_specs=[vmem],
        out_specs=vmem,
        out_shape=jax.ShapeDtypeStruct((2 * sources, depth - PAD, lanes), jnp.bfloat16),
        scratch_shapes=[pltpu.VMEM((sources, PAD, lanes), jnp.float32)],
        compiler_params=params(4),
        name="merge",
    )(parts)


def assemble_kernel(p0, p1, p2, p3, cache_hbm, sems):
    group = lax.axis_index("pre")
    copies = []
    for k, (turn, piece) in enumerate(zip(TURNS, (p0, p1, p2, p3))):
        rows = piece.shape[1]
        at = pl.multiple_of((group ^ turn) * rows, rows)
        copies.append(
            pltpu.make_async_copy(piece, cache_hbm.at[:, pl.ds(at, rows)], sems.at[k])
        )
    for copy in copies:
        copy.start()
    for copy in copies:
        copy.wait()


def assemble(pieces):
    width, rows = pieces[0].shape
    return pl.pallas_call(
        assemble_kernel,
        in_specs=[pl.BlockSpec(memory_space=pltpu.VMEM)] * 4,
        out_specs=pl.BlockSpec(memory_space=pl.ANY),
        out_shape=jax.ShapeDtypeStruct((width, rows * len(pieces)), pieces[0].dtype),
        scratch_shapes=[pltpu.SemaphoreType.DMA((len(pieces),))],
        compiler_params=params(4),
        name="assemble",
    )(*pieces)


def spread_kernel(result_ref, out_ref, wide_ref):
    items, heads, lanes = result_ref.shape

    def widen(k, carry):
        device = items - 1 - k
        item = (device & 1) * (items // 2) + lax.shift_right_logical(device, 1)
        at = pl.ds(pl.multiple_of(item * heads, heads), heads)
        wide_ref[at, :] = result_ref[k].astype(jnp.float32)
        return carry

    lax.fori_loop(0, items, widen, 0, unroll=8)

    def body(h, carry):
        piece = wide_ref[pl.ds(h, items, stride=heads), :]
        at = pl.multiple_of(h * lanes, lanes)
        out_ref[:, pl.ds(at, lanes)] = piece.astype(out_ref.dtype)
        return carry

    lax.fori_loop(0, heads, body, 0, unroll=4)


def spread(result):
    items, heads, lanes = result.shape
    vmem = pl.BlockSpec(memory_space=pltpu.VMEM)
    return pl.pallas_call(
        spread_kernel,
        in_specs=[vmem],
        out_specs=vmem,
        out_shape=jax.ShapeDtypeStruct((items, heads * lanes), result.dtype),
        scratch_shapes=[pltpu.VMEM((items * heads, lanes), jnp.float32)],
        compiler_params=params(4),
        name="spread",
    )(result)


def exchange(piece, groups, turn):
    return lax.ppermute(piece, "pre", [(i, i ^ turn) for i in range(groups)])


def around(piece, groups, owners):
    core = lax.axis_index("dec") % 2
    first = exchange(piece, groups, 3)
    second = exchange(piece, groups, 1)
    forward = [
        (g * owners + d, (g ^ (1 if d % 2 == 0 else 3)) * owners + d)
        for g in range(groups)
        for d in range(owners)
    ]
    chosen = jnp.where(core == 0, first, second)
    far = lax.ppermute(chosen, ("pre", "dec"), forward)
    return [piece, first, second, far], chosen


def per_device(
    hidden,
    w_down,
    kv_gain,
    query_latent,
    query_rope,
    w_up_value,
    request_rows,
    row_request,
    step_position,
    destination,
):
    groups = lax.axis_size("pre")
    owners = lax.axis_size("dec")
    steps, batch, heads, _ = query_latent.shape
    items = steps * batch
    plane = [[2 * k + core for k in reversed(range(SIDE * SIDE))] for core in range(2)]
    everyone = [list(reversed(range(owners)))]
    sibling = [(d, d ^ 1) for d in range(owners)]

    produced, packed = produce(
        groups, owners, request_rows, destination, hidden, w_down.T, kv_gain
    )
    chunks, chosen = around(produced, groups, owners)

    exchanged = functools.partial(
        lax.all_to_all, axis_name="dec", split_axis=0, concat_axis=0, tiled=True
    )
    lengths, _ = lax.optimization_barrier((request_rows, chosen))
    near_bias, far_bias, valid, chunks[0] = prepare(
        owners, groups, lengths, row_request, step_position, produced
    )
    keep, send = attend(
        near_bias,
        far_bias,
        valid,
        query_latent.reshape(items, heads, -1),
        query_rope.reshape(items, heads, -1),
        chunks,
        w_up_value,
    )
    arrived = exchanged(packed, axis_index_groups=everyone)
    quarter = place(arrived, *produced.shape)
    pieces = [quarter] + [exchange(quarter, groups, turn) for turn in TURNS[1:]]

    parts = merge_pair(keep, lax.ppermute(send, "dec", sibling))
    result = merge(exchanged(parts, axis_index_groups=plane))
    kv_cache = assemble(pieces)
    result = spread(exchanged(result, axis_index_groups=everyone))
    attention_out = result.reshape(steps, batch, -1)
    kv_cache = kv_cache.T
    return (attention_out, kv_cache)


def solution(mesh):
    return jax.shard_map(
        per_device,
        mesh=mesh,
        in_specs=(
            P(("pre", "dec"), None),
            P(),
            P(),
            P(None, None, "pre", None),
            P(None, None, "pre", None),
            P("pre", None, None),
            P(),
            P(),
            P(),
            P(),
        ),
        out_specs=(P(None, None, "pre"), P("dec", None)),
        check_vma=False,
    )
```
